32 devices in a mesh: dp: 16 (over z, y, core), tensor: 2 (over x).
Axes of the slice: x: 2, y: 2, z: 4, core: 2. Of those that a mesh axis runs over, the one named last changes fastest.
Arguments:
- tokens: bfloat16 [16, 1024, 768], P('dp'), may hold values from -6 to 6
- counts: int32 [16], P('dp'), may hold values from 102 to 1022, as said below
- indices: int32 [16, 1022], P('dp'), may hold values from 0 to 1023, as said below
- ground_dist: int32 [16], P('dp'), may hold values from 1 to 30
- cotangent: bfloat16 [16, 1024, 768], P('dp'), may hold values from -6 to 6
- attn_weight: float32 [3, 768, 768], P(None, 'dp', 'tensor'), may hold values from -0.21875 to 0.21875
- attn_bias: float32 [2, 12, 64], P(None, 'tensor', 'dp'), may hold values from -0.4375 to 0.4375
- out_weight: float32 [768, 768], P('tensor', 'dp'), may hold values from -3 to 3
- vectors: float32 [6, 768], P(None, 'dp')
- up_weight: float32 [768, 3072], P(None, ('dp', 'tensor')), may hold values from -0.21875 to 0.21875
- up_bias: float32 [3072], P(('dp', 'tensor')), may hold values from -6 to 6
- down_weight: float32 [3072, 768], P(('dp', 'tensor')), may hold values from -0.109375 to 0.109375
Outputs:
- mixed: bfloat16 [16, 1024, 768], P('dp')
- input_grad: bfloat16 [16, 1024, 768], P('dp')
- attn_weight_grad: float32 [3, 768, 768], P(None, 'dp', 'tensor')
- attn_bias_grad: float32 [2, 12, 64], P(None, 'tensor', 'dp')
- out_weight_grad: float32 [768, 768], P('tensor', 'dp')
- vectors_grad: float32 [6, 768], P(None, 'dp')
- up_weight_grad: float32 [768, 3072], P(None, ('dp', 'tensor'))
- up_bias_grad: float32 [3072], P(('dp', 'tensor'))
- down_weight_grad: float32 [3072, 768], P(('dp', 'tensor'))
The draws below stay inside these ranges and needn't reach their ends.
Inputs may be any that keep to these rules, and one draw needn't show every extreme that they name: Chip c has counts[c] visible patches, in slots 2 to counts[c] + 1; some chip has 1022 and some chip 102. The first counts[c] entries of row c are that chip's visible patch indices, distinct and increasing; the remaining entries are other patch indices of the chip.
All inputs are finite; a program needn't handle non-finite values.
Results may differ from the reference program's by a relative error of at most 0.015.
The reference program's roundings to bfloat16 on the way count: a program that leaves them out, or rounds other values in their place, can miss the bound.
Values may be sent and summed in bfloat16 or wider, within the bound.
A program may use at most 192 MiB of HBM per device.

```python
import jax
import jax.numpy as jnp
from jax import lax

D = 768
HEADS = 12
HD = 64
FF = 3072
GRID = 32
SEQ = 1024
QBLOCK = 512
VIS = 1022
VIS_MIN = 102
PATCHES = 1024
CHIPS = 16


def visible_counts(key):
    first, second, third = jax.random.split(key, 3)
    counts = jax.random.randint(first, (CHIPS,), VIS_MIN, VIS + 1)
    fullest = jax.random.randint(second, (), 0, CHIPS)
    counts = counts.at[fullest].set(VIS)
    offset = jax.random.randint(third, (), 1, CHIPS)
    counts = counts.at[(fullest + offset) % CHIPS].set(VIS_MIN)
    return counts.astype(jnp.int32)


def draw_counts(key, part):
    return visible_counts(key)


def draw_indices(key, part):
    counts = visible_counts(key)
    key = jax.random.fold_in(key, 5)
    places = jnp.arange(PATCHES, dtype=jnp.int32)[None, :]
    scores = jax.random.randint(key, (CHIPS, PATCHES), 0, 1 << 20) * PATCHES + places
    order = jnp.argsort(scores, axis=1)
    ranking = jnp.argsort(order, axis=1)
    chosen = ranking < counts[:, None]
    keyed = jnp.where(chosen, 0, PATCHES) + places
    listing = jnp.argsort(keyed, axis=1)[:, :VIS]
    return listing.astype(jnp.int32)


def draw_vectors(key, part):
    key = jax.random.fold_in(key, 7)
    noise = jnp.clip(jax.random.normal(key, (6, D), jnp.float32) * 0.3, -0.6, 0.6)
    leading = jnp.array([1.0, 0.0, 1.0, 0.0, 0.0, 0.0], jnp.float32)[:, None]
    return leading + noise


def set_ends(values, key, least, high):
    dims = values.shape
    place = [jax.random.randint(jax.random.fold_in(key, axis), (), 0, dims[axis]) for axis in range(len(dims))]
    values = values.at[tuple(place)].set(least)
    longest = dims.index(max(dims))
    place[longest] = (place[longest] + 1) % dims[longest]
    return values.at[tuple(place)].set(high)


def spiked(values, stream_key, source, target, parts, factor):
    def block_of(dim):
        return (jnp.arange(values.shape[dim]) // (values.shape[dim] // parts)).reshape((-1,) + (1,) * (values.ndim - 1 - dim))

    one_side = jax.random.permutation(stream_key, parts)[block_of(target)]
    second = (block_of(target) + parts // 2) % parts
    return jnp.where((block_of(source) == one_side) | (block_of(source) == second), factor * values, values)


def steps_of(own_key, dims, cuts, least, largest):
    factor_of, own = 1.0, jax.random.fold_in(own_key, 6)
    for position, shards_of in cuts:
        heights = jnp.exp(jax.random.uniform(jax.random.fold_in(own, position), (shards_of,), jnp.float32, least / len(cuts), largest / len(cuts)))
        factor_of = factor_of * jnp.repeat(heights, dims[position] // shards_of).reshape([-1 if axis == position else 1 for axis in range(len(dims))])
    return factor_of


def gaussian(rng, dims, width, bound, shards=(), held_as=jnp.bfloat16):
    drawn = jax.random.normal(rng, dims, jnp.float32) * width
    if len(shards) > 0:
        drawn = steps_of(rng, dims, shards, -0.22, 0.18) * drawn
    return jnp.clip(drawn, min=-bound, max=bound).astype(held_as)


def noise_with(own_key, extent, width, most, cuts, heavy, kind=jnp.bfloat16):
    drawn = width * jax.random.normal(own_key, extent, jnp.float32)
    if cuts:
        drawn = drawn * steps_of(own_key, extent, cuts, -0.22, 0.18)
    return jnp.clip(spiked(drawn, jax.random.fold_in(own_key, 3), *heavy), -most, most).astype(kind)


def setup_inputs(seed: int = 0) -> dict:
    key_list = jax.random.split(jax.random.key(seed), 13)
    return {
        "tokens": gaussian(key_list[0], (CHIPS, SEQ, D), 1.0, 6.0, ((0, 16),)),
        "counts": draw_counts(jax.random.fold_in(key_list[12], 71), 0),
        "indices": draw_indices(jax.random.fold_in(key_list[12], 71), 0),
        "ground_dist": set_ends(jax.random.randint(key_list[3], (CHIPS,), 1, 31), jax.random.fold_in(key_list[3], 1), 1, 30).astype(jnp.int32),
        "cotangent": noise_with(key_list[4], (CHIPS, SEQ, D), 1.0, 6.0, ((0, 16),), (0, 2, 16, 2.0)),
        "attn_weight": gaussian(key_list[5], (3, D, D), D ** -0.5, 0.21875, ((1, 16), (2, 2)), jnp.float32),
        "attn_bias": gaussian(key_list[6], (2, HEADS, HD), 0.03, 0.4375, ((1, 2), (2, 16)), jnp.float32),
        "out_weight": gaussian(key_list[7], (D, D), (max(D // 192, 1)) ** -0.5, 3.0, ((0, 2), (1, 16)), jnp.float32),
        "vectors": draw_vectors(jax.random.fold_in(key_list[12], 71), 0),
        "up_weight": gaussian(key_list[9], (D, FF), D ** -0.5, 0.21875, ((1, 32),), jnp.float32),
        "up_bias": gaussian(key_list[10], (FF,), 0.5, 6.0, ((0, 32),), jnp.float32),
        "down_weight": gaussian(key_list[11], (FF, D), FF ** -0.5, 0.109375, ((0, 32),), jnp.float32),
    }


EPS = 1e-06
NEGATIVE = -1e+30
HIGH = lax.Precision.HIGHEST

@jax.custom_vjp
def low(v):
    return lax.optimization_barrier(v.astype(jnp.bfloat16)).astype(jnp.float32)

@jax.custom_vjp
def low_back(v):
    return v

def low_keep(v):
    return (low(v), None)

def low_pass(kept, grad):
    return (grad,)

def back_keep(v):
    return (v, None)

def back_low(kept, grad):
    return (low(grad),)
low.defvjp(low_keep, low_pass)
low_back.defvjp(back_keep, back_low)

def position_code(indices, ground):
    quarter = D // 4
    omega = 1.0 / 10000.0 ** (jnp.arange(quarter, dtype=jnp.float32) / quarter)
    scale = (ground.astype(jnp.float32) / 10.0)[:, None, None]
    rows = (indices // GRID).astype(jnp.float32)[:, :, None] * scale * omega
    columns = (indices % GRID).astype(jnp.float32)[:, :, None] * scale * omega
    return jnp.concatenate([jnp.sin(rows), jnp.cos(rows), jnp.sin(columns), jnp.cos(columns)], axis=-1)

def normalize(values, gain, shift):
    average = lax.optimization_barrier(jnp.mean(values, axis=-1, keepdims=True))
    centered = values - average
    variance = lax.optimization_barrier(jnp.mean(centered * centered, axis=-1, keepdims=True))
    return centered * lax.rsqrt(variance + EPS) * gain + shift

def block_attend(block, keys, values, keep):
    raw = jnp.einsum('qhd,khd->hqk', block, keys, precision=HIGH) * HD ** (-0.5)
    scores = jnp.where(keep, low_back(raw), NEGATIVE)
    top = lax.optimization_barrier(jnp.max(scores, axis=-1, keepdims=True))
    weights = jnp.exp(scores - top)
    probs = weights / lax.optimization_barrier(jnp.sum(weights, axis=-1, keepdims=True))
    return jnp.einsum('hqk,khd->qhd', low(probs), values, precision=HIGH)

def chip_layer(row_tokens, attn_weight, attn_bias, out_weight, vectors, up_weight, up_bias, down_weight, count, row_indices, ground):
    live = (jnp.arange(SEQ) < count + 2).astype(jnp.float32)[:, None]
    code = jnp.concatenate([jnp.zeros((2, D), jnp.float32), position_code(row_indices[None], ground[None])[0]], axis=0)
    start = (row_tokens + code) * live
    vec = low(vectors)
    normed = low(normalize(start, vec[0], vec[1]))
    projected = jnp.einsum('rd,kdc->krc', normed, low(attn_weight), precision=HIGH)
    bias = low(attn_bias).reshape(2, D)
    queries = low(low_back(projected[0]) + bias[0]).reshape(SEQ, HEADS, HD)
    keys = low(low_back(projected[1])).reshape(SEQ, HEADS, HD)
    values = low(low_back(projected[2]) + bias[1]).reshape(SEQ, HEADS, HD)
    keep = (jnp.arange(SEQ) < count + 2)[None, None, :]
    blocks = queries.reshape(SEQ // QBLOCK, QBLOCK, HEADS, HD)
    attend = jax.checkpoint(lambda block: block_attend(block, keys, values, keep))
    attended = low(low_back(lax.map(attend, blocks).reshape(SEQ, D)))
    mid = start + (low_back(jnp.dot(attended, low(out_weight), precision=HIGH)) + vec[4])
    normed2 = low(normalize(mid, vec[2], vec[3]))
    hidden = low_back(jnp.dot(normed2, low(up_weight), precision=HIGH)) + low(up_bias)
    act = low(jax.nn.gelu(hidden, approximate=False))
    down = jnp.dot(act, low(down_weight), precision=HIGH) + vec[5]
    return live * (mid + down)

def reference(tokens, counts, indices, ground_dist, cotangent, attn_weight, attn_bias, out_weight, vectors, up_weight, up_bias, down_weight):
    params = (attn_weight, attn_bias, out_weight, vectors, up_weight, up_bias, down_weight)

    def one_chip(totals, items):
        row_tokens, row_cot, count, row_indices, ground = items

        def run(row_in, *weights):
            return chip_layer(row_in, *weights, count, row_indices, ground)
        result, pullback = jax.vjp(run, row_tokens.astype(jnp.float32), *params)
        gradients = pullback(row_cot.astype(jnp.float32))
        totals = tuple((summed + gradient for summed, gradient in zip(totals, gradients[1:])))
        return (totals, (result.astype(jnp.bfloat16), gradients[0].astype(jnp.bfloat16)))
    zeros = tuple((jnp.zeros_like(weight) for weight in params))
    totals, (mixed, input_grad) = lax.scan(one_chip, zeros, (tokens, cotangent, counts, indices, ground_dist))
    return (mixed, input_grad, totals[0], totals[1], totals[2], totals[3], totals[4], totals[5], totals[6])
```

```python
import functools

import jax
import jax.numpy as jnp
from jax import lax
from jax.experimental import pallas as pl
from jax.experimental.pallas import tpu as pltpu
from jax.sharding import PartitionSpec as P

D = 768
HD = 64
GRID = 32
EPS = 1e-06
DEAD = -1e30
PAIR = 2 * HD
ROOT_HALF = 0.7071067811865476
ROOT_TWO_PI_INV = 0.3989422804014327

F32 = jnp.float32
BF16 = jnp.bfloat16
MESH = pl.DeviceIdType.MESH
MIB = 1 << 20


def nn(a, b):
    return lax.dot_general(a, b, (((1,), (0,)), ((), ())), preferred_element_type=F32)


def nt(a, b):
    return lax.dot_general(a, b, (((1,), (1,)), ((), ())), preferred_element_type=F32)


def tn(a, b):
    return lax.dot_general(a, b, (((0,), (0,)), ((), ())), preferred_element_type=F32)


class Cube:
    def __init__(self, dp_size):
        self.dp = lax.axis_index("dp")
        self.t = lax.axis_index("tensor")
        self.core = lax.rem(self.dp, 2)
        c = self.core

        def flip(b):
            return b * (1 - 2 * lax.rem(lax.div(self.dp, b), 2))

        dt, dy, dc = 1 - 2 * self.t, flip(2), flip(1)
        steps = []
        b = dp_size // 2
        while b >= 4:
            steps.append((flip(b), 0))
            b //= 2
        steps.append((c * dy, (1 - c) * dt))
        steps.append(((1 - c) * dy, c * dt))
        steps.append((dc, 0))
        self.steps = steps
        self.sibling = (self.dp + dc, self.t)
        self.across = (self.dp, self.t + dt)
        self.diagonal = (self.dp + dc, self.t + dt)

    def partner(self, p):
        return (self.dp + self.steps[p][0], self.t + self.steps[p][1])

    def entry(self, mask):
        dp, t = self.dp, self.t
        for p, (ddp, dt) in enumerate(self.steps):
            if mask >> p & 1:
                dp, t = dp + ddp, t + dt
        return dp, t


def phases_of(dp_size):
    return (2 * dp_size).bit_length() - 1


def enter(devices):
    barrier = pltpu.get_barrier_semaphore()
    for device in devices:
        pl.semaphore_signal(barrier, inc=1, device_id=device, device_id_type=MESH)
    pl.semaphore_wait(barrier, len(devices))


class Gather:
    def __init__(self, cube, count, own, slot, send_sem, recv_sem):
        self.cube, self.own, self.slot = cube, own, slot
        self.send_sem, self.recv_sem = send_sem, recv_sem
        self.count = count
        self.sent = []
        self.order = sorted(
            ((p, m) for p in range(count) for m in range(1 << p)),
            key=lambda item: (item[1].bit_count(), item[0], item[1]),
        )

    def copy(self, p, mask, source):
        place = self.slot(*self.cube.entry(mask))
        k = (1 << p) - 1 + mask
        return pltpu.make_async_remote_copy(
            src_ref=source if source is not None else place,
            dst_ref=place,
            send_sem=self.send_sem.at[k],
            recv_sem=self.recv_sem.at[k],
            device_id=self.cube.partner(p),
            device_id_type=MESH,
        )

    def send(self, p, mask):
        copy = self.copy(p, mask, self.own if mask == 0 else None)
        copy.start()
        self.sent.append(copy)

    def start(self):
        for p in range(self.count):
            self.send(p, 0)

    def step(self, k):
        p, mask = self.order[k]
        place = self.slot(*self.cube.entry(mask | 1 << p))
        j = (1 << p) - 1 + mask
        pltpu.make_async_remote_copy(
            src_ref=place,
            dst_ref=place,
            send_sem=self.send_sem.at[j],
            recv_sem=self.recv_sem.at[j],
            device_id=self.cube.partner(p),
            device_id_type=MESH,
        ).wait_recv()
        for later in range(p + 1, self.count):
            self.send(later, mask | 1 << p)

    def finish(self):
        for copy in self.sent:
            copy.wait_send()


def low_bit(m):
    return (m & -m).bit_length() - 1 if m else 99


def mirrored(m):
    return m & ~6 | (m >> 1 & 1) << 2 | (m >> 2 & 1) << 1


class Scatter:
    def __init__(self, cube, count, part, staged, landed, send_sem, recv_sem):
        self.cube, self.count = cube, count
        self.part, self.staged, self.landed = part, staged, landed
        self.send_sem, self.recv_sem = send_sem, recv_sem
        self.sent = []
        masks = [m for m in range(1, 1 << count)]
        masks.sort(key=lambda m: (low_bit(m), low_bit(m & (m - 1)), m))
        self.order = masks + [0]

    def device(self, q):
        return self.cube.partner(self.count - 1 - q)

    def entry(self, m):
        flipped = 0
        for q in range(self.count):
            if m >> q & 1:
                flipped |= 1 << (self.count - 1 - q)
        return self.cube.entry(flipped)

    def index(self, q, m):
        return (1 << (self.count - 1 - q)) - 1 + (m >> (q + 1))

    def describe(self, q, m, source):
        k = self.index(q, mirrored(m) if q == 0 else m)
        return pltpu.make_async_remote_copy(
            src_ref=source,
            dst_ref=self.landed.at[k],
            send_sem=self.send_sem.at[k],
            recv_sem=self.recv_sem.at[k],
            device_id=self.device(q),
            device_id_type=MESH,
        )

    def start(self):
        for m in self.order:
            m = mirrored(m)
            if m & 1:
                copy = self.describe(0, m, self.part(*self.entry(m)))
                copy.start()
                self.sent.append(copy)
        self.rest = [m for m in self.order if not m & 1]

    def total(self, m):
        first = low_bit(m)
        here = self.part(*self.entry(m))
        total = here[...].astype(F32)
        for q in range(min(first, self.count)):
            k = self.index(q, m)
            self.describe(q, mirrored(m) if q == 0 else m, self.landed.at[k]).wait_recv()
            total = total + self.landed[k].astype(F32)
        return total

    def step(self, k):
        m = self.rest[k]
        q = low_bit(m)
        total = self.total(m)
        j = self.index(q, m)
        self.staged[j] = total.astype(BF16)
        copy = self.describe(q, m, self.staged.at[j])
        copy.start()
        self.sent.append(copy)

    def last(self):
        return self.total(0)

    def finish(self):
        for copy in self.sent:
            copy.wait_send()


def spread(cube, half, out, send_sem, recv_sem):
    c, t = cube.core, cube.t
    mine = out.at[c]

    def push(device, k):
        return pltpu.make_async_remote_copy(
            src_ref=half,
            dst_ref=mine,
            send_sem=send_sem.at[k],
            recv_sem=recv_sem.at[c],
            device_id=device,
            device_id_type=MESH,
        )

    def arrival(h):
        return pltpu.make_async_remote_copy(
            src_ref=half,
            dst_ref=out.at[h],
            send_sem=send_sem.at[0],
            recv_sem=recv_sem.at[h],
            device_id=cube.sibling,
            device_id_type=MESH,
        )

    keep = pltpu.make_async_copy(half, mine, send_sem.at[0])

    @pl.when(c == t)
    def _():
        push(cube.across, 1).start()
        keep.start()

    @pl.when(c != t)
    def _():
        push(cube.diagonal, 1).start()
        push(cube.sibling, 0).start()

    def wait():
        @pl.when(c == t)
        def _():
            keep.wait()
            push(cube.across, 1).wait_send()
            arrival(1 - c).wait_recv()

        @pl.when(c != t)
        def _():
            push(cube.sibling, 0).wait_send()
            push(cube.diagonal, 1).wait_send()
            arrival(c).wait_recv()
            arrival(1 - c).wait_recv()

    return wait


def gather_kernel(
    dp_size,
    tok,
    cot,
    ints,
    packs,
    attn,
    up,
    down,
    tok2,
    cot2,
    ints2,
    packs_all,
    attn_all,
    up_all,
    down_all,
    send_sem,
    recv_sem,
    pair_sem,
    local_sem,
):
    cube = Cube(dp_size)
    count = phases_of(dp_size)
    rows = cot2.shape[1]
    c = cube.core
    other = pl.ds(pl.multiple_of((1 - c) * rows, rows), rows)
    own = pl.ds(pl.multiple_of(c * rows, rows), rows)
    locals_ = [
        pltpu.make_async_copy(tok, tok2.at[c], local_sem.at[0]),
        pltpu.make_async_copy(cot.at[own], cot2.at[c], local_sem.at[1]),
        pltpu.make_async_copy(ints, ints2.at[c], local_sem.at[2]),
        pltpu.make_async_copy(packs, packs_all.at[cube.dp, cube.t], local_sem.at[3]),
        pltpu.make_async_copy(attn, attn_all.at[cube.t, :, cube.dp], local_sem.at[4]),
        pltpu.make_async_copy(up, up_all.at[cube.dp, cube.t], local_sem.at[5]),
        pltpu.make_async_copy(down, down_all.at[cube.dp, cube.t], local_sem.at[6]),
    ]
    for copy in locals_:
        copy.start()
    enter([cube.partner(p) for p in range(count)])
    jobs = [
        Gather(
            cube,
            count,
            source,
            slot,
            send_sem.at[k],
            recv_sem.at[k],
        )
        for k, (source, slot) in enumerate(
            (
                (packs, lambda dp, t: packs_all.at[dp, t]),
                (attn, lambda dp, t: attn_all.at[t, :, dp]),
                (up, lambda dp, t: up_all.at[dp, t]),
                (down, lambda dp, t: down_all.at[dp, t]),
            )
        )
    ]
    pairs = [
        pltpu.make_async_remote_copy(
            src_ref=source,
            dst_ref=target.at[c],
            send_sem=pair_sem.at[0, k],
            recv_sem=pair_sem.at[1, k],
            device_id=cube.sibling,
            device_id_type=MESH,
        )
        for k, (source, target) in enumerate(
            ((ints, ints2), (tok, tok2), (cot.at[other], cot2))
        )
    ]
    for copy in pairs:
        copy.start()
    for job in jobs:
        job.start()
        for k in range(len(job.order)):
            job.step(k)
    for job in jobs:
        job.finish()
    for copy in pairs:
        copy.wait()
    for copy in locals_:
        copy.wait()


def centre(values):
    mean = jnp.mean(values, axis=-1, keepdims=True)
    centred = values - mean
    rstd = lax.rsqrt(jnp.mean(centred * centred, axis=-1, keepdims=True) + EPS)
    return centred * rstd, rstd


def row_live(count, offset, rows):
    places = lax.broadcasted_iota(jnp.int32, (rows, 1), 0) + offset
    return (places < count + 2).astype(F32)


def lane_sets():
    lane = lax.broadcasted_iota(jnp.int32, (1, PAIR), 1)
    own = [(lane < HD).astype(F32).astype(BF16), (lane >= HD).astype(F32).astype(BF16)]
    mark = [(lane == HD).astype(F32).astype(BF16), (lane == 0).astype(F32).astype(BF16)]
    return lane, own, mark


def forward_kernel(
    tok,
    ints,
    table,
    weights,
    vec,
    bias,
    normed,
    start_own,
    qs,
    keys,
    values,
    mixed_heads,
    attended,
    lse,
    mid,
    start,
):
    length = tok.shape[0]
    half = start_own.shape[0]
    c = lax.rem(lax.axis_index("dp"), 2)
    base = pl.multiple_of(c * half, half)
    count = ints[0:1, 0:1]
    full = table[...]
    hi = full.astype(BF16)
    rest = full - hi.astype(F32)
    middle = rest.astype(BF16)
    little = (rest - middle.astype(F32)).astype(BF16)
    stack = jnp.concatenate([hi, middle, little], axis=0)
    tile = 256
    for r in range(length // tile):
        span = slice(r * tile, (r + 1) * tile)
        index = ints[0:1, span]
        slots = lax.broadcasted_iota(jnp.int32, (1, tile), 1) + r * tile
        places = lax.broadcasted_iota(jnp.int32, (GRID, tile), 0)
        parts = []
        for part in (lax.shift_right_logical(index, 5), lax.bitwise_and(index, GRID - 1)):
            part = jnp.where(slots < 2, -1, part)
            hot = (places == part).astype(F32).astype(BF16)
            parts.append(tn(jnp.concatenate([hot, hot, hot], axis=0), stack))
        code = jnp.concatenate(parts, axis=1)
        live = row_live(count, r * tile, tile)
        rows = (tok[span, :].astype(F32) + code) * live
        start[span, :] = rows
        xhat, rstd = centre(rows)
        normed[span, :] = (xhat * vec[0:1, :] + vec[1:2, :]).astype(BF16)
    start_own[...] = start[pl.ds(base, half), :]
    width = weights.shape[3]
    for t in range(weights.shape[0]):
        cols = slice(t * width, (t + 1) * width)
        query = nn(normed[pl.ds(base, half), :], weights[t, 0]) + bias[0:1, cols]
        qs[:, cols] = query.astype(BF16) * jnp.asarray(HD**-0.5, BF16)
        for r in range(length // half):
            span = slice(r * half, (r + 1) * half)
            keys[span, cols] = nn(normed[span, :], weights[t, 1]).astype(BF16)
            values[span, cols] = (nn(normed[span, :], weights[t, 2]) + bias[1:2, cols]).astype(BF16)
    lane, own, mark = lane_sets()
    dead = ((1.0 - row_live(count, 0, length)) * DEAD).astype(BF16)
    wide = lax.broadcasted_iota(jnp.int32, (1, PAIR), 1)
    block = 256
    for r in range(half // block):
        span = slice(r * block, (r + 1) * block)
        sums = jnp.zeros((block, PAIR), F32)
        for p in range(D // PAIR):
            cols = slice(p * PAIR, (p + 1) * PAIR)
            outs = []
            for h in range(2):
                kx = keys[:, cols] * own[h] + dead * mark[h]
                qx = qs[span, cols] * own[h] + mark[h]
                scores = nt(qx, kx)
                top = jnp.max(scores, axis=1, keepdims=True)
                grown = jnp.exp(scores - top)
                total = jnp.sum(grown, axis=1, keepdims=True)
                outs.append(nn(grown.astype(BF16), values[:, cols]) / total)
                sums = jnp.where(wide == 2 * p + h, top + jnp.log(total), sums)
            both = jnp.where(lane < HD, outs[0], outs[1])
            mixed_heads[span, cols] = both
            attended[span, cols] = both.astype(BF16)
        lse[:, span] = sums.T
    out = nt(attended[:, :width], weights[0, 3])
    for t in range(1, weights.shape[0]):
        out = out + nt(attended[:, t * width : (t + 1) * width], weights[t, 3])
    mid[...] = start_own[...] + (out + vec[4:5, :])


def norm_back(xhat, rstd, gain, upstream):
    scaled = upstream * gain
    return rstd * (
        scaled
        - jnp.mean(scaled, axis=-1, keepdims=True)
        - xhat * jnp.mean(scaled * xhat, axis=-1, keepdims=True)
    )


def total_rows(values):
    return jnp.sum(values, axis=0, keepdims=True)


def feed_kernel(
    mid,
    cot,
    ints,
    vec,
    up,
    up_bias,
    down,
    mixed,
    mid_grad,
    mid_low,
    small,
    up_bias_grad,
    up_grad,
    down_grad,
    normed2,
    grad_low,
    down_sum,
    norm_sum,
):
    j = pl.program_id(0)
    half = mid.shape[0]
    c = lax.rem(lax.axis_index("dp"), 2)
    live = row_live(ints[0:1, 0:1], c * half, half)

    @pl.when(j == 0)
    def _():
        xhat, rstd = centre(mid[...])
        normed2[...] = (xhat * vec[2:3, :] + vec[3:4, :]).astype(BF16)
        grad_low[...] = (cot[...].astype(F32) * live).astype(BF16)
        down_sum[...] = jnp.zeros_like(down_sum)
        norm_sum[...] = jnp.zeros_like(norm_sum)

    hidden = nt(normed2[...], up[...]) + up_bias[...]
    bell = 0.5 + 0.5 * lax.erf(hidden * ROOT_HALF)
    act = (hidden * bell).astype(BF16)
    slope = bell + hidden * (ROOT_TWO_PI_INV * jnp.exp(-0.5 * hidden * hidden))
    hidden_grad = nt(grad_low[...], down[...]) * slope
    up_bias_grad[...] = total_rows(hidden_grad)
    hidden_low = hidden_grad.astype(BF16)
    down_sum[...] += nn(act, down[...])
    norm_sum[...] += nn(hidden_low, up[...])
    up_grad[...] = tn(hidden_low, normed2[...]).astype(BF16)
    down_grad[...] = tn(act, grad_low[...]).astype(BF16)

    @pl.when(j == pl.num_programs(0) - 1)
    def _():
        middle = mid[...]
        mixed[...] = (live * (middle + (down_sum[...] + vec[5:6, :]))).astype(BF16)
        xhat, rstd = centre(middle)
        upstream = norm_sum[...]
        grad_out = grad_low[...].astype(F32)
        grad = grad_out + norm_back(xhat, rstd, vec[2:3, :], upstream)
        mid_grad[...] = grad
        mid_low[...] = grad.astype(BF16)
        small[0:1, :] = total_rows(upstream * xhat)
        small[1:2, :] = total_rows(upstream)
        small[2:3, :] = total_rows(grad)
        small[3:4, :] = total_rows(grad_out)
        small[4:8, :] = jnp.zeros((4, D), F32)


def backward_kernel(
    mid_low,
    weights,
    attended,
    mixed_heads,
    qs,
    keys,
    values,
    lse,
    normed,
    ints,
    grads,
    norm_own,
    norm_other,
    small,
    heads_grad,
    q_low,
    k_low,
    v_low,
):
    half = mid_low.shape[0]
    length = keys.shape[0]
    width = weights.shape[3]
    c = lax.rem(lax.axis_index("dp"), 2)
    base = pl.multiple_of(c * half, half)
    other = pl.multiple_of((1 - c) * half, half)
    count = ints[0:1, 0:1]
    for t in range(weights.shape[0]):
        cols = slice(t * width, (t + 1) * width)
        heads_grad[:, cols] = nn(mid_low[...], weights[t, 3]).astype(BF16)
        grads[t, 3] = tn(mid_low[...], attended[:, cols]).astype(BF16)
    product = heads_grad[...].astype(F32) * mixed_heads[...]
    head_of = lax.broadcasted_iota(jnp.int32, (16, D), 0)
    place = lax.broadcasted_iota(jnp.int32, (16, D), 1)
    pick = jnp.where(
        (place >= head_of * HD) & (place < head_of * HD + HD), 1.0, 0.0
    ).astype(BF16)
    hi = product.astype(BF16)
    delta = nt(pick, hi) + nt(pick, (product - hi.astype(F32)).astype(BF16))
    lane, own, mark = lane_sets()
    dead = ((1.0 - row_live(count, 0, length)) * DEAD).astype(BF16)
    block = 512
    for p in range(D // PAIR):
        cols = slice(p * PAIR, (p + 1) * PAIR)
        q_parts = []
        v_parts = [0.0] * (length // block)
        k_parts = [0.0] * (length // block)
        for h in range(2):
            head = 2 * p + h
            qx = qs[:, cols] * own[h] + mark[h]
            gx = heads_grad[:, cols] * own[h]
            q_sum = jnp.zeros((half, PAIR), F32)
            for b in range(length // block):
                span = slice(b * block, (b + 1) * block)
                kx = keys[span, cols] * own[h] + dead[span] * mark[h]
                probs = jnp.exp(nt(kx, qx) - lse[head : head + 1, :])
                prob_grad = nt(values[span, cols], gx)
                score_low = (probs * (prob_grad - delta[head : head + 1, :])).astype(BF16)
                v_parts[b] = v_parts[b] + nn(probs.astype(BF16), gx)
                k_parts[b] = k_parts[b] + nn(score_low, qx) * own[h].astype(F32)
                q_sum = q_sum + tn(score_low, kx)
            q_parts.append(q_sum)
        q_grad = jnp.where(lane < HD, q_parts[0], q_parts[1]) * HD**-0.5
        q_low[:, cols] = q_grad.astype(BF16)
        small[0:1, cols] = total_rows(q_grad)
        v_total = 0.0
        for b in range(length // block):
            span = slice(b * block, (b + 1) * block)
            k_low[span, cols] = k_parts[b].astype(BF16)
            v_low[span, cols] = v_parts[b].astype(BF16)
            v_total = v_total + total_rows(v_parts[b])
        small[1:2, cols] = v_total
    small[2:8, :] = jnp.zeros((6, D), F32)
    own_part = 0.0
    other_part = 0.0
    for t in range(weights.shape[0]):
        cols = slice(t * width, (t + 1) * width)
        grads[t, 0] = tn(normed[pl.ds(base, half), :], q_low[:, cols]).astype(BF16)
        grads[t, 1] = tn(normed[...], k_low[:, cols]).astype(BF16)
        grads[t, 2] = tn(normed[...], v_low[:, cols]).astype(BF16)
        own_part = (
            own_part
            + nt(q_low[:, cols], weights[t, 0])
            + nt(k_low[pl.ds(base, half), cols], weights[t, 1])
            + nt(v_low[pl.ds(base, half), cols], weights[t, 2])
        )
        other_part = (
            other_part
            + nt(k_low[pl.ds(other, half), cols], weights[t, 1])
            + nt(v_low[pl.ds(other, half), cols], weights[t, 2])
        )
    norm_own[...] = own_part
    norm_other[...] = other_part.astype(BF16)


def reduce_kernel(
    dp_size,
    attn,
    up,
    down,
    mixed,
    norm_own,
    norm_other,
    start_own,
    mid_grad,
    vec,
    small,
    ints,
    attn_sum,
    up_sum,
    down_sum,
    mixed_out,
    input_out,
    small_sum,
    attn_stage,
    attn_land,
    up_stage,
    up_land,
    down_stage,
    down_land,
    norm_land,
    input_half,
    small_send,
    small_land,
    send_sem,
    recv_sem,
    small_sem,
    spread_send,
    spread_recv,
    pair_sem,
):
    cube = Cube(dp_size)
    count = phases_of(dp_size)
    half = norm_own.shape[0]
    enter([cube.partner(p) for p in range(count)] + [cube.diagonal])
    exchange = pltpu.make_async_remote_copy(
        src_ref=norm_other,
        dst_ref=norm_land,
        send_sem=pair_sem.at[0],
        recv_sem=pair_sem.at[1],
        device_id=cube.sibling,
        device_id_type=MESH,
    )
    exchange.start()
    jobs = [
        Scatter(cube, count, part, stage, land, send_sem.at[k], recv_sem.at[k])
        for k, (part, stage, land) in enumerate(
            (
                (lambda dp, t: down.at[dp, t], down_stage, down_land),
                (lambda dp, t: up.at[dp, t], up_stage, up_land),
                (lambda dp, t: attn.at[t, :, dp], attn_stage, attn_land),
            )
        )
    ]
    for job in jobs:
        job.start()
    wait_mixed = spread(cube, mixed, mixed_out, spread_send.at[0], spread_recv.at[0])
    exchange.wait()
    upstream = norm_own[...] + norm_land[...].astype(F32)
    xhat, rstd = centre(start_own[...])
    live = row_live(ints[0:1, 0:1], cube.core * half, half)
    grad = mid_grad[...] + norm_back(xhat, rstd, vec[0:1, :], upstream)
    input_half[...] = (live * grad).astype(BF16)
    wait_input = spread(cube, input_half, input_out, spread_send.at[1], spread_recv.at[1])
    small_send[0] = small[...]
    small_send[0, 0:1, :] = total_rows(upstream * xhat)
    small_send[0, 1:2, :] = total_rows(upstream)
    smalls = []

    def small_step(p):
        copy = pltpu.make_async_remote_copy(
            src_ref=small_send.at[p],
            dst_ref=small_land.at[p],
            send_sem=small_sem.at[0, p],
            recv_sem=small_sem.at[1, p],
            device_id=cube.partner(p),
            device_id_type=MESH,
        )
        copy.start()
        smalls.append(copy)

    def small_close(p):
        smalls[p].wait_recv()
        value = small_send[p] + small_land[p]
        if p + 1 < count:
            small_send[p + 1] = value
        else:
            small_sum[...] = value

    small_step(0)
    for job in jobs:
        for k in range(len(job.rest) - 1):
            job.step(k)
    for p in range(count):
        small_close(p)
        if p + 1 < count:
            small_step(p + 1)
    down_sum[...] = jobs[0].last()
    up_sum[...] = jobs[1].last()
    attn_sum[...] = jobs[2].last()
    wait_mixed()
    wait_input()
    exchange_done = smalls
    for copy in exchange_done:
        copy.wait_send()
    for job in jobs:
        job.finish()


ANY = pl.BlockSpec(memory_space=pl.ANY)
VMEM = pl.BlockSpec(memory_space=pltpu.VMEM)


def shape(dims, kind):
    return jax.ShapeDtypeStruct(dims, kind)


def local(
    dp_size,
    tokens,
    counts,
    indices,
    ground_dist,
    cotangent,
    attn_weight,
    attn_bias,
    out_weight,
    vectors,
    up_weight,
    up_bias,
    down_weight,
):
    tensor = 2
    chips, length, width = tokens.shape
    half = length // 2
    attn_rows, attn_cols = attn_weight.shape[1:]
    ff_rows = down_weight.shape[0]
    ff = ff_rows * dp_size * tensor
    count = phases_of(dp_size)
    devices = 1 << count
    dp = lax.axis_index("dp")
    t = lax.axis_index("tensor")

    attn_pack = jnp.concatenate([attn_weight, out_weight.T[None]], axis=0).astype(BF16)
    up_pack = up_weight.T.astype(BF16)
    down_pack = down_weight.astype(BF16)
    flat = jnp.concatenate(
        [vectors.reshape(-1), attn_bias.reshape(-1), up_bias.reshape(-1)]
    ).astype(BF16)
    vec_size, bias_size = vectors.size, attn_bias.size
    used = flat.shape[0]
    packs = jnp.pad(flat, (0, 16 * 128 - used)).reshape(16, 128)
    ints = jnp.concatenate([counts, ground_dist, indices[0]]).astype(jnp.int32)
    ints = jnp.broadcast_to(ints[None, :], (8, length))

    big = [
        shape((2, length, width), BF16),
        shape((2, half, width), BF16),
        shape((2, 8, length), jnp.int32),
        shape((dp_size, tensor, 16, 128), BF16),
        shape((tensor, 4, dp_size, attn_rows, attn_cols), BF16),
        shape((dp_size, tensor, ff_rows, width), BF16),
        shape((dp_size, tensor, ff_rows, width), BF16),
    ]
    tok2, cot2, ints2, packs_all, attn_all, up_all, down_all = pl.pallas_call(
        functools.partial(gather_kernel, dp_size),
        name="gather",
        out_shape=big,
        in_specs=[ANY] * 7,
        out_specs=[ANY] * 7,
        scratch_shapes=[
            pltpu.SemaphoreType.DMA((4, devices)),
            pltpu.SemaphoreType.DMA((4, devices)),
            pltpu.SemaphoreType.DMA((2, 3)),
            pltpu.SemaphoreType.DMA((7,)),
        ],
        compiler_params=pltpu.CompilerParams(
            collective_id=0, has_side_effects=True, vmem_limit_bytes=32 * MIB
        ),
    )(tokens[0], cotangent[0], ints, packs, attn_pack, up_pack, down_pack)

    tok = lax.dynamic_index_in_dim(tok2, t, 0, False)
    cot = lax.dynamic_index_in_dim(cot2, t, 0, False)
    image = lax.dynamic_index_in_dim(ints2, t, 0, False)
    weights = attn_all.reshape(tensor, 4, width, attn_cols)
    up_t = up_all.reshape(ff, width)
    down = down_all.reshape(ff, width)
    every = packs_all.reshape(dp_size, tensor, 16 * 128).astype(F32)
    vec = (
        every[:, 0, :vec_size]
        .reshape(dp_size, 6, attn_rows)
        .transpose(1, 0, 2)
        .reshape(6, width)
    )
    vec = jnp.pad(vec, ((0, 2), (0, 0)))
    heads = attn_bias.shape[1]
    bias = (
        every[:, :, vec_size : vec_size + bias_size]
        .reshape(dp_size, tensor, 2, heads, attn_bias.shape[2])
        .transpose(2, 1, 3, 0, 4)
        .reshape(2, width)
    )
    bias = jnp.pad(bias, ((0, 6), (0, 0)))
    hidden_bias = every[:, :, vec_size + bias_size : used].reshape(1, ff)

    quarter = width // 4
    omega = 1.0 / 10000.0 ** (jnp.arange(quarter, dtype=F32) / quarter)
    scale = image[0, 1].astype(F32) / 10.0
    angle = jnp.arange(GRID, dtype=F32)[:, None] * scale * omega
    table = jnp.concatenate([jnp.sin(angle), jnp.cos(angle)], axis=1)

    normed, start_own, qs, keys, values, mixed_heads, attended, lse, mid = pl.pallas_call(
        forward_kernel,
        name="attend",
        out_shape=[
            shape((length, width), BF16),
            shape((half, width), F32),
            shape((half, width), BF16),
            shape((length, width), BF16),
            shape((length, width), BF16),
            shape((half, width), F32),
            shape((half, width), BF16),
            shape((PAIR, half), F32),
            shape((half, width), F32),
        ],
        in_specs=[VMEM] * 6,
        out_specs=[VMEM] * 9,
        scratch_shapes=[pltpu.VMEM((length, width), F32)],
        compiler_params=pltpu.CompilerParams(vmem_limit_bytes=60 * MIB),
    )(tok, image, table, weights, vec, bias)

    tile = 512
    whole = lambda dims: pl.BlockSpec(dims, lambda j: (0,) * len(dims))
    mixed, mid_grad, mid_low, small_ff, up_bias_grad, up_grad, down_grad = pl.pallas_call(
        feed_kernel,
        name="feed",
        grid=(ff // tile,),
        out_shape=[
            shape((half, width), BF16),
            shape((half, width), F32),
            shape((half, width), BF16),
            shape((8, width), F32),
            shape((1, ff), F32),
            shape((ff, width), BF16),
            shape((ff, width), BF16),
        ],
        in_specs=[
            whole((half, width)),
            whole((half, width)),
            whole((8, length)),
            whole((8, width)),
            pl.BlockSpec((tile, width), lambda j: (j, 0)),
            pl.BlockSpec((1, tile), lambda j: (0, j)),
            pl.BlockSpec((tile, width), lambda j: (j, 0)),
        ],
        out_specs=[
            whole((half, width)),
            whole((half, width)),
            whole((half, width)),
            whole((8, width)),
            pl.BlockSpec((1, tile), lambda j: (0, j)),
            pl.BlockSpec((tile, width), lambda j: (j, 0)),
            pl.BlockSpec((tile, width), lambda j: (j, 0)),
        ],
        scratch_shapes=[
            pltpu.VMEM((half, width), BF16),
            pltpu.VMEM((half, width), BF16),
            pltpu.VMEM((half, width), F32),
            pltpu.VMEM((half, width), F32),
        ],
        compiler_params=pltpu.CompilerParams(vmem_limit_bytes=60 * MIB),
    )(mid, cot, image, vec, up_t, hidden_bias, down)

    grads, norm_own, norm_other, small_attn = pl.pallas_call(
        backward_kernel,
        name="attend_back",
        out_shape=[
            shape((tensor, 4, width, attn_cols), BF16),
            shape((half, width), F32),
            shape((half, width), BF16),
            shape((8, width), F32),
        ],
        in_specs=[VMEM] * 10,
        out_specs=[VMEM] * 4,
        scratch_shapes=[
            pltpu.VMEM((half, width), BF16),
            pltpu.VMEM((half, width), BF16),
            pltpu.VMEM((length, width), BF16),
            pltpu.VMEM((length, width), BF16),
        ],
        compiler_params=pltpu.CompilerParams(vmem_limit_bytes=60 * MIB),
    )(mid_low, weights, attended, mixed_heads, qs, keys, values, lse, normed, image)

    small = jnp.concatenate(
        [
            jnp.zeros((2, width), F32),
            small_ff[:4],
            small_attn[:2],
            up_bias_grad.reshape(ff // width, width),
        ],
        axis=0,
    )
    small = jnp.pad(small, ((0, -small.shape[0] % 8), (0, 0)))
    attn_dims = (4, attn_rows, attn_cols)
    ff_dims = (ff_rows, width)
    staged = devices // 2
    attn_sum, up_sum, down_sum, mixed_out, input_out, small_sum = pl.pallas_call(
        functools.partial(reduce_kernel, dp_size),
        name="reduce",
        out_shape=[
            shape(attn_dims, F32),
            shape(ff_dims, F32),
            shape(ff_dims, F32),
            shape((2, half, width), BF16),
            shape((2, half, width), BF16),
            shape(small.shape, F32),
        ],
        in_specs=[VMEM] * 3 + [ANY] + [VMEM] * 7,
        out_specs=[VMEM] * 3 + [ANY] * 2 + [VMEM],
        scratch_shapes=[
            pltpu.VMEM((staged,) + attn_dims, BF16),
            pltpu.VMEM((devices,) + attn_dims, BF16),
            pltpu.VMEM((staged,) + ff_dims, BF16),
            pltpu.VMEM((devices,) + ff_dims, BF16),
            pltpu.VMEM((staged,) + ff_dims, BF16),
            pltpu.VMEM((devices,) + ff_dims, BF16),
            pltpu.VMEM((half, width), BF16),
            pltpu.VMEM((half, width), BF16),
            pltpu.VMEM((count,) + small.shape, F32),
            pltpu.VMEM((count,) + small.shape, F32),
            pltpu.SemaphoreType.DMA((3, devices)),
            pltpu.SemaphoreType.DMA((3, devices)),
            pltpu.SemaphoreType.DMA((2, count)),
            pltpu.SemaphoreType.DMA((2, 2)),
            pltpu.SemaphoreType.DMA((2, 2)),
            pltpu.SemaphoreType.DMA((2,)),
        ],
        compiler_params=pltpu.CompilerParams(
            collective_id=1, has_side_effects=True, vmem_limit_bytes=62 * MIB
        ),
    )(
        grads.reshape(tensor, 4, dp_size, attn_rows, attn_cols),
        up_grad.reshape(dp_size, tensor, ff_rows, width),
        down_grad.reshape(dp_size, tensor, ff_rows, width),
        mixed,
        norm_own,
        norm_other,
        start_own,
        mid_grad,
        vec,
        small,
        image,
    )

    vec_grad = lax.dynamic_slice_in_dim(small_sum[:6], dp * attn_rows, attn_rows, 1)
    bias_grad = small_sum[6:8].reshape(2, tensor, heads, dp_size, attn_bias.shape[2])
    bias_grad = lax.dynamic_index_in_dim(bias_grad, t, 1, False)
    bias_grad = lax.dynamic_index_in_dim(bias_grad, dp, 2, False)
    hidden_grad = small_sum[8 : 8 + ff // width].reshape(ff)
    hidden_grad = lax.dynamic_slice_in_dim(hidden_grad, (dp * tensor + t) * ff_rows, ff_rows, 0)
    return (
        mixed_out.reshape(1, length, width),
        input_out.reshape(1, length, width),
        attn_sum[:3],
        bias_grad,
        attn_sum[3].T,
        vec_grad,
        up_sum.T,
        hidden_grad,
        down_sum,
    )


def solution(mesh):
    placed = (
        P("dp", None, None),
        P("dp"),
        P("dp", None),
        P("dp"),
        P("dp", None, None),
        P(None, "dp", "tensor"),
        P(None, "tensor", "dp"),
        P("tensor", "dp"),
        P(None, "dp"),
        P(None, ("dp", "tensor")),
        P(("dp", "tensor")),
        P(("dp", "tensor"), None),
    )
    return jax.shard_map(
        functools.partial(local, mesh.shape["dp"]),
        mesh=mesh,
        in_specs=placed,
        out_specs=(
            P("dp", None, None),
            P("dp", None, None),
            P(None, "dp", "tensor"),
            P(None, "tensor", "dp"),
            P("tensor", "dp"),
            P(None, "dp"),
            P(None, ("dp", "tensor")),
            P(("dp", "tensor")),
            P(("dp", "tensor"), None),
        ),
        check_vma=False,
    )
```

```python
import functools

import jax
import jax.numpy as jnp
from jax import lax
from jax.experimental import pallas as pl
from jax.experimental.pallas import tpu as pltpu
from jax.sharding import PartitionSpec as P

D = 768
HD = 64
GRID = 32
EPS = 1e-06
DEAD = -1e30
PAIR = 2 * HD
ROOT_HALF = 0.7071067811865476
ROOT_TWO_PI_INV = 0.3989422804014327

F32 = jnp.float32
BF16 = jnp.bfloat16
MESH = pl.DeviceIdType.MESH
MIB = 1 << 20


def nn(a, b):
    return lax.dot_general(a, b, (((1,), (0,)), ((), ())), preferred_element_type=F32)


def nt(a, b):
    return lax.dot_general(a, b, (((1,), (1,)), ((), ())), preferred_element_type=F32)


def tn(a, b):
    return lax.dot_general(a, b, (((0,), (0,)), ((), ())), preferred_element_type=F32)


class Path:
    def __init__(self, cube, steps, mirror):
        self.cube, self.steps, self.mirror = cube, steps, mirror
        self.count = len(steps)

    def partner(self, p):
        return (self.cube.dp + self.steps[p][0], self.cube.t + self.steps[p][1])

    def entry(self, mask):
        dp, t = self.cube.dp, self.cube.t
        for p, (ddp, dt) in enumerate(self.steps):
            if mask >> p & 1:
                dp, t = dp + ddp, t + dt
        return dp, t

    def mirrored(self, mask):
        if self.mirror is None:
            return mask
        i, j = self.mirror
        return mask & ~(1 << i | 1 << j) | (mask >> i & 1) << j | (mask >> j & 1) << i


class Cube:
    def __init__(self, dp_size):
        self.dp = lax.axis_index("dp")
        self.t = lax.axis_index("tensor")
        self.core = lax.rem(self.dp, 2)

        def flip(b):
            return b * (1 - 2 * lax.rem(lax.div(self.dp, b), 2))

        self.dt, self.dy, self.dc = 1 - 2 * self.t, flip(2), flip(1)
        self.far = []
        b = dp_size // 2
        while b >= 4:
            self.far.append((flip(b), 0))
            b //= 2
        self.sibling = (self.dp + self.dc, self.t)
        self.across = (self.dp, self.t + self.dt)
        self.diagonal = (self.dp + self.dc, self.t + self.dt)

    def path(self, first, wrap):
        s = {"x": 0, "y": 1, "core": self.core}[first]
        a = (s * self.dy, (1 - s) * self.dt)
        b = ((1 - s) * self.dy, s * self.dt)
        n = len(self.far)
        steps = [a, *self.far, b] if wrap else [*self.far, a, b]
        mirror = ((0, n + 1) if wrap else (n, n + 1)) if first == "core" else None
        return Path(self, steps + [(self.dc, 0)], mirror)

    def partners(self):
        return [(self.dp + ddp, self.t + dt) for ddp, dt in self.far] + [
            (self.dp + self.dy, self.t),
            self.across,
            self.sibling,
        ]


def phases_of(dp_size):
    return (2 * dp_size).bit_length() - 1


def enter(devices):
    barrier = pltpu.get_barrier_semaphore()
    for device in devices:
        pl.semaphore_signal(barrier, inc=1, device_id=device, device_id_type=MESH)
    pl.semaphore_wait(barrier, len(devices))


class Gather:
    def __init__(self, path, own, slot, send_sem, recv_sem):
        self.path, self.own, self.slot = path, own, slot
        self.send_sem, self.recv_sem = send_sem, recv_sem
        self.count = path.count
        self.sent = []
        self.order = sorted(
            ((p, m) for p in range(self.count) for m in range(1 << p)),
            key=lambda item: (item[1].bit_count(), item[0], item[1]),
        )

    def copy(self, p, mask, place, source):
        k = (1 << p) - 1 + mask
        there = (1 << p) - 1 + (self.path.mirrored(mask) if p == self.count - 1 else mask)
        return pltpu.make_async_remote_copy(
            src_ref=source,
            dst_ref=place,
            send_sem=self.send_sem.at[k],
            recv_sem=self.recv_sem.at[there],
            device_id=self.path.partner(p),
            device_id_type=MESH,
        )

    def send(self, p, mask):
        place = self.slot(*self.path.entry(mask))
        copy = self.copy(p, mask, place, self.own if mask == 0 else place)
        copy.start()
        self.sent.append(copy)

    def start(self):
        for p in range(self.count):
            self.send(p, 0)

    def step(self, k):
        p, mask = self.order[k]
        place = self.slot(*self.path.entry(mask | 1 << p))
        there = self.path.mirrored(mask) if p == self.count - 1 else mask
        self.copy(p, there, place, place).wait_recv()
        for later in range(p + 1, self.count):
            self.send(later, mask | 1 << p)

    def finish(self):
        for copy in self.sent:
            copy.wait_send()


def low_bit(m):
    return (m & -m).bit_length() - 1 if m else 99


class Scatter:
    def __init__(self, path, part, staged, landed, send_sem, recv_sem):
        self.path, self.count = path, path.count
        self.part, self.staged, self.landed = part, staged, landed
        self.send_sem, self.recv_sem = send_sem, recv_sem
        self.sent = []
        masks = list(range(1, 1 << self.count))
        masks.sort(key=lambda m: (low_bit(m), low_bit(m & (m - 1)), m))
        self.order = masks + [0]
        self.rest = [m for m in masks if not m & 1]

    def reverse(self, m):
        return sum((m >> q & 1) << (self.count - 1 - q) for q in range(self.count))

    def entry(self, m):
        return self.path.entry(self.reverse(m))

    def mirrored(self, m):
        return self.reverse(self.path.mirrored(self.reverse(m)))

    def index(self, q, m):
        return (1 << (self.count - 1 - q)) - 1 + (m >> (q + 1))

    def describe(self, q, m, source):
        k = self.index(q, self.mirrored(m) if q == 0 else m)
        return pltpu.make_async_remote_copy(
            src_ref=source,
            dst_ref=self.landed.at[k],
            send_sem=self.send_sem.at[k],
            recv_sem=self.recv_sem.at[k],
            device_id=self.path.partner(self.count - 1 - q),
            device_id_type=MESH,
        )

    def start(self):
        for m in self.order:
            if m & 1:
                m = self.mirrored(m)
                copy = self.describe(0, m, self.part(*self.entry(m)))
                copy.start()
                self.sent.append(copy)

    def total(self, m):
        total = self.part(*self.entry(m))[...].astype(F32)
        for q in range(min(low_bit(m), self.count)):
            k = self.index(q, m)
            self.describe(q, self.mirrored(m) if q == 0 else m, self.landed.at[k]).wait_recv()
            total = total + self.landed[k].astype(F32)
        return total

    def step(self, k):
        m = self.rest[k]
        q = low_bit(m)
        j = self.index(q, m)
        self.staged[j] = self.total(m).astype(BF16)
        copy = self.describe(q, m, self.staged.at[j])
        copy.start()
        self.sent.append(copy)

    def last(self):
        return self.total(0)

    def finish(self):
        for copy in self.sent:
            copy.wait_send()


def spread(cube, half, out, send_sem, recv_sem):
    c, t = cube.core, cube.t
    mine = out.at[c]

    def push(device, k):
        return pltpu.make_async_remote_copy(
            src_ref=half,
            dst_ref=mine,
            send_sem=send_sem.at[k],
            recv_sem=recv_sem.at[c],
            device_id=device,
            device_id_type=MESH,
        )

    def arrival(h):
        return pltpu.make_async_remote_copy(
            src_ref=half,
            dst_ref=out.at[h],
            send_sem=send_sem.at[0],
            recv_sem=recv_sem.at[h],
            device_id=cube.sibling,
            device_id_type=MESH,
        )

    keep = pltpu.make_async_copy(half, mine, send_sem.at[0])

    @pl.when(c == t)
    def _():
        push(cube.across, 1).start()
        keep.start()

    @pl.when(c != t)
    def _():
        push(cube.diagonal, 1).start()
        push(cube.sibling, 0).start()

    def wait():
        @pl.when(c == t)
        def _():
            keep.wait()
            push(cube.across, 1).wait_send()
            arrival(1 - c).wait_recv()

        @pl.when(c != t)
        def _():
            push(cube.sibling, 0).wait_send()
            push(cube.diagonal, 1).wait_send()
            arrival(c).wait_recv()
            arrival(1 - c).wait_recv()

    return wait


PACK = 32


def gather_kernel(
    dp_size,
    tok,
    cot,
    ints,
    attn_f,
    out_f,
    up_f,
    down_f,
    vec_f,
    bias_f,
    hidden_f,
    tok2,
    cot2,
    ints2,
    packs_all,
    attn_all,
    up,
    down,
    attn_in,
    out_in,
    up_in,
    down_in,
    vec_in,
    bias_in,
    hidden_in,
    attn,
    pack,
    up_low,
    down_low,
    send_sem,
    recv_sem,
    pair_sem,
    local_sem,
):
    cube = Cube(dp_size)
    rows = cot2.shape[1]
    c = cube.core
    other = pl.ds(pl.multiple_of((1 - c) * rows, rows), rows)
    own = pl.ds(pl.multiple_of(c * rows, rows), rows)
    loads = [
        pltpu.make_async_copy(source, target, local_sem.at[k])
        for k, (source, target) in enumerate(
            (
                (attn_f, attn_in),
                (out_f, out_in),
                (vec_f, vec_in),
                (bias_f, bias_in),
                (hidden_f, hidden_in),
                (up_f, up_in),
                (down_f, down_in),
            )
        )
    ]
    for copy in loads:
        copy.start()
    keeps = [
        pltpu.make_async_copy(tok, tok2.at[c], local_sem.at[7]),
        pltpu.make_async_copy(cot.at[own], cot2.at[c], local_sem.at[8]),
        pltpu.make_async_copy(ints, ints2.at[c], local_sem.at[9]),
    ]
    for copy in keeps:
        copy.start()
    for copy in loads[:5]:
        copy.wait()
    attn[0:3] = attn_in[...].astype(BF16)
    attn[3] = out_in[...].T.astype(BF16)
    pack[...] = jnp.zeros_like(pack)
    pack[0:6, 0 : vec_in.shape[1]] = vec_in[...]
    pack[6:7, 0 : hidden_in.shape[1]] = hidden_in[...]
    for k in range(2):
        pack[8 + 8 * k : 8 + 8 * k + bias_in.shape[1], 0 : bias_in.shape[2]] = bias_in[k]
    pack_low = pack[...].astype(BF16)
    packs_all[cube.dp, cube.t] = pack_low
    enter(cube.partners())
    keep = pltpu.make_async_copy(attn, attn_all.at[cube.t, :, cube.dp], local_sem.at[10])
    keep.start()
    jobs = [
        Gather(
            cube.path("core", True),
            packs_all.at[cube.dp, cube.t],
            lambda dp, t: packs_all.at[dp, t],
            send_sem.at[0],
            recv_sem.at[0],
        )
    ]
    for k in range(2):
        span = slice(2 * k, 2 * k + 2)
        jobs.append(
            Gather(
                cube.path("core", k == 1),
                attn.at[span],
                lambda dp, t, span=span: attn_all.at[t, span, dp],
                send_sem.at[k + 1],
                recv_sem.at[k + 1],
            )
        )
    for job in jobs:
        job.start()
    pairs = [
        pltpu.make_async_remote_copy(
            src_ref=source,
            dst_ref=target.at[c],
            send_sem=pair_sem.at[0, k],
            recv_sem=pair_sem.at[1, k],
            device_id=cube.sibling,
            device_id_type=MESH,
        )
        for k, (source, target) in enumerate(
            ((ints, ints2), (tok, tok2), (cot.at[other], cot2))
        )
    ]
    for copy in pairs:
        copy.start()
    for copy in loads[5:]:
        copy.wait()
    up_low[...] = up_in[...].T.astype(BF16)
    down_low[...] = down_in[...].astype(BF16)
    stores = [
        pltpu.make_async_copy(up_low, up, local_sem.at[11]),
        pltpu.make_async_copy(down_low, down, local_sem.at[12]),
    ]
    for copy in stores:
        copy.start()
    for k in range(len(jobs[0].order)):
        for job in jobs:
            job.step(k)
    for job in jobs:
        job.finish()
    for copy in pairs:
        copy.wait()
    for copy in keeps + [keep] + stores:
        copy.wait()


def centre(values):
    mean = jnp.mean(values, axis=-1, keepdims=True)
    centred = values - mean
    rstd = lax.rsqrt(jnp.mean(centred * centred, axis=-1, keepdims=True) + EPS)
    return centred * rstd, rstd


def row_live(count, offset, rows):
    places = lax.broadcasted_iota(jnp.int32, (rows, 1), 0) + offset
    return (places < count + 2).astype(F32)


def lane_sets():
    lane = lax.broadcasted_iota(jnp.int32, (1, PAIR), 1)
    own = [(lane < HD).astype(F32).astype(BF16), (lane >= HD).astype(F32).astype(BF16)]
    mark = [(lane == HD).astype(F32).astype(BF16), (lane == 0).astype(F32).astype(BF16)]
    return lane, own, mark


def place_rows(rows, offset, columns):
    a, r = divmod(offset, 128)
    lane = lax.broadcasted_iota(jnp.int32, rows.shape, 1)
    turned = pltpu.roll(rows, r, 1) if r else rows
    columns[a] = columns[a] + jnp.where(lane >= r, turned, 0.0)
    if r and a + 1 < len(columns):
        columns[a + 1] = columns[a + 1] + jnp.where(lane < r, turned, 0.0)


def read_packs(dp_size, heads, packs, vec, bias, hidden):
    per = vec.shape[1] // dp_size
    tensor = packs.shape[1]
    each = hidden.shape[1] // (dp_size * tensor)
    row = lax.broadcasted_iota(jnp.int32, (8, 128), 0)
    vec_columns = [jnp.zeros((8, 128), F32) for k in range(vec.shape[1] // 128)]
    hidden_columns = [jnp.zeros((1, 128), F32) for k in range(hidden.shape[1] // 128)]
    spans = [[jnp.zeros((8, 128), F32) for k in range(2)] for t in range(tensor)]
    for dp in range(dp_size):
        for t in range(tensor):
            data = packs[dp, t].astype(F32)
            if t == 0:
                place_rows(jnp.where(row < 6, data[0:8], 0.0), dp * per, vec_columns)
            place_rows(data[6:7], (dp * tensor + t) * each, hidden_columns)
            for k in range(2):
                turn = dp * (HD // dp_size)
                part = data[8 + 8 * k : 16 + 8 * k]
                spans[t][k] = spans[t][k] + (pltpu.roll(part, turn, 1) if turn else part)
    for k, column in enumerate(vec_columns):
        vec[:, k * 128 : (k + 1) * 128] = column
    for k, column in enumerate(hidden_columns):
        hidden[:, k * 128 : (k + 1) * 128] = column
    for k in range(2):
        columns = [jnp.zeros((1, 128), F32) for j in range(bias.shape[1] // 128)]
        for t in range(tensor):
            for h in range(heads):
                place_rows(spans[t][k][h : h + 1], (t * heads + h) * HD, columns)
        for j, column in enumerate(columns):
            bias[k : k + 1, j * 128 : (j + 1) * 128] = column


def forward_kernel(
    dp_size,
    heads,
    tok2,
    ints2,
    omega,
    packs,
    weights_all,
    up,
    down,
    normed,
    start_own,
    qs,
    keys,
    values,
    mixed_heads,
    attended,
    lse,
    mid,
    vec,
    hidden_bias,
    ints,
    weights,
    up_all,
    down_all,
    start,
    tok,
    bias,
    send_sem,
    recv_sem,
    local_sem,
):
    cube = Cube(dp_size)
    c, own_image = cube.core, cube.t
    loads = [
        pltpu.make_async_copy(ints2.at[own_image], ints, local_sem.at[0]),
        pltpu.make_async_copy(tok2.at[own_image], tok, local_sem.at[1]),
        pltpu.make_async_copy(weights_all, weights, local_sem.at[3]),
    ]
    for copy in loads:
        copy.start()
    keeps = [
        pltpu.make_async_copy(up, up_all.at[cube.dp, cube.t], local_sem.at[4]),
        pltpu.make_async_copy(down, down_all.at[cube.dp, cube.t], local_sem.at[5]),
    ]
    for copy in keeps:
        copy.start()
    enter(cube.partners())
    jobs = [
        Gather(
            cube.path("core", k == 1),
            source,
            lambda dp, t, target=target: target.at[dp, t],
            send_sem.at[k],
            recv_sem.at[k],
        )
        for k, (source, target) in enumerate(((up, up_all), (down, down_all)))
    ]
    for job in jobs:
        job.start()
    todo = [(job, k) for k in range(len(jobs[0].order)) for job in jobs]

    def pump(number):
        for job, k in todo[:number]:
            job.step(k)
        del todo[:number]

    length = tok.shape[0]
    half = start_own.shape[0]
    base = pl.multiple_of(c * half, half)
    for copy in loads[:2]:
        copy.wait()
    read_packs(dp_size, heads, packs, vec, bias, hidden_bias)
    count = ints[0:1, 0:1]
    quarter = D // 4
    scale = ints[0:1, 1:2].astype(F32) / 10.0
    angle = lax.broadcasted_iota(jnp.int32, (GRID, 2 * quarter), 0).astype(F32) * scale * omega[0:1, :]
    wave = lax.broadcasted_iota(jnp.int32, (GRID, 2 * quarter), 1)
    full = jnp.where(wave < quarter, jnp.sin(angle), jnp.cos(angle))
    hi = full.astype(BF16)
    rest = full - hi.astype(F32)
    middle = rest.astype(BF16)
    little = (rest - middle.astype(F32)).astype(BF16)
    stack = jnp.concatenate([hi, middle, little], axis=0)
    tile = 256
    for r in range(length // tile):
        span = slice(r * tile, (r + 1) * tile)
        index = ints[0:1, span]
        slots = lax.broadcasted_iota(jnp.int32, (1, tile), 1) + r * tile
        places = lax.broadcasted_iota(jnp.int32, (GRID, tile), 0)
        parts = []
        for part in (lax.shift_right_logical(index, 5), lax.bitwise_and(index, GRID - 1)):
            part = jnp.where(slots < 2, -1, part)
            hot = (places == part).astype(F32).astype(BF16)
            parts.append(tn(jnp.concatenate([hot, hot, hot], axis=0), stack))
        code = jnp.concatenate(parts, axis=1)
        live = row_live(count, r * tile, tile)
        rows = (tok[span, :].astype(F32) + code) * live
        start[span, :] = rows
        xhat, rstd = centre(rows)
        normed[span, :] = (xhat * vec[0:1, :] + vec[1:2, :]).astype(BF16)
    start_own[...] = start[pl.ds(base, half), :]
    loads[2].wait()
    pump(4)
    width = weights.shape[3]
    for t in range(weights.shape[0]):
        cols = slice(t * width, (t + 1) * width)
        query = nn(normed[pl.ds(base, half), :], weights[t, 0]) + bias[0:1, cols]
        qs[:, cols] = query.astype(BF16) * jnp.asarray(HD**-0.5, BF16)
        for r in range(length // half):
            span = slice(r * half, (r + 1) * half)
            keys[span, cols] = nn(normed[span, :], weights[t, 1]).astype(BF16)
            values[span, cols] = (nn(normed[span, :], weights[t, 2]) + bias[1:2, cols]).astype(BF16)
    pump(4)
    lane, own, mark = lane_sets()
    dead = ((1.0 - row_live(count, 0, length)) * DEAD).astype(BF16)
    wide = lax.broadcasted_iota(jnp.int32, (1, PAIR), 1)
    block = 256
    for r in range(half // block):
        span = slice(r * block, (r + 1) * block)
        sums = jnp.zeros((block, PAIR), F32)
        for p in range(D // PAIR):
            cols = slice(p * PAIR, (p + 1) * PAIR)
            outs = []
            for h in range(2):
                kx = keys[:, cols] * own[h] + dead * mark[h]
                qx = qs[span, cols] * own[h] + mark[h]
                scores = nt(qx, kx)
                top = jnp.max(scores, axis=1, keepdims=True)
                grown = jnp.exp(scores - top)
                total = jnp.sum(grown, axis=1, keepdims=True)
                outs.append(nn(grown.astype(BF16), values[:, cols]) / total)
                sums = jnp.where(wide == 2 * p + h, top + jnp.log(total), sums)
            both = jnp.where(lane < HD, outs[0], outs[1])
            mixed_heads[span, cols] = both
            attended[span, cols] = both.astype(BF16)
            pump(2)
        lse[:, span] = sums.T
    out = nt(attended[:, :width], weights[0, 3])
    for t in range(1, weights.shape[0]):
        out = out + nt(attended[:, t * width : (t + 1) * width], weights[t, 3])
    mid[...] = start_own[...] + (out + vec[4:5, :])
    pump(len(todo))
    for job in jobs:
        job.finish()
    for copy in keeps:
        copy.wait()


def norm_back(xhat, rstd, gain, upstream):
    scaled = upstream * gain
    return rstd * (
        scaled
        - jnp.mean(scaled, axis=-1, keepdims=True)
        - xhat * jnp.mean(scaled * xhat, axis=-1, keepdims=True)
    )


def total_rows(values):
    return jnp.sum(values, axis=0, keepdims=True)


def feed_kernel(
    mid,
    cot2,
    ints,
    vec,
    up,
    up_bias,
    down,
    mixed,
    mid_grad,
    mid_low,
    small,
    up_bias_grad,
    up_grad,
    down_grad,
    normed2,
    grad_low,
    down_sum,
    norm_sum,
    cot,
    local_sem,
):
    j = pl.program_id(0)
    half = mid.shape[0]
    c = lax.rem(lax.axis_index("dp"), 2)
    live = row_live(ints[0:1, 0:1], c * half, half)

    @pl.when(j == 0)
    def _():
        load = pltpu.make_async_copy(cot2.at[lax.axis_index("tensor")], cot, local_sem)
        load.start()
        xhat, rstd = centre(mid[...])
        load.wait()
        normed2[...] = (xhat * vec[2:3, :] + vec[3:4, :]).astype(BF16)
        grad_low[...] = (cot[...].astype(F32) * live).astype(BF16)
        down_sum[...] = jnp.zeros_like(down_sum)
        norm_sum[...] = jnp.zeros_like(norm_sum)

    hidden = nt(normed2[...], up[...]) + up_bias[...]
    bell = 0.5 + 0.5 * lax.erf(hidden * ROOT_HALF)
    act = (hidden * bell).astype(BF16)
    slope = bell + hidden * (ROOT_TWO_PI_INV * jnp.exp(-0.5 * hidden * hidden))
    hidden_grad = nt(grad_low[...], down[...]) * slope
    up_bias_grad[...] = total_rows(hidden_grad)
    hidden_low = hidden_grad.astype(BF16)
    down_sum[...] += nn(act, down[...])
    norm_sum[...] += nn(hidden_low, up[...])
    up_grad[...] = tn(hidden_low, normed2[...]).astype(BF16)
    down_grad[...] = tn(act, grad_low[...]).astype(BF16)

    @pl.when(j == pl.num_programs(0) - 1)
    def _():
        middle = mid[...]
        mixed[...] = (live * (middle + (down_sum[...] + vec[5:6, :]))).astype(BF16)
        xhat, rstd = centre(middle)
        upstream = norm_sum[...]
        grad_out = grad_low[...].astype(F32)
        grad = grad_out + norm_back(xhat, rstd, vec[2:3, :], upstream)
        mid_grad[...] = grad
        mid_low[...] = grad.astype(BF16)
        small[0:1, :] = total_rows(upstream * xhat)
        small[1:2, :] = total_rows(upstream)
        small[2:3, :] = total_rows(grad)
        small[3:4, :] = total_rows(grad_out)
        small[4:8, :] = jnp.zeros((4, D), F32)


def backward_kernel(
    dp_size,
    mid_low,
    weights,
    attended,
    mixed_heads,
    qs,
    keys,
    values,
    lse,
    normed,
    ints,
    up,
    down,
    mixed,
    grads,
    norm_own,
    norm_other,
    small,
    up_sum,
    down_sum,
    mixed_out,
    heads_grad,
    q_low,
    k_low,
    v_low,
    up_stage,
    up_land,
    down_stage,
    down_land,
    send_sem,
    recv_sem,
    spread_send,
    spread_recv,
):
    cube = Cube(dp_size)
    enter(cube.partners() + [cube.diagonal])
    jobs = [
        Scatter(cube.path(first, True), part, stage, land, send_sem.at[k], recv_sem.at[k])
        for k, (first, part, stage, land) in enumerate(
            (
                ("x", lambda dp, t: down.at[dp, t], down_stage, down_land),
                ("core", lambda dp, t: up.at[dp, t], up_stage, up_land),
            )
        )
    ]
    for job in jobs:
        job.start()
    wait_mixed = spread(cube, mixed, mixed_out, spread_send, spread_recv)
    todo = [(job, k) for k in range(len(jobs[0].rest)) for job in jobs]

    def pump(number):
        for job, k in todo[:number]:
            job.step(k)
        del todo[:number]

    half = mid_low.shape[0]
    length = keys.shape[0]
    width = weights.shape[3]
    c = cube.core
    base = pl.multiple_of(c * half, half)
    other = pl.multiple_of((1 - c) * half, half)
    count = ints[0:1, 0:1]
    for t in range(weights.shape[0]):
        cols = slice(t * width, (t + 1) * width)
        heads_grad[:, cols] = nn(mid_low[...], weights[t, 3]).astype(BF16)
        grads[t, 3] = tn(mid_low[...], attended[:, cols]).astype(BF16)
    pump(8)
    product = heads_grad[...].astype(F32) * mixed_heads[...]
    head_of = lax.broadcasted_iota(jnp.int32, (16, D), 0)
    place = lax.broadcasted_iota(jnp.int32, (16, D), 1)
    pick = jnp.where(
        (place >= head_of * HD) & (place < head_of * HD + HD), 1.0, 0.0
    ).astype(BF16)
    hi = product.astype(BF16)
    delta = nt(pick, hi) + nt(pick, (product - hi.astype(F32)).astype(BF16))
    lane, own, mark = lane_sets()
    dead = ((1.0 - row_live(count, 0, length)) * DEAD).astype(BF16)
    block = 512
    for p in range(D // PAIR):
        cols = slice(p * PAIR, (p + 1) * PAIR)
        q_parts = []
        v_parts = [0.0] * (length // block)
        k_parts = [0.0] * (length // block)
        for h in range(2):
            head = 2 * p + h
            qx = qs[:, cols] * own[h] + mark[h]
            gx = heads_grad[:, cols] * own[h]
            q_sum = jnp.zeros((half, PAIR), F32)
            for b in range(length // block):
                span = slice(b * block, (b + 1) * block)
                kx = keys[span, cols] * own[h] + dead[span] * mark[h]
                probs = jnp.exp(nt(kx, qx) - lse[head : head + 1, :])
                prob_grad = nt(values[span, cols], gx)
                score_low = (probs * (prob_grad - delta[head : head + 1, :])).astype(BF16)
                v_parts[b] = v_parts[b] + nn(probs.astype(BF16), gx)
                k_parts[b] = k_parts[b] + nn(score_low, qx) * own[h].astype(F32)
                q_sum = q_sum + tn(score_low, kx)
            q_parts.append(q_sum)
        q_grad = jnp.where(lane < HD, q_parts[0], q_parts[1]) * HD**-0.5
        q_low[:, cols] = q_grad.astype(BF16)
        small[0:1, cols] = total_rows(q_grad)
        v_total = 0.0
        for b in range(length // block):
            span = slice(b * block, (b + 1) * block)
            k_low[span, cols] = k_parts[b].astype(BF16)
            v_low[span, cols] = v_parts[b].astype(BF16)
            v_total = v_total + total_rows(v_parts[b])
        small[1:2, cols] = v_total
        pump((8, 0, 2, 4, 2, 2)[p % 6])
    small[2:8, :] = jnp.zeros((6, D), F32)
    own_part = 0.0
    other_part = 0.0
    for t in range(weights.shape[0]):
        cols = slice(t * width, (t + 1) * width)
        grads[t, 0] = tn(normed[pl.ds(base, half), :], q_low[:, cols]).astype(BF16)
        grads[t, 1] = tn(normed[...], k_low[:, cols]).astype(BF16)
        grads[t, 2] = tn(normed[...], v_low[:, cols]).astype(BF16)
        own_part = (
            own_part
            + nt(q_low[:, cols], weights[t, 0])
            + nt(k_low[pl.ds(base, half), cols], weights[t, 1])
            + nt(v_low[pl.ds(base, half), cols], weights[t, 2])
        )
        other_part = (
            other_part
            + nt(k_low[pl.ds(other, half), cols], weights[t, 1])
            + nt(v_low[pl.ds(other, half), cols], weights[t, 2])
        )
    norm_own[...] = own_part
    norm_other[...] = other_part.astype(BF16)
    pump(len(todo))
    down_sum[...] = jobs[0].last()
    up_sum[...] = jobs[1].last()
    wait_mixed()
    for job in jobs:
        job.finish()


def reduce_kernel(
    dp_size,
    attn,
    norm_own,
    norm_other,
    start_own,
    mid_grad,
    vec,
    small_ff,
    small_attn,
    small_hidden,
    ints,
    attn_sum,
    input_out,
    small_sum,
    attn_stage,
    attn_land,
    norm_land,
    input_half,
    small_send,
    small_land,
    send_sem,
    recv_sem,
    small_sem,
    spread_send,
    spread_recv,
    pair_sem,
):
    cube = Cube(dp_size)
    half = norm_own.shape[0]
    enter(cube.partners() + [cube.diagonal])
    exchange = pltpu.make_async_remote_copy(
        src_ref=norm_other,
        dst_ref=norm_land,
        send_sem=pair_sem.at[0],
        recv_sem=pair_sem.at[1],
        device_id=cube.sibling,
        device_id_type=MESH,
    )
    exchange.start()
    job = Scatter(
        cube.path("x", True),
        lambda dp, t: attn.at[t, :, dp],
        attn_stage,
        attn_land,
        send_sem,
        recv_sem,
    )
    job.start()
    xhat, rstd = centre(start_own[...])
    live = row_live(ints[0:1, 0:1], cube.core * half, half)
    exchange.wait()
    upstream = norm_own[...] + norm_land[...].astype(F32)
    grad = mid_grad[...] + norm_back(xhat, rstd, vec[0:1, :], upstream)
    input_half[...] = (live * grad).astype(BF16)
    wait_input = spread(cube, input_half, input_out, spread_send, spread_recv)
    small_send[0, 0:1, :] = total_rows(upstream * xhat)
    small_send[0, 1:2, :] = total_rows(upstream)
    small_send[0, 2:6, :] = small_ff[0:4, :]
    small_send[0, 6:8, :] = small_attn[0:2, :]
    for k in range(small_hidden.shape[1] // D):
        small_send[0, 8 + k : 9 + k, :] = small_hidden[0:1, k * D : (k + 1) * D]
    small_send[0, 8 + small_hidden.shape[1] // D :, :] = jnp.zeros(
        (small_send.shape[1] - 8 - small_hidden.shape[1] // D, D), F32
    )
    path = job.path
    smalls = []

    def small_step(p):
        copy = pltpu.make_async_remote_copy(
            src_ref=small_send.at[p],
            dst_ref=small_land.at[p],
            send_sem=small_sem.at[0, p],
            recv_sem=small_sem.at[1, p],
            device_id=path.partner(p),
            device_id_type=MESH,
        )
        copy.start()
        smalls.append(copy)

    def small_close(p):
        smalls[p].wait_recv()
        value = small_send[p] + small_land[p]
        if p + 1 < path.count:
            small_send[p + 1] = value
            small_step(p + 1)
        else:
            small_sum[...] = value

    small_step(0)
    for k in range(len(job.rest)):
        job.step(k)
        if k % 3 == 2 and k // 3 < path.count:
            small_close(k // 3)
    for p in range(len(job.rest) // 3, path.count):
        small_close(p)
    attn_sum[...] = job.last()
    wait_input()
    exchange_sent = smalls
    for copy in exchange_sent:
        copy.wait_send()
    job.finish()


def finish_kernel(
    dp_size,
    heads,
    attn_sum,
    up_sum,
    down_sum,
    small,
    mixed_half,
    input_half,
    mixed,
    inputs,
    attn_out,
    bias_out,
    out_out,
    vec_out,
    up_out,
    hidden_out,
    down_out,
    local_sem,
):
    copies = [
        pltpu.make_async_copy(mixed_half, mixed, local_sem.at[0]),
        pltpu.make_async_copy(input_half, inputs, local_sem.at[1]),
    ]
    for copy in copies:
        copy.start()
    dp, t = lax.axis_index("dp"), lax.axis_index("tensor")
    attn_out[...] = attn_sum[0:3]
    out_out[...] = attn_sum[3].T
    up_out[...] = up_sum[...].T
    down_out[...] = down_sum[...]
    per = vec_out.shape[1]
    vec_out[...] = pltpu.roll(small[0:8, :], lax.rem(D - dp * per, D), 1)[0:6, 0:per]
    each = bias_out.shape[2]
    turned = pltpu.roll(small[0:8, :], lax.rem(2 * D - t * (D // 2) - dp * each, D), 1)
    for k in range(2):
        for h in range(heads):
            bias_out[k, h : h + 1, :] = turned[6 + k : 7 + k, h * HD : h * HD + each]
    rows = hidden_out.shape[1]
    fit = D // rows
    place = dp * 2 + t
    line = small[8:16, :]
    row = lax.broadcasted_iota(jnp.int32, (8, D), 0)
    picked = jnp.sum(jnp.where(row == lax.div(place, fit), line, 0.0), axis=0, keepdims=True)
    picked = jnp.broadcast_to(picked, (8, D))
    hidden_out[...] = pltpu.roll(picked, lax.rem(D - lax.rem(place, fit) * rows, D), 1)[0:1, 0:rows]
    for copy in copies:
        copy.wait()


ANY = pl.BlockSpec(memory_space=pl.ANY)
VMEM = pl.BlockSpec(memory_space=pltpu.VMEM)


def shape(dims, kind):
    return jax.ShapeDtypeStruct(dims, kind)


def local(
    dp_size,
    tokens,
    counts,
    indices,
    ground_dist,
    cotangent,
    attn_weight,
    attn_bias,
    out_weight,
    vectors,
    up_weight,
    up_bias,
    down_weight,
):
    tensor = 2
    chips, length, width = tokens.shape
    half = length // 2
    attn_rows, attn_cols = attn_weight.shape[1:]
    ff_rows = down_weight.shape[0]
    ff = ff_rows * dp_size * tensor
    heads = attn_bias.shape[1]
    count = phases_of(dp_size)
    devices = 1 << count
    dma = pltpu.SemaphoreType.DMA

    ints = jnp.concatenate([counts, ground_dist, indices[0]]).astype(jnp.int32)
    ints = jnp.broadcast_to(ints[None, :], (8, length))

    tok2, cot2, ints2, packs_all, attn_all, up, down = pl.pallas_call(
        functools.partial(gather_kernel, dp_size),
        name="gather",
        out_shape=[
            shape((2, length, width), BF16),
            shape((2, half, width), BF16),
            shape((2, 8, length), jnp.int32),
            shape((dp_size, tensor, PACK, 128), BF16),
            shape((tensor, 4, dp_size, attn_rows, attn_cols), BF16),
            shape((ff_rows, width), BF16),
            shape((ff_rows, width), BF16),
        ],
        in_specs=[ANY] * 10,
        out_specs=[ANY] * 3 + [VMEM] + [ANY] * 3,
        scratch_shapes=[
            pltpu.VMEM(attn_weight.shape, F32),
            pltpu.VMEM(out_weight.shape, F32),
            pltpu.VMEM(up_weight.shape, F32),
            pltpu.VMEM(down_weight.shape, F32),
            pltpu.VMEM(vectors.shape, F32),
            pltpu.VMEM(attn_bias.shape, F32),
            pltpu.VMEM((1,) + up_bias.shape, F32),
            pltpu.VMEM((4, attn_rows, attn_cols), BF16),
            pltpu.VMEM((PACK, 128), F32),
            pltpu.VMEM((ff_rows, width), BF16),
            pltpu.VMEM((ff_rows, width), BF16),
            dma((3, devices)),
            dma((3, devices)),
            dma((2, 3)),
            dma((13,)),
        ],
        compiler_params=pltpu.CompilerParams(
            collective_id=0, has_side_effects=True, vmem_limit_bytes=32 * MIB
        ),
    )(
        tokens[0],
        cotangent[0],
        ints,
        attn_weight,
        out_weight,
        up_weight,
        down_weight,
        vectors,
        attn_bias,
        up_bias[None],
    )

    quarter = width // 4
    omega = 1.0 / 10000.0 ** (jnp.arange(quarter, dtype=F32) / quarter)
    omega = jnp.broadcast_to(jnp.concatenate([omega, omega])[None], (8, 2 * quarter))

    (
        normed,
        start_own,
        qs,
        keys,
        values,
        mixed_heads,
        attended,
        lse,
        mid,
        vec,
        hidden_bias,
        image,
        weights,
        up_all,
        down_all,
    ) = pl.pallas_call(
        functools.partial(forward_kernel, dp_size, heads),
        name="attend",
        out_shape=[
            shape((length, width), BF16),
            shape((half, width), F32),
            shape((half, width), BF16),
            shape((length, width), BF16),
            shape((length, width), BF16),
            shape((half, width), F32),
            shape((half, width), BF16),
            shape((PAIR, half), F32),
            shape((half, width), F32),
            shape((8, width), F32),
            shape((1, ff), F32),
            shape((8, length), jnp.int32),
            shape((tensor, 4, width, attn_cols), BF16),
            shape((dp_size, tensor, ff_rows, width), BF16),
            shape((dp_size, tensor, ff_rows, width), BF16),
        ],
        in_specs=[ANY] * 2 + [VMEM] * 2 + [ANY] * 3,
        out_specs=[VMEM] * 13 + [ANY] * 2,
        scratch_shapes=[
            pltpu.VMEM((length, width), F32),
            pltpu.VMEM((length, width), BF16),
            pltpu.VMEM((8, width), F32),
            dma((2, devices)),
            dma((2, devices)),
            dma((6,)),
        ],
        compiler_params=pltpu.CompilerParams(
            collective_id=1, has_side_effects=True, vmem_limit_bytes=60 * MIB
        ),
    )(
        tok2,
        ints2,
        omega,
        packs_all,
        attn_all.reshape(tensor, 4, width, attn_cols),
        up,
        down,
    )

    tile = 512
    whole = lambda dims: pl.BlockSpec(dims, lambda j: (0,) * len(dims))
    mixed, mid_grad, mid_low, small_ff, up_bias_grad, up_grad, down_grad = pl.pallas_call(
        feed_kernel,
        name="feed",
        grid=(ff // tile,),
        out_shape=[
            shape((half, width), BF16),
            shape((half, width), F32),
            shape((half, width), BF16),
            shape((8, width), F32),
            shape((1, ff), F32),
            shape((ff, width), BF16),
            shape((ff, width), BF16),
        ],
        in_specs=[
            whole((half, width)),
            ANY,
            whole((8, length)),
            whole((8, width)),
            pl.BlockSpec((tile, width), lambda j: (j, 0)),
            pl.BlockSpec((1, tile), lambda j: (0, j)),
            pl.BlockSpec((tile, width), lambda j: (j, 0)),
        ],
        out_specs=[
            whole((half, width)),
            whole((half, width)),
            whole((half, width)),
            whole((8, width)),
            pl.BlockSpec((1, tile), lambda j: (0, j)),
            pl.BlockSpec((tile, width), lambda j: (j, 0)),
            pl.BlockSpec((tile, width), lambda j: (j, 0)),
        ],
        scratch_shapes=[
            pltpu.VMEM((half, width), BF16),
            pltpu.VMEM((half, width), BF16),
            pltpu.VMEM((half, width), F32),
            pltpu.VMEM((half, width), F32),
            pltpu.VMEM((half, width), BF16),
            dma,
        ],
        compiler_params=pltpu.CompilerParams(vmem_limit_bytes=60 * MIB),
    )(mid, cot2, image, vec, up_all.reshape(ff, width), hidden_bias, down_all.reshape(ff, width))

    ff_dims = (ff_rows, width)
    staged = devices // 2
    grads, norm_own, norm_other, small_attn, up_sum, down_sum, mixed_out = pl.pallas_call(
        functools.partial(backward_kernel, dp_size),
        name="attend_back",
        out_shape=[
            shape((tensor, 4, width, attn_cols), BF16),
            shape((half, width), F32),
            shape((half, width), BF16),
            shape((8, width), F32),
            shape(ff_dims, F32),
            shape(ff_dims, F32),
            shape((2, half, width), BF16),
        ],
        in_specs=[VMEM] * 12 + [ANY],
        out_specs=[VMEM] * 6 + [ANY],
        scratch_shapes=[
            pltpu.VMEM((half, width), BF16),
            pltpu.VMEM((half, width), BF16),
            pltpu.VMEM((length, width), BF16),
            pltpu.VMEM((length, width), BF16),
            pltpu.VMEM((staged,) + ff_dims, BF16),
            pltpu.VMEM((devices,) + ff_dims, BF16),
            pltpu.VMEM((staged,) + ff_dims, BF16),
            pltpu.VMEM((devices,) + ff_dims, BF16),
            dma((2, devices)),
            dma((2, devices)),
            dma((2,)),
            dma((2,)),
        ],
        compiler_params=pltpu.CompilerParams(
            collective_id=2, has_side_effects=True, vmem_limit_bytes=63 * MIB
        ),
    )(
        mid_low,
        weights,
        attended,
        mixed_heads,
        qs,
        keys,
        values,
        lse,
        normed,
        image,
        up_grad.reshape(dp_size, tensor, ff_rows, width),
        down_grad.reshape(dp_size, tensor, ff_rows, width),
        mixed,
    )

    attn_dims = (4, attn_rows, attn_cols)
    small_rows = -(-(8 + ff // width) // 8) * 8
    attn_sum, input_out, small_sum = pl.pallas_call(
        functools.partial(reduce_kernel, dp_size),
        name="reduce",
        out_shape=[
            shape(attn_dims, F32),
            shape((2, half, width), BF16),
            shape((small_rows, width), F32),
        ],
        in_specs=[VMEM] * 10,
        out_specs=[VMEM, ANY, VMEM],
        scratch_shapes=[
            pltpu.VMEM((staged,) + attn_dims, BF16),
            pltpu.VMEM((devices,) + attn_dims, BF16),
            pltpu.VMEM((half, width), BF16),
            pltpu.VMEM((half, width), BF16),
            pltpu.VMEM((count, small_rows, width), F32),
            pltpu.VMEM((count, small_rows, width), F32),
            dma((devices,)),
            dma((devices,)),
            dma((2, count)),
            dma((2,)),
            dma((2,)),
            dma((2,)),
        ],
        compiler_params=pltpu.CompilerParams(
            collective_id=3, has_side_effects=True, vmem_limit_bytes=60 * MIB
        ),
    )(
        grads.reshape(tensor, 4, dp_size, attn_rows, attn_cols),
        norm_own,
        norm_other,
        start_own,
        mid_grad,
        vec,
        small_ff,
        small_attn,
        up_bias_grad,
        image,
    )

    results = pl.pallas_call(
        functools.partial(finish_kernel, dp_size, heads),
        name="finish",
        out_shape=[
            shape((2, half, width), BF16),
            shape((2, half, width), BF16),
            shape(attn_weight.shape, F32),
            shape(attn_bias.shape, F32),
            shape(out_weight.shape, F32),
            shape(vectors.shape, F32),
            shape(up_weight.shape, F32),
            shape((1, ff_rows), F32),
            shape(down_weight.shape, F32),
        ],
        in_specs=[VMEM] * 4 + [ANY] * 2,
        out_specs=[ANY] * 2 + [VMEM] * 7,
        scratch_shapes=[dma((2,))],
        compiler_params=pltpu.CompilerParams(vmem_limit_bytes=32 * MIB),
    )(attn_sum, up_sum, down_sum, small_sum, mixed_out, input_out)
    return (
        results[0].reshape(1, length, width),
        results[1].reshape(1, length, width),
        *results[2:7],
        results[7].reshape(ff_rows),
        results[8],
    )


def solution(mesh):
    placed = (
        P("dp", None, None),
        P("dp"),
        P("dp", None),
        P("dp"),
        P("dp", None, None),
        P(None, "dp", "tensor"),
        P(None, "tensor", "dp"),
        P("tensor", "dp"),
        P(None, "dp"),
        P(None, ("dp", "tensor")),
        P(("dp", "tensor")),
        P(("dp", "tensor"), None),
    )
    return jax.shard_map(
        functools.partial(local, mesh.shape["dp"]),
        mesh=mesh,
        in_specs=placed,
        out_specs=(
            P("dp", None, None),
            P("dp", None, None),
            P(None, "dp", "tensor"),
            P(None, "tensor", "dp"),
            P("tensor", "dp"),
            P(None, "dp"),
            P(None, ("dp", "tensor")),
            P(("dp", "tensor")),
            P(("dp", "tensor"), None),
        ),
        check_vma=False,
    )
```

```python
import functools

import jax
import jax.numpy as jnp
from jax import lax
from jax.experimental import pallas as pl
from jax.experimental.pallas import tpu as pltpu
from jax.sharding import PartitionSpec as P

D = 768
HD = 64
GRID = 32
EPS = 1e-06
DEAD = -1e30
PAIR = 2 * HD
ROOT_HALF = 0.7071067811865476
ROOT_TWO_PI_INV = 0.3989422804014327

F32 = jnp.float32
BF16 = jnp.bfloat16
MESH = pl.DeviceIdType.MESH
MIB = 1 << 20
BACK = "xYZ"


def nn(a, b):
    return lax.dot_general(a, b, (((1,), (0,)), ((), ())), preferred_element_type=F32)


def nt(a, b):
    return lax.dot_general(a, b, (((1,), (1,)), ((), ())), preferred_element_type=F32)


def tn(a, b):
    return lax.dot_general(a, b, (((0,), (0,)), ((), ())), preferred_element_type=F32)


class Path:
    def __init__(self, cube, steps, mirror):
        self.cube, self.steps, self.mirror = cube, steps, mirror
        self.count = len(steps)

    def partner(self, p):
        return (self.cube.dp + self.steps[p][0], self.cube.t + self.steps[p][1])

    def entry(self, mask):
        dp, t = self.cube.dp, self.cube.t
        for p, (ddp, dt) in enumerate(self.steps):
            if mask >> p & 1:
                dp, t = dp + ddp, t + dt
        return dp, t

    def mirrored(self, mask):
        if self.mirror is None:
            return mask
        i, j = self.mirror
        return mask & ~(1 << i | 1 << j) | (mask >> i & 1) << j | (mask >> j & 1) << i


class Cube:
    def __init__(self, dp_size):
        self.dp = lax.axis_index("dp")
        self.t = lax.axis_index("tensor")
        self.core = lax.rem(self.dp, 2)

        def flip(b):
            return b * (1 - 2 * lax.rem(lax.div(self.dp, b), 2))

        self.dt, self.dy, self.dc = 1 - 2 * self.t, flip(2), flip(1)
        self.far = []
        b = dp_size // 2
        while b >= 4:
            self.far.append((flip(b), 0))
            b //= 2
        self.sibling = (self.dp + self.dc, self.t)
        self.across = (self.dp, self.t + self.dt)
        self.diagonal = (self.dp + self.dc, self.t + self.dt)

    def path(self, kind):
        c = self.core
        x, y, far, last = (0, self.dt), (self.dy, 0), self.far[:-1], self.far[-1]
        n = len(self.far)

        def pick(first, second):
            return tuple((1 - c) * f + c * s for f, s in zip(first, second))

        if kind == "zXY":
            steps, mirror = [*far, last, pick(x, y), pick(y, x)], (n, n + 1)
        elif kind == "XzY":
            steps, mirror = [*far, pick(x, y), last, pick(y, x)], (n - 1, n + 1)
        elif kind == "xYZ":
            steps, mirror = [*far, x, pick(y, last), pick(last, y)], (n, n + 1)
        else:
            steps, mirror = [*far, x, last, y], None
        return Path(self, steps + [(self.dc, 0)], mirror)

    def partners(self):
        return [(self.dp + ddp, self.t + dt) for ddp, dt in self.far] + [
            (self.dp + self.dy, self.t),
            self.across,
            self.sibling,
        ]


def phases_of(dp_size):
    return (2 * dp_size).bit_length() - 1


def enter(devices):
    barrier = pltpu.get_barrier_semaphore()
    for device in devices:
        pl.semaphore_signal(barrier, inc=1, device_id=device, device_id_type=MESH)
    pl.semaphore_wait(barrier, len(devices))


class Gather:
    def __init__(self, path, own, slot, send_sem, recv_sem):
        self.path, self.own, self.slot = path, own, slot
        self.send_sem, self.recv_sem = send_sem, recv_sem
        self.count = path.count
        self.sent = []
        self.order = sorted(
            ((p, m) for p in range(self.count) for m in range(1 << p)),
            key=lambda item: (item[1].bit_count(), item[0], item[1]),
        )

    def copy(self, p, mask, place, source):
        k = (1 << p) - 1 + mask
        there = (1 << p) - 1 + (self.path.mirrored(mask) if p == self.count - 1 else mask)
        return pltpu.make_async_remote_copy(
            src_ref=source,
            dst_ref=place,
            send_sem=self.send_sem.at[k],
            recv_sem=self.recv_sem.at[there],
            device_id=self.path.partner(p),
            device_id_type=MESH,
        )

    def send(self, p, mask):
        place = self.slot(*self.path.entry(mask))
        copy = self.copy(p, mask, place, self.own if mask == 0 else place)
        copy.start()
        self.sent.append(copy)

    def start(self):
        for p in range(self.count):
            self.send(p, 0)

    def step(self, k):
        p, mask = self.order[k]
        place = self.slot(*self.path.entry(mask | 1 << p))
        there = self.path.mirrored(mask) if p == self.count - 1 else mask
        self.copy(p, there, place, place).wait_recv()
        for later in range(p + 1, self.count):
            self.send(later, mask | 1 << p)

    def finish(self):
        for copy in self.sent:
            copy.wait_send()


def low_bit(m):
    return (m & -m).bit_length() - 1 if m else 99


class Scatter:
    def __init__(self, path, part, landed, send_sem, recv_sem):
        self.path, self.count = path, path.count
        self.part, self.landed = part, landed
        self.send_sem, self.recv_sem = send_sem, recv_sem
        self.sent = []
        self.order = send_order(path)

    def index(self, q, m):
        return (1 << (self.count - 1 - q)) - 1 + (m >> (q + 1))

    def describe(self, q, m, source):
        k = self.index(q, other_name(self.path, m) if q == 0 else m)
        return pltpu.make_async_remote_copy(
            src_ref=source,
            dst_ref=self.landed.at[k],
            send_sem=self.send_sem.at[k],
            recv_sem=self.recv_sem.at[k],
            device_id=self.path.partner(self.count - 1 - q),
            device_id_type=MESH,
        )

    def send(self, q, m):
        copy = self.describe(q, m, self.part(m))
        copy.start()
        self.sent.append(copy)

    def total(self, m):
        total = self.part(m)[...].astype(F32)
        for q in range(min(low_bit(m), self.count)):
            k = self.index(q, m)
            name = other_name(self.path, m) if q == 0 else m
            self.describe(q, name, self.landed.at[k]).wait_recv()
            total = total + self.landed[k].astype(F32)
        return total

    def step(self, m):
        self.part(m)[...] = self.total(m).astype(BF16)
        self.send(low_bit(m), m)

    def finish(self):
        for copy in self.sent:
            copy.wait_send()


def reverse(count, m):
    return sum((m >> q & 1) << (count - 1 - q) for q in range(count))


def other_name(path, m):
    return reverse(path.count, path.mirrored(reverse(path.count, m)))


def send_order(path):
    def rank(name):
        rest = name & ~3
        return (low_bit(rest), low_bit(rest & (rest - 1)), name)

    masks = range(1 << path.count)
    given = sorted((m for m in masks if m & 1), key=lambda m: rank(other_name(path, m)))
    kept = sorted((m for m in masks if not m & 1), key=rank)
    return [
        [m for m in given if other_name(path, m) & 2],
        [m for m in kept if m & 2],
        [m for m in given if not other_name(path, m) & 2],
        [m for m in kept if not m & 2],
    ]


def scatter_entry(path, m):
    return path.entry(reverse(path.count, m))


def spread(cube, half, out, send_sem, recv_sem):
    c, t = cube.core, cube.t
    mine = out.at[c]

    def push(device, k):
        return pltpu.make_async_remote_copy(
            src_ref=half,
            dst_ref=mine,
            send_sem=send_sem.at[k],
            recv_sem=recv_sem.at[c],
            device_id=device,
            device_id_type=MESH,
        )

    def arrival(h):
        return pltpu.make_async_remote_copy(
            src_ref=half,
            dst_ref=out.at[h],
            send_sem=send_sem.at[0],
            recv_sem=recv_sem.at[h],
            device_id=cube.sibling,
            device_id_type=MESH,
        )

    keep = pltpu.make_async_copy(half, mine, send_sem.at[0])

    @pl.when(c == t)
    def _():
        push(cube.across, 1).start()
        keep.start()

    @pl.when(c != t)
    def _():
        push(cube.diagonal, 1).start()
        push(cube.sibling, 0).start()

    def wait():
        @pl.when(c == t)
        def _():
            keep.wait()
            push(cube.across, 1).wait_send()
            arrival(1 - c).wait_recv()

        @pl.when(c != t)
        def _():
            push(cube.sibling, 0).wait_send()
            push(cube.diagonal, 1).wait_send()
            arrival(c).wait_recv()
            arrival(1 - c).wait_recv()

    return wait


PACK = 32


def gather_kernel(
    dp_size,
    tok,
    cot,
    ints,
    attn_f,
    out_f,
    up_f,
    down_f,
    vec_f,
    bias_f,
    hidden_f,
    tok2,
    cot2,
    ints2,
    packs_all,
    attn_all,
    up,
    down,
    attn_in,
    out_in,
    up_in,
    down_in,
    vec_in,
    bias_in,
    hidden_in,
    attn,
    pack,
    cot_in,
    send_sem,
    recv_sem,
    pair_sem,
    local_sem,
):
    cube = Cube(dp_size)
    rows = cot2.shape[1]
    c = cube.core
    other = pl.ds(pl.multiple_of((1 - c) * rows, rows), rows)
    own = pl.ds(pl.multiple_of(c * rows, rows), rows)
    loads = [
        pltpu.make_async_copy(source, target, local_sem.at[k])
        for k, (source, target) in enumerate(
            (
                (attn_f, attn_in),
                (out_f, out_in),
                (vec_f, vec_in),
                (bias_f, bias_in),
                (hidden_f, hidden_in),
                (up_f, up_in),
                (down_f, down_in),
                (cot, cot_in),
            )
        )
    ]
    for copy in loads:
        copy.start()
    keeps = [
        pltpu.make_async_copy(tok, tok2.at[c], local_sem.at[8]),
    ]
    for copy in keeps:
        copy.start()
    ints2[c] = ints[...]
    for copy in loads[:5]:
        copy.wait()
    attn[0:3] = attn_in[...].astype(BF16)
    attn[3] = out_in[...].astype(BF16)
    pack[...] = jnp.zeros_like(pack)
    pack[0:6, 0 : vec_in.shape[1]] = vec_in[...]
    pack[6:7, 0 : hidden_in.shape[1]] = hidden_in[...]
    for k in range(2):
        pack[8 + 8 * k : 8 + 8 * k + bias_in.shape[1], 0 : bias_in.shape[2]] = bias_in[k]
    pack_low = pack[...].astype(BF16)
    packs_all[cube.dp, cube.t] = pack_low
    enter(cube.partners())
    keep = pltpu.make_async_copy(attn, attn_all.at[cube.t, :, cube.dp], local_sem.at[10])
    keep.start()
    jobs = [
        Gather(
            cube.path("XzY"),
            packs_all.at[cube.dp, cube.t],
            lambda dp, t: packs_all.at[dp, t],
            send_sem.at[0],
            recv_sem.at[0],
        )
    ]
    for k in range(2):
        span = slice(2 * k, 2 * k + 2)
        jobs.append(
            Gather(
                cube.path("XzY"),
                attn.at[span],
                lambda dp, t, span=span: attn_all.at[t, span, dp],
                send_sem.at[k + 1],
                recv_sem.at[k + 1],
            )
        )
    for job in jobs:
        job.start()
    pairs = [
        pltpu.make_async_remote_copy(
            src_ref=source,
            dst_ref=target.at[c],
            send_sem=pair_sem.at[0, k],
            recv_sem=pair_sem.at[1, k],
            device_id=cube.sibling,
            device_id_type=MESH,
        )
        for k, (source, target) in enumerate(
            ((ints, ints2), (tok, tok2), (cot_in.at[other], cot2))
        )
    ]
    for copy in loads[5:]:
        copy.wait()
    for copy in pairs:
        copy.start()
    up[...] = up_in[...].astype(BF16)
    down[...] = down_in[...].astype(BF16)
    stores = [pltpu.make_async_copy(cot_in.at[own], cot2.at[c], local_sem.at[9])]
    for copy in stores:
        copy.start()
    for k in range(len(jobs[0].order)):
        for job in jobs:
            job.step(k)
    for job in jobs:
        job.finish()
    for copy in pairs:
        copy.wait()
    for copy in keeps + [keep] + stores:
        copy.wait()


def centre(values):
    mean = jnp.mean(values, axis=-1, keepdims=True)
    centred = values - mean
    rstd = lax.rsqrt(jnp.mean(centred * centred, axis=-1, keepdims=True) + EPS)
    return centred * rstd, rstd


def row_live(count, offset, rows):
    places = lax.broadcasted_iota(jnp.int32, (rows, 1), 0) + offset
    return (places < count + 2).astype(F32)


def lane_sets():
    lane = lax.broadcasted_iota(jnp.int32, (1, PAIR), 1)
    own = [(lane < HD).astype(F32).astype(BF16), (lane >= HD).astype(F32).astype(BF16)]
    mark = [(lane == HD).astype(F32).astype(BF16), (lane == 0).astype(F32).astype(BF16)]
    return lane, own, mark


def place_rows(rows, offset, columns):
    a, r = divmod(offset, 128)
    lane = lax.broadcasted_iota(jnp.int32, rows.shape, 1)
    turned = pltpu.roll(rows, r, 1) if r else rows
    columns[a] = columns[a] + jnp.where(lane >= r, turned, 0.0)
    if r and a + 1 < len(columns):
        columns[a + 1] = columns[a + 1] + jnp.where(lane < r, turned, 0.0)


def read_packs(dp_size, heads, slots, packs, vec, bias, hidden):
    per = vec.shape[1] // dp_size
    tensor = packs.shape[1]
    each = hidden.shape[1] // (dp_size * tensor)
    row = lax.broadcasted_iota(jnp.int32, (8, 128), 0)
    vec_columns = [jnp.zeros((8, 128), F32) for k in range(vec.shape[1] // 128)]
    hidden_columns = [jnp.zeros((1, 128), F32) for k in range(hidden.shape[1] // 128)]
    spans = [[jnp.zeros((8, 128), F32) for k in range(2)] for t in range(tensor)]
    for dp in range(dp_size):
        for t in range(tensor):
            data = packs[dp, t].astype(F32)
            if t == 0:
                place_rows(jnp.where(row < 6, data[0:8], 0.0), dp * per, vec_columns)
            for k in range(2):
                turn = dp * (HD // dp_size)
                part = data[8 + 8 * k : 16 + 8 * k]
                spans[t][k] = spans[t][k] + (pltpu.roll(part, turn, 1) if turn else part)
    for k, (dp, t) in enumerate(slots):
        place_rows(packs[dp, t].astype(F32)[6:7], k * each, hidden_columns)
    for k, column in enumerate(vec_columns):
        vec[:, k * 128 : (k + 1) * 128] = column
    for k, column in enumerate(hidden_columns):
        hidden[:, k * 128 : (k + 1) * 128] = column
    for k in range(2):
        columns = [jnp.zeros((1, 128), F32) for j in range(bias.shape[1] // 128)]
        for t in range(tensor):
            for h in range(heads):
                place_rows(spans[t][k][h : h + 1], (t * heads + h) * HD, columns)
        for j, column in enumerate(columns):
            bias[k : k + 1, j * 128 : (j + 1) * 128] = column


def forward_kernel(
    dp_size,
    heads,
    tok2,
    ints2,
    omega,
    packs,
    weights_all,
    up,
    down,
    normed,
    start_own,
    qs,
    keys,
    values,
    mixed_heads,
    attended,
    lse,
    mid,
    vec,
    hidden_bias,
    ints,
    weights,
    feed_all,
    start,
    bias,
    send_sem,
    recv_sem,
    local_sem,
):
    cube = Cube(dp_size)
    c, own_image = cube.core, cube.t
    loads = [
        pltpu.make_async_copy(weights_all, weights, local_sem.at[3]),
    ]
    for copy in loads:
        copy.start()
    keeps = [
        pltpu.make_async_copy(source, feed_all.at[cube.dp, cube.t, k], local_sem.at[4 + k])
        for k, source in enumerate((up, down))
    ]
    for copy in keeps:
        copy.start()
    enter(cube.partners())
    jobs = [
        Gather(
            cube.path("XzY"),
            source,
            lambda dp, t, k=k: feed_all.at[dp, t, k],
            send_sem.at[k],
            recv_sem.at[k],
        )
        for k, source in enumerate((up, down))
    ]
    for job in jobs:
        job.start()
    todo = [(job, k) for k in range(len(jobs[0].order)) for job in jobs]

    def pump(number):
        for job, k in todo[:number]:
            job.step(k)
        del todo[:number]

    length = start.shape[0]
    half = start_own.shape[0]
    base = pl.multiple_of(c * half, half)
    ints[...] = ints2[own_image]
    path = cube.path(BACK)
    slots = [scatter_entry(path, m) for group in send_order(path) for m in group]
    read_packs(dp_size, heads, slots, packs, vec, bias, hidden_bias)
    count = ints[0:1, 0:1]
    quarter = D // 4
    scale = ints[0:1, 1:2].astype(F32) / 10.0
    angle = lax.broadcasted_iota(jnp.int32, (GRID, 2 * quarter), 0).astype(F32) * scale * omega[0:1, :]
    wave = lax.broadcasted_iota(jnp.int32, (GRID, 2 * quarter), 1)
    full = jnp.where(wave < quarter, jnp.sin(angle), jnp.cos(angle))
    hi = full.astype(BF16)
    rest = full - hi.astype(F32)
    middle = rest.astype(BF16)
    little = (rest - middle.astype(F32)).astype(BF16)
    stack = jnp.concatenate([hi, middle, little], axis=0)
    tile = 256
    for r in range(length // tile):
        span = slice(r * tile, (r + 1) * tile)
        index = ints[0:1, span]
        slots = lax.broadcasted_iota(jnp.int32, (1, tile), 1) + r * tile
        places = lax.broadcasted_iota(jnp.int32, (GRID, tile), 0)
        parts = []
        for part in (lax.shift_right_logical(index, 5), lax.bitwise_and(index, GRID - 1)):
            part = jnp.where(slots < 2, -1, part)
            hot = (places == part).astype(F32).astype(BF16)
            parts.append(tn(jnp.concatenate([hot, hot, hot], axis=0), stack))
        code = jnp.concatenate(parts, axis=1)
        live = row_live(count, r * tile, tile)
        rows = (tok2[own_image, span, :].astype(F32) + code) * live
        start[span, :] = rows
        xhat, rstd = centre(rows)
        normed[span, :] = (xhat * vec[0:1, :] + vec[1:2, :]).astype(BF16)
    keep = pltpu.make_async_copy(start.at[pl.ds(base, half)], start_own, local_sem.at[2])
    keep.start()
    keeps.append(keep)
    loads[0].wait()
    pump(4)
    width = weights.shape[3]
    for t in range(weights.shape[0]):
        cols = slice(t * width, (t + 1) * width)
        query = nn(normed[pl.ds(base, half), :], weights[t, 0]) + bias[0:1, cols]
        qs[:, cols] = query.astype(BF16) * jnp.asarray(HD**-0.5, BF16)
        for r in range(length // half):
            span = slice(r * half, (r + 1) * half)
            keys[span, cols] = nn(normed[span, :], weights[t, 1]).astype(BF16)
            values[span, cols] = (nn(normed[span, :], weights[t, 2]) + bias[1:2, cols]).astype(BF16)
    pump(4)
    lane, own, mark = lane_sets()
    dead = ((1.0 - row_live(count, 0, length)) * DEAD).astype(BF16)
    wide = lax.broadcasted_iota(jnp.int32, (1, PAIR), 1)
    block = 256
    for r in range(half // block):
        span = slice(r * block, (r + 1) * block)
        sums = jnp.zeros((block, PAIR), F32)
        for p in range(D // PAIR):
            cols = slice(p * PAIR, (p + 1) * PAIR)
            outs = []
            for h in range(2):
                kx = keys[:, cols] * own[h] + dead * mark[h]
                qx = qs[span, cols] * own[h] + mark[h]
                scores = nt(qx, kx)
                top = jnp.max(scores, axis=1, keepdims=True)
                grown = jnp.exp(scores - top)
                total = jnp.sum(grown, axis=1, keepdims=True)
                outs.append(nn(grown.astype(BF16), values[:, cols]) / total)
                sums = jnp.where(wide == 2 * p + h, top + jnp.log(total), sums)
            both = jnp.where(lane < HD, outs[0], outs[1])
            mixed_heads[span, cols] = both
            attended[span, cols] = both.astype(BF16)
            pump(2)
        lse[:, span] = sums.T
    out = nt(attended[:, :width], weights[0, 3])
    for t in range(1, weights.shape[0]):
        out = out + nt(attended[:, t * width : (t + 1) * width], weights[t, 3])
    mid[...] = start[pl.ds(base, half), :] + (out + vec[4:5, :])
    pump(len(todo))
    for job in jobs:
        job.finish()
    for copy in keeps:
        copy.wait()


def norm_back(xhat, rstd, gain, upstream):
    scaled = upstream * gain
    return rstd * (
        scaled
        - jnp.mean(scaled, axis=-1, keepdims=True)
        - xhat * jnp.mean(scaled * xhat, axis=-1, keepdims=True)
    )


def total_rows(values):
    return jnp.sum(values, axis=0, keepdims=True)


def rows_of(ref, start, number, k, loose):
    rows = ref.shape[2]
    if rows % 16 == 0:
        return ref[start : start + number, k].reshape(number * rows, ref.shape[3])
    for e in range(number):
        loose[e * rows : (e + 1) * rows, :] = ref[start + e, k].astype(F32)
    return loose[0 : number * rows, :].astype(BF16)


def put_rows(ref, start, number, k, value, loose):
    rows = ref.shape[2]
    if rows % 16 == 0:
        ref[start : start + number, k] = value.astype(BF16).reshape(number, rows, ref.shape[3])
        return
    loose[0 : number * rows, :] = value
    for e in range(number):
        ref[start + e, k] = loose[e * rows : (e + 1) * rows, :].astype(BF16)


def put_attn(ref, t, k, value, loose):
    number, rows, cols = ref.shape[2:]
    if rows % 16 == 0:
        ref[t, k] = value.astype(BF16).reshape(number, rows, cols)
        return
    loose[0 : number * rows, 0:cols] = value
    for e in range(number):
        ref[t, k, e] = loose[e * rows : (e + 1) * rows, 0:cols].astype(BF16)


def back_kernel(
    dp_size,
    mid,
    cot2,
    feed_all,
    vec,
    hidden_bias,
    weights,
    attended,
    mixed_heads,
    qs,
    keys,
    values,
    lse,
    normed,
    ints,
    start_own,
    attn_sum,
    feed_sum,
    small_sum,
    mixed_out,
    input_out,
    feed,
    feed_land,
    attn,
    attn_land,
    normed2,
    act,
    hidden_low,
    grad_low,
    down_sum,
    norm_sum,
    mid_low,
    k_low,
    v_low,
    norm_land,
    delta,
    small_send,
    small_land,
    loose,
    load_sem,
    local_sem,
    feed_send,
    feed_recv,
    attn_send,
    attn_recv,
    small_sem,
    spread_send,
    spread_recv,
    pair_sem,
):
    cube = Cube(dp_size)
    c = cube.core
    mixed, heads_grad, q_low, start, mid_grad = normed2, act, hidden_low, down_sum, norm_sum
    input_half, norm_other = grad_low, mid_low
    path = cube.path(BACK)
    groups = send_order(path)
    slots = [m for group in groups for m in group]
    place = {m: k for k, m in enumerate(slots)}
    cot_load = pltpu.make_async_copy(cot2.at[cube.t], grad_low, local_sem.at[0])
    cot_load.start()
    loads = []
    for k, m in enumerate(slots):
        dp, t = scatter_entry(path, m)
        loads.append(pltpu.make_async_copy(feed_all.at[dp, t], feed.at[k], load_sem.at[k]))
        loads[k].start()
    enter(cube.partners() + [cube.diagonal])
    feed_job = Scatter(path, lambda m: feed.at[place[m]], feed_land, feed_send, feed_recv)

    def attn_part(m):
        dp, t = scatter_entry(path, m)
        return attn.at[t, :, dp]

    attn_job = Scatter(path, attn_part, attn_land, attn_send, attn_recv)

    half = mid.shape[0]
    length = keys.shape[0]
    width = weights.shape[3]
    base = pl.multiple_of(c * half, half)
    other = pl.multiple_of((1 - c) * half, half)
    count = ints[0:1, 0:1]
    live = row_live(count, c * half, half)
    rows = feed.shape[2]
    xhat, rstd = centre(mid[...])
    normed2[...] = (xhat * vec[2:3, :] + vec[3:4, :]).astype(BF16)
    cot_load.wait()
    grad_low[...] = (grad_low[...].astype(F32) * live).astype(BF16)
    down_sum[...] = mid[...] + vec[5:6, :]
    norm_sum[...] = jnp.zeros_like(norm_sum)
    first = 0
    for g, group in enumerate(groups):
        number = len(group)
        for k in range(first, first + number):
            loads[k].wait()
        up = rows_of(feed, first, number, 0, loose)
        down = rows_of(feed, first, number, 1, loose)
        span = slice(first * rows, (first + number) * rows)
        bias_grad = 0.0
        for r in range(2):
            part = slice(r * half // 2, (r + 1) * half // 2)
            hidden = nt(normed2[part, :], up) + hidden_bias[:, span]
            bell = 0.5 + 0.5 * lax.erf(hidden * ROOT_HALF)
            act[part, :] = (hidden * bell).astype(BF16)
            slope = bell + hidden * (ROOT_TWO_PI_INV * jnp.exp(-0.5 * hidden * hidden))
            hidden_grad = nt(grad_low[part, :], down) * slope
            bias_grad = bias_grad + total_rows(hidden_grad)
            hidden_low[part, :] = hidden_grad.astype(BF16)
        down_sum[...] += nn(act[...], down)
        norm_sum[...] += nn(hidden_low[...], up)
        put_rows(feed, first, number, 0, tn(hidden_low[...], normed2[...]), loose)
        put_rows(feed, first, number, 1, tn(act[...], grad_low[...]), loose)
        for e, m in enumerate(group):
            dp, t = scatter_entry(path, m)
            begin, turn = divmod(e * rows, 128)
            piece = bias_grad[:, begin * 128 : min((begin + 2) * 128, bias_grad.shape[1])]
            piece = pltpu.roll(piece, piece.shape[1] - turn, 1) if turn else piece
            small_send[0, pl.ds(48 + dp * 2 + t, 1), :] = piece[:, 0:128]
        if g % 2 == 0:
            for m in group:
                feed_job.send(0, m)
        elif g == 1:
            for m in group:
                feed_job.step(m)
        first += number
    later = [m for m in groups[3] if m]

    def pump(number):
        for m in later[:number]:
            feed_job.step(m)
        del later[:number]

    mixed[...] = (live * down_sum[...]).astype(BF16)
    start_load = pltpu.make_async_copy(start_own, start, local_sem.at[1])
    start_load.start()
    wait_mixed = spread(cube, mixed, mixed_out, spread_send.at[0], spread_recv.at[0])
    pump(len(later) * 2 // 7)
    xhat, rstd = centre(mid[...])
    upstream = norm_sum[...]
    grad_out = grad_low[...].astype(F32)
    grad = grad_out + norm_back(xhat, rstd, vec[2:3, :], upstream)
    mid_grad[...] = grad
    mid_low[...] = grad.astype(BF16)
    sums = [
        None,
        None,
        total_rows(upstream * xhat),
        total_rows(upstream),
        total_rows(grad),
        total_rows(grad_out),
    ]

    for t in range(weights.shape[0]):
        cols = slice(t * width, (t + 1) * width)
        heads_grad[:, cols] = nn(mid_low[...], weights[t, 3]).astype(BF16)
        put_attn(attn, t, 3, tn(mid_low[...], attended[:, cols]), loose)
    product = heads_grad[...].astype(F32) * mixed_heads[...]
    head_of = lax.broadcasted_iota(jnp.int32, (16, D), 0)
    lanes = lax.broadcasted_iota(jnp.int32, (16, D), 1)
    pick = jnp.where(
        (lanes >= head_of * HD) & (lanes < head_of * HD + HD), 1.0, 0.0
    ).astype(BF16)
    hi = product.astype(BF16)
    delta[...] = nt(pick, hi) + nt(pick, (product - hi.astype(F32)).astype(BF16))
    lane, own, mark = lane_sets()
    dead = ((1.0 - row_live(count, 0, length)) * DEAD).astype(BF16)
    block = 512
    pumps = (2, 0, 1, 1, 1, len(later))
    q_sums, v_sums = [], []
    for p in range(D // PAIR):
        cols = slice(p * PAIR, (p + 1) * PAIR)
        q_parts = []
        v_parts = [0.0] * (length // block)
        k_parts = [0.0] * (length // block)
        for h in range(2):
            head = 2 * p + h
            qx = qs[:, cols] * own[h] + mark[h]
            gx = heads_grad[:, cols] * own[h]
            q_sum = jnp.zeros((half, PAIR), F32)
            for b in range(length // block):
                span = slice(b * block, (b + 1) * block)
                kx = keys[span, cols] * own[h] + dead[span] * mark[h]
                probs = jnp.exp(nt(kx, qx) - lse[head : head + 1, :])
                prob_grad = nt(values[span, cols], gx)
                score_low = (probs * (prob_grad - delta[head : head + 1, :])).astype(BF16)
                v_parts[b] = v_parts[b] + nn(probs.astype(BF16), gx)
                k_parts[b] = k_parts[b] + nn(score_low, qx) * own[h].astype(F32)
                q_sum = q_sum + tn(score_low, kx)
            q_parts.append(q_sum)
        q_grad = jnp.where(lane < HD, q_parts[0], q_parts[1]) * HD**-0.5
        q_low[:, cols] = q_grad.astype(BF16)
        q_sums.append(total_rows(q_grad))
        v_total = 0.0
        for b in range(length // block):
            span = slice(b * block, (b + 1) * block)
            k_low[span, cols] = k_parts[b].astype(BF16)
            v_low[span, cols] = v_parts[b].astype(BF16)
            v_total = v_total + total_rows(v_parts[b])
        v_sums.append(v_total)
        pump(pumps[p])

    halves = [slice(t * width, (t + 1) * width) for t in range(weights.shape[0])]
    part = 0.0
    for t, cols in enumerate(halves):
        part = (
            part
            + nt(k_low[pl.ds(other, half), cols], weights[t, 1])
            + nt(v_low[pl.ds(other, half), cols], weights[t, 2])
        )
    norm_other[...] = part.astype(BF16)
    exchange = pltpu.make_async_remote_copy(
        src_ref=norm_other,
        dst_ref=norm_land,
        send_sem=pair_sem.at[0],
        recv_sem=pair_sem.at[1],
        device_id=cube.sibling,
        device_id_type=MESH,
    )
    exchange.start()
    for t, cols in enumerate(halves):
        put_attn(attn, t, 0, tn(normed[pl.ds(base, half), :], q_low[:, cols]), loose)
        put_attn(attn, t, 1, tn(normed[...], k_low[:, cols]), loose)
        put_attn(attn, t, 2, tn(normed[...], v_low[:, cols]), loose)
    for g in (0, 2):
        for m in groups[g]:
            attn_job.send(0, m)
    upstream = 0.0
    for t, cols in enumerate(halves):
        upstream = (
            upstream
            + nt(q_low[:, cols], weights[t, 0])
            + nt(k_low[pl.ds(base, half), cols], weights[t, 1])
            + nt(v_low[pl.ds(base, half), cols], weights[t, 2])
        )
    for m in groups[1]:
        attn_job.step(m)
    start_load.wait()
    xhat, rstd = centre(start[...])
    exchange.wait()
    upstream = upstream + norm_land[...].astype(F32)
    grad = mid_grad[...] + norm_back(xhat, rstd, vec[0:1, :], upstream)
    input_half[...] = (live * grad).astype(BF16)
    wait_input = spread(cube, input_half, input_out, spread_send.at[1], spread_recv.at[1])
    sums[0], sums[1] = total_rows(upstream * xhat), total_rows(upstream)
    for j in range(D // 128):
        cols = slice(j * 128, (j + 1) * 128)
        for k, line in enumerate(sums):
            small_send[0, 8 * j + k : 8 * j + k + 1, :] = line[:, cols]
        small_send[0, 8 * j + 6 : 8 * j + 7, :] = q_sums[j]
        small_send[0, 8 * j + 7 : 8 * j + 8, :] = v_sums[j]
    smalls = []

    def small_step(p):
        copy = pltpu.make_async_remote_copy(
            src_ref=small_send.at[p],
            dst_ref=small_land.at[p],
            send_sem=small_sem.at[0, p],
            recv_sem=small_sem.at[1, p],
            device_id=path.partner(path.count - 1 - p),
            device_id_type=MESH,
        )
        copy.start()
        smalls.append(copy)

    def small_close(p):
        smalls[p].wait_recv()
        value = small_send[p] + small_land[p]
        if p + 1 < path.count:
            small_send[p + 1] = value
            small_step(p + 1)
        else:
            small_sum[...] = value

    small_step(0)
    closed = 0
    rest = [m for m in groups[3] if m]
    for k, m in enumerate(rest):
        attn_job.step(m)
        if k % 2 == 1 and closed < path.count:
            small_close(closed)
            closed += 1
    feed_sum[...] = feed_job.total(0)
    while closed < path.count:
        small_close(closed)
        closed += 1
    attn_sum[...] = attn_job.total(0)
    wait_mixed()
    wait_input()
    exchange_sent = smalls
    for copy in exchange_sent:
        copy.wait_send()
    feed_job.finish()
    attn_job.finish()


def finish_kernel(
    dp_size,
    heads,
    attn_sum,
    feed_sum,
    small,
    mixed_half,
    input_half,
    mixed,
    inputs,
    attn_out,
    bias_out,
    out_out,
    vec_out,
    up_out,
    hidden_out,
    down_out,
    room,
    local_sem,
):
    copies = []
    for k, (source, target) in enumerate(((mixed_half, mixed), (input_half, inputs))):
        for h in range(2):
            load = pltpu.make_async_copy(source.at[h], room.at[k, h], local_sem.at[0, k, h])
            load.start()
            copies.append(
                (load, pltpu.make_async_copy(room.at[k, h], target.at[h], local_sem.at[1, k, h]))
            )
    dp, t = lax.axis_index("dp"), lax.axis_index("tensor")
    attn_out[...] = attn_sum[0:3]
    out_out[...] = attn_sum[3]
    up_out[...] = feed_sum[0]
    down_out[...] = feed_sum[1]
    for load, store in copies:
        load.wait()
        store.start()
    per = vec_out.shape[1]
    lines = jnp.concatenate([small[8 * j : 8 * j + 8, :] for j in range(D // 128)], axis=1)
    vec_out[...] = pltpu.roll(lines, lax.rem(D - dp * per, D), 1)[0:6, 0:per]
    each = bias_out.shape[2]
    turned = pltpu.roll(lines, lax.rem(2 * D - t * (D // 2) - dp * each, D), 1)
    for k in range(2):
        for h in range(heads):
            bias_out[k, h : h + 1, :] = turned[6 + k : 7 + k, h * HD : h * HD + each]
    hidden_out[...] = small[pl.ds(48 + dp * 2 + t, 1), :][:, 0 : hidden_out.shape[1]]
    for load, store in copies:
        store.wait()


ANY = pl.BlockSpec(memory_space=pltpu.HBM)
VMEM = pl.BlockSpec(memory_space=pltpu.VMEM)


def shape(dims, kind):
    return jax.ShapeDtypeStruct(dims, kind)


def local(
    dp_size,
    tokens,
    counts,
    indices,
    ground_dist,
    cotangent,
    attn_weight,
    attn_bias,
    out_weight,
    vectors,
    up_weight,
    up_bias,
    down_weight,
):
    tensor = 2
    chips, length, width = tokens.shape
    half = length // 2
    attn_rows, attn_cols = attn_weight.shape[1:]
    ff_rows = down_weight.shape[0]
    ff = ff_rows * dp_size * tensor
    heads = attn_bias.shape[1]
    count = phases_of(dp_size)
    devices = 1 << count
    dma = pltpu.SemaphoreType.DMA

    ints = jnp.concatenate([counts, ground_dist, indices[0]]).astype(jnp.int32)
    ints = jnp.broadcast_to(ints[None, :], (8, length))

    tok2, cot2, ints2, packs_all, attn_all, up, down = pl.pallas_call(
        functools.partial(gather_kernel, dp_size),
        name="gather",
        out_shape=[
            shape((2, length, width), BF16),
            shape((2, half, width), BF16),
            shape((2, 8, length), jnp.int32),
            shape((dp_size, tensor, PACK, 128), BF16),
            shape((tensor, 4, dp_size, attn_rows, attn_cols), BF16),
            shape((ff_rows, width), BF16),
            shape((ff_rows, width), BF16),
        ],
        in_specs=[ANY] * 2 + [VMEM] + [ANY] * 7,
        out_specs=[VMEM, ANY] + [VMEM] * 2 + [ANY] + [VMEM] * 2,
        scratch_shapes=[
            pltpu.VMEM(attn_weight.shape, F32),
            pltpu.VMEM(out_weight.shape[::-1], F32),
            pltpu.VMEM(up_weight.shape[::-1], F32),
            pltpu.VMEM(down_weight.shape, F32),
            pltpu.VMEM(vectors.shape, F32),
            pltpu.VMEM(attn_bias.shape, F32),
            pltpu.VMEM((1,) + up_bias.shape, F32),
            pltpu.VMEM((4, attn_rows, attn_cols), BF16),
            pltpu.VMEM((PACK, 128), F32),
            pltpu.VMEM((length, width), BF16),
            dma((3, devices)),
            dma((3, devices)),
            dma((2, 3)),
            dma((13,)),
        ],
        compiler_params=pltpu.CompilerParams(
            collective_id=0, has_side_effects=True, vmem_limit_bytes=60 * MIB
        ),
    )(
        tokens[0],
        cotangent[0],
        ints,
        attn_weight,
        out_weight.T,
        up_weight.T,
        down_weight,
        vectors,
        attn_bias,
        up_bias[None],
    )

    quarter = width // 4
    omega = 1.0 / 10000.0 ** (jnp.arange(quarter, dtype=F32) / quarter)
    omega = jnp.broadcast_to(jnp.concatenate([omega, omega])[None], (8, 2 * quarter))

    (
        normed,
        start_own,
        qs,
        keys,
        values,
        mixed_heads,
        attended,
        lse,
        mid,
        vec,
        hidden_bias,
        image,
        weights,
        feed_all,
    ) = pl.pallas_call(
        functools.partial(forward_kernel, dp_size, heads),
        name="attend",
        out_shape=[
            shape((length, width), BF16),
            shape((half, width), F32),
            shape((half, width), BF16),
            shape((length, width), BF16),
            shape((length, width), BF16),
            shape((half, width), F32),
            shape((half, width), BF16),
            shape((PAIR, half), F32),
            shape((half, width), F32),
            shape((8, width), F32),
            shape((1, ff), F32),
            shape((8, length), jnp.int32),
            shape((tensor, 4, width, attn_cols), BF16),
            shape((dp_size, tensor, 2, ff_rows, width), BF16),
        ],
        in_specs=[VMEM] * 4 + [ANY] + [VMEM] * 2,
        out_specs=[VMEM] + [ANY] + [VMEM] * 11 + [ANY],
        scratch_shapes=[
            pltpu.VMEM((length, width), F32),
            pltpu.VMEM((8, width), F32),
            dma((2, devices)),
            dma((2, devices)),
            dma((6,)),
        ],
        compiler_params=pltpu.CompilerParams(
            collective_id=1, has_side_effects=True, vmem_limit_bytes=60 * MIB
        ),
    )(
        tok2,
        ints2,
        omega,
        packs_all,
        attn_all.reshape(tensor, 4, width, attn_cols),
        up,
        down,
    )

    ff_dims = (2, ff_rows, width)
    attn_dims = (4, attn_rows, attn_cols)
    half_rows, all_rows = (half, width), (length, width)
    quarter_ff = ff // 4
    small_dims = (-(-(48 + devices) // 8) * 8, 128)
    tight = attn_rows % 16 == 0 and ff_rows % 16 == 0
    attn_sum, feed_sum, small_sum, mixed_out, input_out = pl.pallas_call(
        functools.partial(back_kernel, dp_size),
        name="back",
        out_shape=[
            shape(attn_dims, F32),
            shape(ff_dims, F32),
            shape(small_dims, F32),
            shape((2, half, width), BF16),
            shape((2, half, width), BF16),
        ],
        in_specs=[VMEM] + [ANY] * 2 + [VMEM] * 11 + [ANY],
        out_specs=[VMEM] * 3 + [ANY] * 2,
        scratch_shapes=[
            pltpu.VMEM((devices,) + ff_dims, BF16),
            pltpu.VMEM((devices - 1,) + ff_dims, BF16),
            pltpu.VMEM((tensor, 4, dp_size, attn_rows, attn_cols), BF16),
            pltpu.VMEM((devices - 1,) + attn_dims, BF16),
            pltpu.VMEM(half_rows, BF16),
            pltpu.VMEM((half, quarter_ff), BF16),
            pltpu.VMEM((half, quarter_ff), BF16),
            pltpu.VMEM(half_rows, BF16),
            pltpu.VMEM(half_rows, F32),
            pltpu.VMEM(half_rows, F32),
            pltpu.VMEM(half_rows, BF16),
            pltpu.VMEM(all_rows, BF16),
            pltpu.VMEM(all_rows, BF16),
            pltpu.VMEM(half_rows, BF16),
            pltpu.VMEM((16, half), F32),
            pltpu.VMEM((count,) + small_dims, F32),
            pltpu.VMEM((count,) + small_dims, F32),
            pltpu.VMEM((8, 128) if tight else (quarter_ff, width), F32),
            dma((devices,)),
            dma((2,)),
            dma((devices,)),
            dma((devices,)),
            dma((devices,)),
            dma((devices,)),
            dma((2, count)),
            dma((2, 2)),
            dma((2, 2)),
            dma((2,)),
        ],
        compiler_params=pltpu.CompilerParams(
            collective_id=2, has_side_effects=True, vmem_limit_bytes=64 * MIB - 65536
        ),
    )(
        mid,
        cot2,
        feed_all,
        vec,
        hidden_bias,
        weights,
        attended,
        mixed_heads,
        qs,
        keys,
        values,
        lse,
        normed,
        image,
        start_own,
    )

    results = pl.pallas_call(
        functools.partial(finish_kernel, dp_size, heads),
        name="finish",
        out_shape=[
            shape((2, half, width), BF16),
            shape((2, half, width), BF16),
            shape(attn_weight.shape, F32),
            shape(attn_bias.shape, F32),
            shape(out_weight.shape[::-1], F32),
            shape(vectors.shape, F32),
            shape(up_weight.shape[::-1], F32),
            shape((1, ff_rows), F32),
            shape(down_weight.shape, F32),
        ],
        in_specs=[VMEM] * 3 + [ANY] * 2,
        out_specs=[ANY] * 2 + [VMEM] * 7,
        scratch_shapes=[pltpu.VMEM((2, 2, half, width), BF16), dma((2, 2, 2))],
        compiler_params=pltpu.CompilerParams(vmem_limit_bytes=60 * MIB),
    )(attn_sum, feed_sum, small_sum, mixed_out, input_out)
    return (
        results[0].reshape(1, length, width),
        results[1].reshape(1, length, width),
        results[2],
        results[3],
        results[4].T,
        results[5],
        results[6].T,
        results[7].reshape(ff_rows),
        results[8],
    )


def solution(mesh):
    placed = (
        P("dp", None, None),
        P("dp"),
        P("dp", None),
        P("dp"),
        P("dp", None, None),
        P(None, "dp", "tensor"),
        P(None, "tensor", "dp"),
        P("tensor", "dp"),
        P(None, "dp"),
        P(None, ("dp", "tensor")),
        P(("dp", "tensor")),
        P(("dp", "tensor"), None),
    )
    return jax.shard_map(
        functools.partial(local, mesh.shape["dp"]),
        mesh=mesh,
        in_specs=placed,
        out_specs=(
            P("dp", None, None),
            P("dp", None, None),
            P(None, "dp", "tensor"),
            P(None, "tensor", "dp"),
            P("tensor", "dp"),
            P(None, "dp"),
            P(None, ("dp", "tensor")),
            P(("dp", "tensor")),
            P(("dp", "tensor"), None),
        ),
        check_vma=False,
    )
```

```python
import functools

import jax
import jax.numpy as jnp
import numpy as np
from jax import lax
from jax.experimental import pallas as pl
from jax.experimental.pallas import tpu as pltpu
from jax.sharding import PartitionSpec as P

D = 768
HD = 64
GRID = 32
EPS = 1e-06
DEAD = -1e30
PAIR = 2 * HD
ROOT_HALF = 0.7071067811865476
ROOT_TWO_PI_INV = 0.3989422804014327

F32 = jnp.float32
BF16 = jnp.bfloat16
MESH = pl.DeviceIdType.MESH
MIB = 1 << 20
BACK = "xYZ"


def nn(a, b):
    return lax.dot_general(a, b, (((1,), (0,)), ((), ())), preferred_element_type=F32)


def nt(a, b):
    return lax.dot_general(a, b, (((1,), (1,)), ((), ())), preferred_element_type=F32)


def tn(a, b):
    return lax.dot_general(a, b, (((0,), (0,)), ((), ())), preferred_element_type=F32)


class Path:
    def __init__(self, cube, steps, mirror):
        self.cube, self.steps, self.mirror = cube, steps, mirror
        self.count = len(steps)

    def partner(self, p):
        return (self.cube.dp + self.steps[p][0], self.cube.t + self.steps[p][1])

    def entry(self, mask):
        dp, t = self.cube.dp, self.cube.t
        for p, (ddp, dt) in enumerate(self.steps):
            if mask >> p & 1:
                dp, t = dp + ddp, t + dt
        return dp, t

    def mirrored(self, mask):
        if self.mirror is None:
            return mask
        i, j = self.mirror
        return mask & ~(1 << i | 1 << j) | (mask >> i & 1) << j | (mask >> j & 1) << i


class Cube:
    def __init__(self, dp_size):
        self.dp = lax.axis_index("dp")
        self.t = lax.axis_index("tensor")
        self.core = lax.rem(self.dp, 2)

        def flip(b):
            return b * (1 - 2 * lax.rem(lax.div(self.dp, b), 2))

        self.dt, self.dy, self.dc = 1 - 2 * self.t, flip(2), flip(1)
        self.far = []
        b = dp_size // 2
        while b >= 4:
            self.far.append((flip(b), 0))
            b //= 2
        self.sibling = (self.dp + self.dc, self.t)
        self.across = (self.dp, self.t + self.dt)
        self.diagonal = (self.dp + self.dc, self.t + self.dt)

    def path(self, kind):
        c = self.core
        x, y, far, last = (0, self.dt), (self.dy, 0), self.far[:-1], self.far[-1]
        n = len(self.far)

        def pick(first, second):
            return tuple((1 - c) * f + c * s for f, s in zip(first, second))

        if kind == "zXY":
            steps, mirror = [*far, last, pick(x, y), pick(y, x)], (n, n + 1)
        elif kind == "XzY":
            steps, mirror = [*far, pick(x, y), last, pick(y, x)], (n - 1, n + 1)
        elif kind == "xYZ":
            steps, mirror = [*far, x, pick(y, last), pick(last, y)], (n, n + 1)
        else:
            steps, mirror = [*far, x, last, y], None
        return Path(self, steps + [(self.dc, 0)], mirror)

    def partners(self):
        return [(self.dp + ddp, self.t + dt) for ddp, dt in self.far] + [
            (self.dp + self.dy, self.t),
            self.across,
            self.sibling,
        ]


def phases_of(dp_size):
    return (2 * dp_size).bit_length() - 1


def enter(devices):
    barrier = pltpu.get_barrier_semaphore()
    for device in devices:
        pl.semaphore_signal(barrier, inc=1, device_id=device, device_id_type=MESH)
    pl.semaphore_wait(barrier, len(devices))


class Gather:
    def __init__(self, path, own, slot, send_sem, recv_sem):
        self.path, self.own, self.slot = path, own, slot
        self.send_sem, self.recv_sem = send_sem, recv_sem
        self.count = path.count
        self.sent = []
        self.order = sorted(
            ((p, m) for p in range(self.count) for m in range(1 << p)),
            key=lambda item: (item[1].bit_count(), item[0], item[1]),
        )

    def copy(self, p, mask, place, source):
        k = (1 << p) - 1 + mask
        there = (1 << p) - 1 + (self.path.mirrored(mask) if p == self.count - 1 else mask)
        return pltpu.make_async_remote_copy(
            src_ref=source,
            dst_ref=place,
            send_sem=self.send_sem.at[k],
            recv_sem=self.recv_sem.at[there],
            device_id=self.path.partner(p),
            device_id_type=MESH,
        )

    def send(self, p, mask):
        place = self.slot(*self.path.entry(mask))
        copy = self.copy(p, mask, place, self.own if mask == 0 else place)
        copy.start()
        self.sent.append(copy)

    def start(self):
        for p in range(self.count):
            self.send(p, 0)

    def step(self, k):
        p, mask = self.order[k]
        place = self.slot(*self.path.entry(mask | 1 << p))
        there = self.path.mirrored(mask) if p == self.count - 1 else mask
        self.copy(p, there, place, place).wait_recv()
        for later in range(p + 1, self.count):
            self.send(later, mask | 1 << p)

    def finish(self):
        for copy in self.sent:
            copy.wait_send()


def low_bit(m):
    return (m & -m).bit_length() - 1 if m else 99


class Scatter:
    def __init__(self, path, part, landed, send_sem, recv_sem):
        self.path, self.count = path, path.count
        self.part, self.landed = part, landed
        self.send_sem, self.recv_sem = send_sem, recv_sem
        self.sent = []
        self.order = send_order(path)

    def index(self, q, m):
        return (1 << (self.count - 1 - q)) - 1 + (m >> (q + 1))

    def describe(self, q, m, source):
        k = self.index(q, other_name(self.path, m) if q == 0 else m)
        return pltpu.make_async_remote_copy(
            src_ref=source,
            dst_ref=self.landed.at[k],
            send_sem=self.send_sem.at[k],
            recv_sem=self.recv_sem.at[k],
            device_id=self.path.partner(self.count - 1 - q),
            device_id_type=MESH,
        )

    def send(self, q, m):
        copy = self.describe(q, m, self.part(m))
        copy.start()
        self.sent.append(copy)

    def total(self, m):
        total = self.part(m)[...].astype(F32)
        for q in range(min(low_bit(m), self.count)):
            k = self.index(q, m)
            name = other_name(self.path, m) if q == 0 else m
            self.describe(q, name, self.landed.at[k]).wait_recv()
            total = total + self.landed[k].astype(F32)
        return total

    def step(self, m):
        self.part(m)[...] = self.total(m).astype(BF16)
        self.send(low_bit(m), m)

    def finish(self):
        for copy in self.sent:
            copy.wait_send()


def reverse(count, m):
    return sum((m >> q & 1) << (count - 1 - q) for q in range(count))


def other_name(path, m):
    return reverse(path.count, path.mirrored(reverse(path.count, m)))


def send_order(path):
    def rank(name):
        rest = name & ~3
        return (low_bit(rest), low_bit(rest & (rest - 1)), name)

    masks = range(1 << path.count)
    given = sorted((m for m in masks if m & 1), key=lambda m: rank(other_name(path, m)))
    kept = sorted((m for m in masks if not m & 1), key=rank)
    return [
        [m for m in given if other_name(path, m) & 2],
        [m for m in kept if m & 2],
        [m for m in given if not other_name(path, m) & 2],
        [m for m in kept if not m & 2],
    ]


def scatter_entry(path, m):
    return path.entry(reverse(path.count, m))


def spread(cube, half, out, send_sem, recv_sem):
    c, t = cube.core, cube.t
    mine = out.at[c]

    def push(device, k):
        return pltpu.make_async_remote_copy(
            src_ref=half,
            dst_ref=mine,
            send_sem=send_sem.at[k],
            recv_sem=recv_sem.at[c],
            device_id=device,
            device_id_type=MESH,
        )

    def arrival(h):
        return pltpu.make_async_remote_copy(
            src_ref=half,
            dst_ref=out.at[h],
            send_sem=send_sem.at[0],
            recv_sem=recv_sem.at[h],
            device_id=cube.sibling,
            device_id_type=MESH,
        )

    keep = pltpu.make_async_copy(half, mine, send_sem.at[0])

    @pl.when(c == t)
    def _():
        push(cube.across, 1).start()
        keep.start()

    @pl.when(c != t)
    def _():
        push(cube.diagonal, 1).start()
        push(cube.sibling, 0).start()

    def wait():
        @pl.when(c == t)
        def _():
            keep.wait()
            push(cube.across, 1).wait_send()
            arrival(1 - c).wait_recv()

        @pl.when(c != t)
        def _():
            push(cube.sibling, 0).wait_send()
            push(cube.diagonal, 1).wait_send()
            arrival(c).wait_recv()
            arrival(1 - c).wait_recv()

    return wait


PACK = 32


def centre(values):
    mean = jnp.mean(values, axis=-1, keepdims=True)
    centred = values - mean
    rstd = lax.rsqrt(jnp.mean(centred * centred, axis=-1, keepdims=True) + EPS)
    return centred * rstd, rstd


def row_live(count, offset, rows):
    places = lax.broadcasted_iota(jnp.int32, (rows, 1), 0) + offset
    return (places < count + 2).astype(F32)


def lane_sets():
    lane = lax.broadcasted_iota(jnp.int32, (1, PAIR), 1)
    own = [(lane < HD).astype(F32).astype(BF16), (lane >= HD).astype(F32).astype(BF16)]
    mark = [(lane == HD).astype(F32).astype(BF16), (lane == 0).astype(F32).astype(BF16)]
    return lane, own, mark


def place_rows(rows, offset, columns):
    a, r = divmod(offset, 128)
    lane = lax.broadcasted_iota(jnp.int32, rows.shape, 1)
    turned = pltpu.roll(rows, r, 1) if r else rows
    columns[a] = columns[a] + jnp.where(lane >= r, turned, 0.0)
    if r and a + 1 < len(columns):
        columns[a + 1] = columns[a + 1] + jnp.where(lane < r, turned, 0.0)


def read_packs(dp_size, heads, slots, packs, vec, bias, hidden, room):
    per = vec.shape[1] // dp_size
    tensor = packs.shape[1]
    each = hidden.shape[1] // (dp_size * tensor)
    inner = HD // dp_size
    row = lax.broadcasted_iota(jnp.int32, (8, 128), 0)
    vec_columns = [jnp.zeros((8, 128), F32) for k in range(vec.shape[1] // 128)]
    hidden_columns = [jnp.zeros((1, 128), F32) for k in range(hidden.shape[1] // 128)]
    room[...] = jnp.zeros_like(room)
    for dp in range(dp_size):
        for t in range(tensor):
            data = packs[dp, t].astype(F32)
            if t == 0:
                place_rows(jnp.where(row < 6, data[0:8], 0.0), dp * per, vec_columns)
            for k in range(2):
                room[t, k, dp * inner : (dp + 1) * inner, :] = data[8 + 8 * k : 8 + 8 * k + inner]
    for k, (dp, t) in enumerate(slots):
        place_rows(packs[dp, t].astype(F32)[6:7], k * each, hidden_columns)
    for k, column in enumerate(vec_columns):
        vec[:, k * 128 : (k + 1) * 128] = column
    for k, column in enumerate(hidden_columns):
        hidden[:, k * 128 : (k + 1) * 128] = column
    for k in range(2):
        columns = [jnp.zeros((1, 128), F32) for j in range(bias.shape[1] // 128)]
        for t in range(tensor):
            lines = room[t, k].T
            for h in range(heads):
                place_rows(lines[h : h + 1], (t * heads + h) * HD, columns)
        for j, column in enumerate(columns):
            bias[k : k + 1, j * 128 : (j + 1) * 128] = column


def front_kernel(
    dp_size,
    heads,
    counts,
    ground,
    indices,
    omega,
    tok,
    cot,
    attn_f,
    out_f,
    up_f,
    down_f,
    vec_f,
    bias_f,
    hidden_f,
    cot2,
    feed_all,
    start_own,
    weights,
    normed,
    qs,
    keys,
    values,
    mixed_heads,
    attended,
    lse,
    mid,
    vec,
    hidden_bias,
    ints,
    attn_in,
    out_in,
    up_in,
    down_in,
    vec_in,
    bias_in,
    hidden_in,
    attn,
    pack,
    packs,
    up,
    down,
    tok2,
    cot_in,
    ints2,
    line,
    start,
    bias,
    room,
    loose,
    send_sem,
    recv_sem,
    pair_sem,
    local_sem,
):
    cube = Cube(dp_size)
    c, own_image = cube.core, cube.t
    length, half = normed.shape[0], qs.shape[0]
    base = pl.multiple_of(c * half, half)
    other = pl.multiple_of((1 - c) * half, half)
    loads = [
        pltpu.make_async_copy(source, target, local_sem.at[k])
        for k, (source, target) in enumerate(
            (
                (attn_f, attn_in),
                (out_f, out_in),
                (vec_f, vec_in),
                (bias_f, bias_in),
                (hidden_f, hidden_in),
                (tok, tok2.at[c]),
                (cot, cot_in),
                (up_f, up_in),
                (down_f, down_in),
            )
        )
    ]
    for copy in loads:
        copy.start()
    line[...] = jnp.zeros_like(line)
    line[0:1, 0 : indices.shape[1]] = indices[...]
    slot = lax.broadcasted_iota(jnp.int32, line.shape, 1)
    shifted = pltpu.roll(line[...], 2, 1)
    shifted = jnp.where(slot == 0, counts[0], jnp.where(slot == 1, ground[0], shifted))
    ints2[c] = shifted
    for copy in loads[:5]:
        copy.wait()
    attn[0:3] = attn_in[...].astype(BF16)
    attn[3] = out_in[...].astype(BF16)
    pack[...] = jnp.zeros_like(pack)
    pack[0:6, 0 : vec_in.shape[1]] = vec_in[...]
    pack[6:7, 0 : hidden_in.shape[1]] = hidden_in[...]
    for k in range(2):
        pack[8 + 8 * k : 8 + 8 * k + bias_in.shape[1], 0 : bias_in.shape[2]] = bias_in[k]
    packs[cube.dp, cube.t] = pack[...].astype(BF16)
    weights[cube.t, :, cube.dp] = attn[...]
    enter(cube.partners())
    path = cube.path("XzY")
    pack_job = Gather(
        path,
        packs.at[cube.dp, cube.t],
        lambda dp, t: packs.at[dp, t],
        send_sem.at[0],
        recv_sem.at[0],
    )
    attn_jobs = [
        Gather(
            path,
            attn.at[2 * k : 2 * k + 2],
            lambda dp, t, k=k: weights.at[t, 2 * k : 2 * k + 2, dp],
            send_sem.at[k + 1],
            recv_sem.at[k + 1],
        )
        for k in range(2)
    ]
    feed_jobs = [
        Gather(
            path,
            source,
            lambda dp, t, k=k: feed_all.at[dp, t, k],
            send_sem.at[k + 3],
            recv_sem.at[k + 3],
        )
        for k, source in enumerate((up, down))
    ]
    pairs = [
        pltpu.make_async_remote_copy(
            src_ref=source,
            dst_ref=target.at[c],
            send_sem=pair_sem.at[0, k],
            recv_sem=pair_sem.at[1, k],
            device_id=cube.sibling,
            device_id_type=MESH,
        )
        for k, (source, target) in enumerate(
            ((ints2.at[c], ints2), (tok2.at[c], tok2), (cot_in.at[pl.ds(other, half)], cot2))
        )
    ]
    steps = len(pack_job.order)
    pack_job.start()
    for job in attn_jobs:
        job.start()
    pairs[0].start()
    loads[5].wait()
    pairs[1].start()
    early, late, feed_todo = [], [], []
    for k in range(steps):
        (early if 2 * k < steps else late).extend((job, k) for job in attn_jobs)
        early.extend((pack_job, j) for j in (2 * k, 2 * k + 1) if j < steps)
        feed_todo.extend((job, k) for job in feed_jobs)

    def pump(todo, number):
        for job, k in todo[:number]:
            job.step(k)
        del todo[:number]

    for copy in loads[7:]:
        copy.wait()
    up[...] = up_in[...].astype(BF16)
    down[...] = down_in[...].astype(BF16)
    loads[6].wait()
    pairs[2].start()
    keeps = [
        pltpu.make_async_copy(up, feed_all.at[cube.dp, cube.t, 0], local_sem.at[9]),
        pltpu.make_async_copy(down, feed_all.at[cube.dp, cube.t, 1], local_sem.at[10]),
        pltpu.make_async_copy(cot_in.at[pl.ds(base, half)], cot2.at[c], local_sem.at[11]),
    ]
    for copy in keeps:
        copy.start()
    pump(early, 12)
    pairs[0].wait_recv()
    pairs[1].wait_recv()

    ints[...] = ints2[own_image]
    count = ints[0:1, 0:1]
    quarter = D // 4
    scale = ints[0:1, 1:2].astype(F32) / 10.0
    angle = lax.broadcasted_iota(jnp.int32, (GRID, 2 * quarter), 0).astype(F32) * scale * omega[0:1, :]
    wave = lax.broadcasted_iota(jnp.int32, (GRID, 2 * quarter), 1)
    full = jnp.where(wave < quarter, jnp.sin(angle), jnp.cos(angle))
    hi = full.astype(BF16)
    rest = full - hi.astype(F32)
    middle = rest.astype(BF16)
    little = (rest - middle.astype(F32)).astype(BF16)
    stack = jnp.concatenate([hi, middle, little], axis=0)
    tile = 256
    for r in range(length // tile):
        span = slice(r * tile, (r + 1) * tile)
        index = ints[0:1, span]
        slots = lax.broadcasted_iota(jnp.int32, (1, tile), 1) + r * tile
        places = lax.broadcasted_iota(jnp.int32, (GRID, tile), 0)
        parts = []
        for part in (lax.shift_right_logical(index, 5), lax.bitwise_and(index, GRID - 1)):
            part = jnp.where(slots < 2, -1, part)
            hot = (places == part).astype(F32).astype(BF16)
            parts.append(tn(jnp.concatenate([hot, hot, hot], axis=0), stack))
        code = jnp.concatenate(parts, axis=1)
        live = row_live(count, r * tile, tile)
        start[span, :] = (tok2[own_image, span, :].astype(F32) + code) * live
        pump(early, 10)
    keep = pltpu.make_async_copy(start.at[pl.ds(base, half)], start_own, local_sem.at[12])
    keep.start()
    keeps.append(keep)
    pump(early, len(early))
    for job in feed_jobs:
        job.start()
    back_path = cube.path(BACK)
    slots = [scatter_entry(back_path, m) for group in send_order(back_path) for m in group]
    read_packs(dp_size, heads, slots, packs, vec, bias, hidden_bias, room)
    for r in range(length // tile):
        span = slice(r * tile, (r + 1) * tile)
        xhat, rstd = centre(start[span, :])
        normed[span, :] = (xhat * vec[0:1, :] + vec[1:2, :]).astype(BF16)
        pump(late, 4)
    pump(late, len(late))

    width = weights.shape[4]

    def weight(t, k):
        rows = weights.shape[3]
        if rows % 16 == 0:
            return weights[t, k].reshape(D, width)
        for e in range(dp_size):
            loose[e * rows : (e + 1) * rows, :] = weights[t, k, e].astype(F32)
        return loose[...].astype(BF16)

    for t in range(weights.shape[0]):
        cols = slice(t * width, (t + 1) * width)
        query = nn(normed[pl.ds(base, half), :], weight(t, 0)) + bias[0:1, cols]
        qs[:, cols] = query.astype(BF16) * jnp.asarray(HD**-0.5, BF16)
        for r in range(length // half):
            span = slice(r * half, (r + 1) * half)
            keys[span, cols] = nn(normed[span, :], weight(t, 1)).astype(BF16)
            values[span, cols] = (nn(normed[span, :], weight(t, 2)) + bias[1:2, cols]).astype(BF16)
        pump(feed_todo, 6)

    lane, own, mark = lane_sets()
    dead = ((1.0 - row_live(count, 0, length)) * DEAD).astype(BF16)
    wide = lax.broadcasted_iota(jnp.int32, (1, PAIR), 1)
    block = 256
    for r in range(half // block):
        span = slice(r * block, (r + 1) * block)
        sums = jnp.zeros((block, PAIR), F32)
        for p in range(D // PAIR):
            cols = slice(p * PAIR, (p + 1) * PAIR)
            outs = []
            for h in range(2):
                kx = keys[:, cols] * own[h] + dead * mark[h]
                qx = qs[span, cols] * own[h] + mark[h]
                scores = nt(qx, kx)
                top = jnp.max(scores, axis=1, keepdims=True)
                grown = jnp.exp(scores - top)
                total = jnp.sum(grown, axis=1, keepdims=True)
                outs.append(nn(grown.astype(BF16), values[:, cols]) / total)
                sums = jnp.where(wide == 2 * p + h, top + jnp.log(total), sums)
            both = jnp.where(lane < HD, outs[0], outs[1])
            mixed_heads[span, cols] = both
            attended[span, cols] = both.astype(BF16)
            pump(feed_todo, 3)
        lse[:, span] = sums.T
    out = nt(attended[:, :width], weight(0, 3))
    for t in range(1, weights.shape[0]):
        out = out + nt(attended[:, t * width : (t + 1) * width], weight(t, 3))
    mid[...] = start[pl.ds(base, half), :] + (out + vec[4:5, :])
    pump(feed_todo, len(feed_todo))
    for job in [pack_job] + attn_jobs + feed_jobs:
        job.finish()
    for copy in pairs[:2]:
        copy.wait_send()
    pairs[2].wait()
    for copy in keeps:
        copy.wait()


def norm_back(xhat, rstd, gain, upstream):
    scaled = upstream * gain
    return rstd * (
        scaled
        - jnp.mean(scaled, axis=-1, keepdims=True)
        - xhat * jnp.mean(scaled * xhat, axis=-1, keepdims=True)
    )


def total_rows(values):
    return jnp.sum(values, axis=0, keepdims=True)


def rows_of(ref, start, number, k, loose):
    rows = ref.shape[2]
    if rows % 16 == 0:
        return ref[start : start + number, k].reshape(number * rows, ref.shape[3])
    parts = []
    per = loose.shape[0] // rows
    for e in range(number):
        place = e % per * rows
        loose[place : place + rows, :] = ref[start + e, k].astype(F32)
        if place + rows == per * rows:
            parts.append(loose[0 : per * rows, :].astype(BF16))
    return jnp.concatenate(parts, axis=0)


def put_rows(ref, start, number, k, value, loose):
    rows = ref.shape[2]
    if rows % 16 == 0:
        ref[start : start + number, k] = value.astype(BF16).reshape(number, rows, ref.shape[3])
        return
    per = loose.shape[0] // rows
    for e in range(number):
        place = e % per * rows
        if place == 0:
            loose[0 : per * rows, :] = value[e * rows : (e + per) * rows, :]
        ref[start + e, k] = loose[place : place + rows, :].astype(BF16)


def put_attn(ref, t, k, value, loose):
    number, rows, cols = ref.shape[2:]
    if rows % 16 == 0:
        ref[t, k] = value.astype(BF16).reshape(number, rows, cols)
        return
    per = loose.shape[0] // rows
    for e in range(number):
        place = e % per * rows
        if place == 0:
            loose[0 : per * rows, 0:cols] = value[e * rows : (e + per) * rows, :]
        ref[t, k, e] = loose[place : place + rows, 0:cols].astype(BF16)


def back_kernel(
    dp_size,
    mid,
    cot2,
    feed_all,
    vec,
    hidden_bias,
    weights,
    attended,
    mixed_heads,
    qs,
    keys,
    values,
    lse,
    normed,
    ints,
    start_own,
    attn_sum,
    feed_sum,
    small_sum,
    mixed_out,
    input_out,
    feed,
    feed_land,
    attn,
    attn_land,
    normed2,
    act,
    hidden_low,
    grad_low,
    down_sum,
    norm_sum,
    mid_low,
    k_low,
    v_low,
    norm_land,
    delta,
    small_send,
    small_land,
    loose,
    load_sem,
    local_sem,
    feed_send,
    feed_recv,
    attn_send,
    attn_recv,
    small_sem,
    spread_send,
    spread_recv,
    pair_sem,
):
    cube = Cube(dp_size)
    c = cube.core
    mixed, heads_grad, q_low, start, mid_grad = normed2, act, hidden_low, down_sum, norm_sum
    input_half, norm_other = grad_low, mid_low
    path = cube.path(BACK)
    groups = send_order(path)
    slots = [m for group in groups for m in group]
    place = {m: k for k, m in enumerate(slots)}
    cot_load = pltpu.make_async_copy(cot2.at[cube.t], grad_low, local_sem.at[0])
    cot_load.start()
    loads = []
    for k, m in enumerate(slots):
        dp, t = scatter_entry(path, m)
        loads.append(pltpu.make_async_copy(feed_all.at[dp, t], feed.at[k], load_sem.at[k]))
        loads[k].start()
    enter(cube.partners() + [cube.diagonal])
    feed_job = Scatter(path, lambda m: feed.at[place[m]], feed_land, feed_send, feed_recv)

    def attn_part(m):
        dp, t = scatter_entry(path, m)
        return attn.at[t, :, dp]

    attn_job = Scatter(path, attn_part, attn_land, attn_send, attn_recv)

    half = mid.shape[0]
    length = keys.shape[0]
    width = weights.shape[3]
    base = pl.multiple_of(c * half, half)
    other = pl.multiple_of((1 - c) * half, half)
    count = ints[0:1, 0:1]
    live = row_live(count, c * half, half)
    rows = feed.shape[2]
    xhat, rstd = centre(mid[...])
    normed2[...] = (xhat * vec[2:3, :] + vec[3:4, :]).astype(BF16)
    cot_load.wait()
    grad_low[...] = (grad_low[...].astype(F32) * live).astype(BF16)
    down_sum[...] = mid[...] + vec[5:6, :]
    norm_sum[...] = jnp.zeros_like(norm_sum)
    first = 0
    for g, group in enumerate(groups):
        number = len(group)
        for k in range(first, first + number):
            loads[k].wait()
        up = rows_of(feed, first, number, 0, loose)
        down = rows_of(feed, first, number, 1, loose)
        span = slice(first * rows, (first + number) * rows)
        bias_grad = 0.0
        for r in range(2):
            part = slice(r * half // 2, (r + 1) * half // 2)
            hidden = nt(normed2[part, :], up) + hidden_bias[:, span]
            bell = 0.5 + 0.5 * lax.erf(hidden * ROOT_HALF)
            act[part, :] = (hidden * bell).astype(BF16)
            slope = bell + hidden * (ROOT_TWO_PI_INV * jnp.exp(-0.5 * hidden * hidden))
            hidden_grad = nt(grad_low[part, :], down) * slope
            bias_grad = bias_grad + total_rows(hidden_grad)
            hidden_low[part, :] = hidden_grad.astype(BF16)
        down_sum[...] += nn(act[...], down)
        norm_sum[...] += nn(hidden_low[...], up)
        put_rows(feed, first, number, 0, tn(hidden_low[...], normed2[...]), loose)
        put_rows(feed, first, number, 1, tn(act[...], grad_low[...]), loose)
        for e, m in enumerate(group):
            dp, t = scatter_entry(path, m)
            begin, turn = divmod(e * rows, 128)
            piece = bias_grad[:, begin * 128 : min((begin + 2) * 128, bias_grad.shape[1])]
            piece = pltpu.roll(piece, piece.shape[1] - turn, 1) if turn else piece
            small_send[0, pl.ds(48 + dp * 2 + t, 1), :] = piece[:, 0:128]
        if g % 2 == 0:
            for m in group:
                feed_job.send(0, m)
        elif g == 1:
            for m in group:
                feed_job.step(m)
        first += number
    later = [m for m in groups[3] if m]

    def pump(number):
        for m in later[:number]:
            feed_job.step(m)
        del later[:number]

    mixed[...] = (live * down_sum[...]).astype(BF16)
    start_load = pltpu.make_async_copy(start_own, start, local_sem.at[1])
    start_load.start()
    wait_mixed = spread(cube, mixed, mixed_out, spread_send.at[0], spread_recv.at[0])
    pump(1)
    xhat, rstd = centre(mid[...])
    upstream = norm_sum[...]
    grad_out = grad_low[...].astype(F32)
    grad = grad_out + norm_back(xhat, rstd, vec[2:3, :], upstream)
    mid_grad[...] = grad
    mid_low[...] = grad.astype(BF16)
    sums = [
        None,
        None,
        total_rows(upstream * xhat),
        total_rows(upstream),
        total_rows(grad),
        total_rows(grad_out),
    ]

    for t in range(weights.shape[0]):
        cols = slice(t * width, (t + 1) * width)
        heads_grad[:, cols] = nn(mid_low[...], weights[t, 3]).astype(BF16)
        put_attn(attn, t, 3, tn(mid_low[...], attended[:, cols]), loose)
    product = heads_grad[...].astype(F32) * mixed_heads[...]
    head_of = lax.broadcasted_iota(jnp.int32, (16, D), 0)
    lanes = lax.broadcasted_iota(jnp.int32, (16, D), 1)
    pick = jnp.where(
        (lanes >= head_of * HD) & (lanes < head_of * HD + HD), 1.0, 0.0
    ).astype(BF16)
    hi = product.astype(BF16)
    pump(1)
    delta[...] = nt(pick, hi) + nt(pick, (product - hi.astype(F32)).astype(BF16))
    lane, own, mark = lane_sets()
    dead = ((1.0 - row_live(count, 0, length)) * DEAD).astype(BF16)
    block = 512
    pumps = (1, 1, 0, 0, 0, 2)
    q_sums, v_sums = [], []
    for p in range(D // PAIR):
        cols = slice(p * PAIR, (p + 1) * PAIR)
        q_parts = []
        v_parts = [0.0] * (length // block)
        k_parts = [0.0] * (length // block)
        for h in range(2):
            head = 2 * p + h
            qx = qs[:, cols] * own[h] + mark[h]
            gx = heads_grad[:, cols] * own[h]
            q_sum = jnp.zeros((PAIR, half), F32)
            for b in range(length // block):
                span = slice(b * block, (b + 1) * block)
                kx = keys[span, cols] * own[h] + dead[span] * mark[h]
                probs = jnp.exp(nt(kx, qx) - lse[head : head + 1, :])
                prob_grad = nt(values[span, cols], gx)
                score_low = (probs * (prob_grad - delta[head : head + 1, :])).astype(BF16)
                v_parts[b] = v_parts[b] + nn(probs.astype(BF16), gx)
                k_parts[b] = k_parts[b] + nn(score_low, qx) * own[h].astype(F32)
                q_sum = q_sum + tn(kx, score_low)
            q_parts.append(q_sum.T)
        q_grad = jnp.where(lane < HD, q_parts[0], q_parts[1]) * HD**-0.5
        q_low[:, cols] = q_grad.astype(BF16)
        q_sums.append(total_rows(q_grad))
        v_total = 0.0
        for b in range(length // block):
            span = slice(b * block, (b + 1) * block)
            k_low[span, cols] = k_parts[b].astype(BF16)
            v_low[span, cols] = v_parts[b].astype(BF16)
            v_total = v_total + total_rows(v_parts[b])
        v_sums.append(v_total)
        pump(pumps[p])

    halves = [slice(t * width, (t + 1) * width) for t in range(weights.shape[0])]
    part = 0.0
    for t, cols in enumerate(halves):
        part = (
            part
            + nt(k_low[pl.ds(other, half), cols], weights[t, 1])
            + nt(v_low[pl.ds(other, half), cols], weights[t, 2])
        )
    norm_other[...] = part.astype(BF16)
    exchange = pltpu.make_async_remote_copy(
        src_ref=norm_other,
        dst_ref=norm_land,
        send_sem=pair_sem.at[0],
        recv_sem=pair_sem.at[1],
        device_id=cube.sibling,
        device_id_type=MESH,
    )
    exchange.start()
    for t, cols in enumerate(halves):
        put_attn(attn, t, 0, tn(normed[pl.ds(base, half), :], q_low[:, cols]), loose)
        put_attn(attn, t, 1, tn(normed[...], k_low[:, cols]), loose)
        put_attn(attn, t, 2, tn(normed[...], v_low[:, cols]), loose)
    for g in (0, 2):
        for m in groups[g]:
            attn_job.send(0, m)
    pump(len(later))
    upstream = 0.0
    for t, cols in enumerate(halves):
        upstream = (
            upstream
            + nt(q_low[:, cols], weights[t, 0])
            + nt(k_low[pl.ds(base, half), cols], weights[t, 1])
            + nt(v_low[pl.ds(base, half), cols], weights[t, 2])
        )
    for m in groups[1]:
        attn_job.step(m)
    start_load.wait()
    xhat, rstd = centre(start[...])
    exchange.wait()
    upstream = upstream + norm_land[...].astype(F32)
    grad = mid_grad[...] + norm_back(xhat, rstd, vec[0:1, :], upstream)
    input_half[...] = (live * grad).astype(BF16)
    wait_input = spread(cube, input_half, input_out, spread_send.at[1], spread_recv.at[1])
    sums[0], sums[1] = total_rows(upstream * xhat), total_rows(upstream)
    for j in range(D // 128):
        cols = slice(j * 128, (j + 1) * 128)
        for k, line in enumerate(sums):
            small_send[0, 8 * j + k : 8 * j + k + 1, :] = line[:, cols]
        small_send[0, 8 * j + 6 : 8 * j + 7, :] = q_sums[j]
        small_send[0, 8 * j + 7 : 8 * j + 8, :] = v_sums[j]
    smalls = []

    def small_step(p):
        copy = pltpu.make_async_remote_copy(
            src_ref=small_send.at[p],
            dst_ref=small_land.at[p],
            send_sem=small_sem.at[0, p],
            recv_sem=small_sem.at[1, p],
            device_id=path.partner(path.count - 1 - p),
            device_id_type=MESH,
        )
        copy.start()
        smalls.append(copy)

    def small_close(p):
        smalls[p].wait_recv()
        value = small_send[p] + small_land[p]
        if p + 1 < path.count:
            small_send[p + 1] = value
            small_step(p + 1)
        else:
            small_sum[...] = value

    small_step(0)
    closed = 0
    rest = [m for m in groups[3] if m]
    for k, m in enumerate(rest):
        attn_job.step(m)
        if k % 2 == 1 and closed < path.count:
            small_close(closed)
            closed += 1
    feed_sum[...] = feed_job.total(0)
    while closed < path.count:
        small_close(closed)
        closed += 1
    attn_sum[...] = attn_job.total(0)
    wait_mixed()
    wait_input()
    exchange_sent = smalls
    for copy in exchange_sent:
        copy.wait_send()
    feed_job.finish()
    attn_job.finish()


def finish_kernel(
    dp_size,
    heads,
    attn_sum,
    feed_sum,
    small,
    mixed_half,
    input_half,
    mixed,
    inputs,
    attn_out,
    bias_out,
    out_out,
    vec_out,
    up_out,
    hidden_out,
    down_out,
    room,
    local_sem,
):
    copies = []
    for k, (source, target) in enumerate(((mixed_half, mixed), (input_half, inputs))):
        for h in range(2):
            load = pltpu.make_async_copy(source.at[h], room.at[k, h], local_sem.at[0, k, h])
            load.start()
            copies.append(
                (load, pltpu.make_async_copy(room.at[k, h], target.at[h], local_sem.at[1, k, h]))
            )
    dp, t = lax.axis_index("dp"), lax.axis_index("tensor")
    attn_out[...] = attn_sum[0:3]
    out_out[...] = attn_sum[3]
    up_out[...] = feed_sum[0]
    down_out[...] = feed_sum[1]
    for load, store in copies:
        load.wait()
        store.start()
    per = vec_out.shape[1]
    lines = jnp.concatenate([small[8 * j : 8 * j + 8, :] for j in range(D // 128)], axis=1)
    vec_out[...] = pltpu.roll(lines, lax.rem(D - dp * per, D), 1)[0:6, 0:per]
    each = bias_out.shape[1]
    turned = pltpu.roll(lines, lax.rem(2 * D - t * (D // 2) - dp * each, D), 1)
    for k in range(2):
        lines = [turned[6 + k : 7 + k, h * HD : (h + 1) * HD] for h in range(heads)]
        lines.append(jnp.zeros((8 - heads, HD), F32))
        bias_out[k] = jnp.concatenate(lines, axis=0).T[0:each, 0:heads]
    hidden_out[...] = small[pl.ds(48 + dp * 2 + t, 1), :][:, 0 : hidden_out.shape[1]]
    for load, store in copies:
        store.wait()


ANY = pl.BlockSpec(memory_space=pltpu.HBM)
VMEM = pl.BlockSpec(memory_space=pltpu.VMEM)
SMEM = pl.BlockSpec(memory_space=pltpu.SMEM)


def shape(dims, kind):
    return jax.ShapeDtypeStruct(dims, kind)


def local(
    dp_size,
    tokens,
    counts,
    indices,
    ground_dist,
    cotangent,
    attn_weight,
    attn_bias,
    out_weight,
    vectors,
    up_weight,
    up_bias,
    down_weight,
):
    tensor = 2
    chips, length, width = tokens.shape
    half = length // 2
    attn_rows, attn_cols = attn_weight.shape[1:]
    ff_rows = down_weight.shape[0]
    ff = ff_rows * dp_size * tensor
    heads = attn_bias.shape[1]
    count = phases_of(dp_size)
    devices = 1 << count
    dma = pltpu.SemaphoreType.DMA

    quarter = width // 4
    omega = 1.0 / 10000.0 ** (np.arange(quarter) / quarter)
    omega = jnp.asarray(np.tile(omega.astype(np.float32), (8, 2)))
    inner = attn_bias.shape[2]
    half_rows, all_rows = (half, width), (length, width)
    tight = attn_rows % 16 == 0 and ff_rows % 16 == 0

    (
        cot2,
        feed_all,
        start_own,
        weights,
        normed,
        qs,
        keys,
        values,
        mixed_heads,
        attended,
        lse,
        mid,
        vec,
        hidden_bias,
        image,
    ) = pl.pallas_call(
        functools.partial(front_kernel, dp_size, heads),
        name="front",
        out_shape=[
            shape((2, half, width), BF16),
            shape((dp_size, tensor, 2, ff_rows, width), BF16),
            shape(half_rows, F32),
            shape((tensor, 4, dp_size, attn_rows, attn_cols), BF16),
            shape(all_rows, BF16),
            shape(half_rows, BF16),
            shape(all_rows, BF16),
            shape(all_rows, BF16),
            shape(half_rows, F32),
            shape(half_rows, BF16),
            shape((PAIR, half), F32),
            shape(half_rows, F32),
            shape((8, width), F32),
            shape((1, ff), F32),
            shape((8, length), jnp.int32),
        ],
        in_specs=[SMEM] * 2 + [VMEM] * 2 + [ANY] * 9,
        out_specs=[ANY] * 3 + [VMEM] * 12,
        scratch_shapes=[
            pltpu.VMEM(attn_weight.shape, F32),
            pltpu.VMEM(out_weight.shape[::-1], F32),
            pltpu.VMEM(up_weight.shape[::-1], F32),
            pltpu.VMEM(down_weight.shape, F32),
            pltpu.VMEM(vectors.shape, F32),
            pltpu.VMEM((2, inner, heads), F32),
            pltpu.VMEM((1,) + up_bias.shape, F32),
            pltpu.VMEM((4, attn_rows, attn_cols), BF16),
            pltpu.VMEM((PACK, 128), F32),
            pltpu.VMEM((dp_size, tensor, PACK, 128), BF16),
            pltpu.VMEM((ff_rows, width), BF16),
            pltpu.VMEM((ff_rows, width), BF16),
            pltpu.VMEM((2,) + all_rows, BF16),
            pltpu.VMEM(all_rows, BF16),
            pltpu.VMEM((2, 8, length), jnp.int32),
            pltpu.VMEM((8, length), jnp.int32),
            pltpu.VMEM(all_rows, F32),
            pltpu.VMEM((8, width), F32),
            pltpu.VMEM((tensor, 2, 128, 128), F32),
            pltpu.VMEM((8, 128) if tight else (width, attn_cols), F32),
            dma((5, devices)),
            dma((5, devices)),
            dma((2, 3)),
            dma((13,)),
        ],
        compiler_params=pltpu.CompilerParams(
            collective_id=0, has_side_effects=True, vmem_limit_bytes=60 * MIB
        ),
    )(
        counts,
        ground_dist,
        indices,
        omega,
        tokens[0],
        cotangent[0],
        attn_weight,
        out_weight.T,
        up_weight.T,
        down_weight,
        vectors,
        attn_bias.transpose(0, 2, 1),
        up_bias[None],
    )
    weights = weights.reshape(tensor, 4, width, attn_cols)

    ff_dims = (2, ff_rows, width)
    attn_dims = (4, attn_rows, attn_cols)
    quarter_ff = ff // 4
    small_dims = (-(-(48 + devices) // 8) * 8, 128)
    attn_sum, feed_sum, small_sum, mixed_out, input_out = pl.pallas_call(
        functools.partial(back_kernel, dp_size),
        name="back",
        out_shape=[
            shape(attn_dims, F32),
            shape(ff_dims, F32),
            shape(small_dims, F32),
            shape((2, half, width), BF16),
            shape((2, half, width), BF16),
        ],
        in_specs=[VMEM] + [ANY] * 2 + [VMEM] * 11 + [ANY],
        out_specs=[VMEM] * 3 + [ANY] * 2,
        scratch_shapes=[
            pltpu.VMEM((devices,) + ff_dims, BF16),
            pltpu.VMEM((devices - 1,) + ff_dims, BF16),
            pltpu.VMEM((tensor, 4, dp_size, attn_rows, attn_cols), BF16),
            pltpu.VMEM((devices - 1,) + attn_dims, BF16),
            pltpu.VMEM(half_rows, BF16),
            pltpu.VMEM((half, quarter_ff), BF16),
            pltpu.VMEM((half, quarter_ff), BF16),
            pltpu.VMEM(half_rows, BF16),
            pltpu.VMEM(half_rows, F32),
            pltpu.VMEM(half_rows, F32),
            pltpu.VMEM(half_rows, BF16),
            pltpu.VMEM(all_rows, BF16),
            pltpu.VMEM(all_rows, BF16),
            pltpu.VMEM(half_rows, BF16),
            pltpu.VMEM((16, half), F32),
            pltpu.VMEM((count,) + small_dims, F32),
            pltpu.VMEM((count,) + small_dims, F32),
            pltpu.VMEM((8, 128) if tight else (quarter_ff // 4, width), F32),
            dma((devices,)),
            dma((2,)),
            dma((devices,)),
            dma((devices,)),
            dma((devices,)),
            dma((devices,)),
            dma((2, count)),
            dma((2, 2)),
            dma((2, 2)),
            dma((2,)),
        ],
        compiler_params=pltpu.CompilerParams(
            collective_id=2, has_side_effects=True, vmem_limit_bytes=64 * MIB - 65536
        ),
    )(
        mid,
        cot2,
        feed_all,
        vec,
        hidden_bias,
        weights,
        attended,
        mixed_heads,
        qs,
        keys,
        values,
        lse,
        normed,
        image,
        start_own,
    )

    results = pl.pallas_call(
        functools.partial(finish_kernel, dp_size, heads),
        name="finish",
        out_shape=[
            shape((2, half, width), BF16),
            shape((2, half, width), BF16),
            shape(attn_weight.shape, F32),
            shape((2, inner, heads), F32),
            shape(out_weight.shape[::-1], F32),
            shape(vectors.shape, F32),
            shape(up_weight.shape[::-1], F32),
            shape((1, ff_rows), F32),
            shape(down_weight.shape, F32),
        ],
        in_specs=[VMEM] * 3 + [ANY] * 2,
        out_specs=[ANY] * 2 + [VMEM] * 7,
        scratch_shapes=[pltpu.VMEM((2, 2, half, width), BF16), dma((2, 2, 2))],
        compiler_params=pltpu.CompilerParams(vmem_limit_bytes=60 * MIB),
    )(attn_sum, feed_sum, small_sum, mixed_out, input_out)
    return (
        results[0].reshape(1, length, width),
        results[1].reshape(1, length, width),
        results[2],
        results[3].transpose(0, 2, 1),
        results[4].T,
        results[5],
        results[6].T,
        results[7].reshape(ff_rows),
        results[8],
    )


def solution(mesh):
    placed = (
        P("dp", None, None),
        P("dp"),
        P("dp", None),
        P("dp"),
        P("dp", None, None),
        P(None, "dp", "tensor"),
        P(None, "tensor", "dp"),
        P("tensor", "dp"),
        P(None, "dp"),
        P(None, ("dp", "tensor")),
        P(("dp", "tensor")),
        P(("dp", "tensor"), None),
    )
    return jax.shard_map(
        functools.partial(local, mesh.shape["dp"]),
        mesh=mesh,
        in_specs=placed,
        out_specs=(
            P("dp", None, None),
            P("dp", None, None),
            P(None, "dp", "tensor"),
            P(None, "tensor", "dp"),
            P("tensor", "dp"),
            P(None, "dp"),
            P(None, ("dp", "tensor")),
            P(("dp", "tensor")),
            P(("dp", "tensor"), None),
        ),
        check_vma=False,
    )
```

```python
import functools

import jax
import jax.numpy as jnp
import numpy as np
from jax import lax
from jax.experimental import pallas as pl
from jax.experimental.pallas import tpu as pltpu
from jax.sharding import PartitionSpec as P

D = 768
HD = 64
GRID = 32
EPS = 1e-06
DEAD = -1e30
PAIR = 2 * HD
ROOT_HALF = 0.7071067811865476
ROOT_TWO_PI_INV = 0.3989422804014327

F32 = jnp.float32
BF16 = jnp.bfloat16
MESH = pl.DeviceIdType.MESH
MIB = 1 << 20
BACK = "xYZ"


def nn(a, b):
    return lax.dot_general(a, b, (((1,), (0,)), ((), ())), preferred_element_type=F32)


def nt(a, b):
    return lax.dot_general(a, b, (((1,), (1,)), ((), ())), preferred_element_type=F32)


def tn(a, b):
    return lax.dot_general(a, b, (((0,), (0,)), ((), ())), preferred_element_type=F32)


class Path:
    def __init__(self, cube, steps, mirror):
        self.cube, self.steps, self.mirror = cube, steps, mirror
        self.count = len(steps)

    def partner(self, p):
        return (self.cube.dp + self.steps[p][0], self.cube.t + self.steps[p][1])

    def entry(self, mask):
        dp, t = self.cube.dp, self.cube.t
        for p, (ddp, dt) in enumerate(self.steps):
            if mask >> p & 1:
                dp, t = dp + ddp, t + dt
        return dp, t

    def mirrored(self, mask):
        if self.mirror is None:
            return mask
        i, j = self.mirror
        return mask & ~(1 << i | 1 << j) | (mask >> i & 1) << j | (mask >> j & 1) << i


class Cube:
    def __init__(self, dp_size):
        self.dp = lax.axis_index("dp")
        self.t = lax.axis_index("tensor")
        self.core = lax.rem(self.dp, 2)

        def flip(b):
            return b * (1 - 2 * lax.rem(lax.div(self.dp, b), 2))

        self.dt, self.dy, self.dc = 1 - 2 * self.t, flip(2), flip(1)
        self.far = []
        b = dp_size // 2
        while b >= 4:
            self.far.append((flip(b), 0))
            b //= 2
        self.sibling = (self.dp + self.dc, self.t)
        self.across = (self.dp, self.t + self.dt)
        self.diagonal = (self.dp + self.dc, self.t + self.dt)

    def path(self, kind):
        c = self.core
        x, y, far, last = (0, self.dt), (self.dy, 0), self.far[:-1], self.far[-1]
        n = len(self.far)

        def pick(first, second):
            return tuple((1 - c) * f + c * s for f, s in zip(first, second))

        if kind == "zXY":
            steps, mirror = [*far, last, pick(x, y), pick(y, x)], (n, n + 1)
        elif kind == "XzY":
            steps, mirror = [*far, pick(x, y), last, pick(y, x)], (n - 1, n + 1)
        elif kind == "xYZ":
            steps, mirror = [*far, x, pick(y, last), pick(last, y)], (n, n + 1)
        else:
            steps, mirror = [*far, x, last, y], None
        return Path(self, steps + [(self.dc, 0)], mirror)

    def partners(self):
        return [(self.dp + ddp, self.t + dt) for ddp, dt in self.far] + [
            (self.dp + self.dy, self.t),
            self.across,
            self.sibling,
        ]


def phases_of(dp_size):
    return (2 * dp_size).bit_length() - 1


def announce(devices):
    barrier = pltpu.get_barrier_semaphore()
    for device in devices:
        pl.semaphore_signal(barrier, inc=1, device_id=device, device_id_type=MESH)


def meet(devices):
    pl.semaphore_wait(pltpu.get_barrier_semaphore(), len(devices))


class Gather:
    def __init__(self, path, own, slot, send_sem, recv_sem):
        self.path, self.own, self.slot = path, own, slot
        self.send_sem, self.recv_sem = send_sem, recv_sem
        self.count = path.count
        self.sent = []
        self.order = sorted(
            ((p, m) for p in range(self.count) for m in range(1 << p)),
            key=lambda item: (item[1].bit_count(), item[0], item[1]),
        )

    def copy(self, p, mask, place, source):
        k = (1 << p) - 1 + mask
        there = (1 << p) - 1 + (self.path.mirrored(mask) if p == self.count - 1 else mask)
        return pltpu.make_async_remote_copy(
            src_ref=source,
            dst_ref=place,
            send_sem=self.send_sem.at[k],
            recv_sem=self.recv_sem.at[there],
            device_id=self.path.partner(p),
            device_id_type=MESH,
        )

    def send(self, p, mask):
        place = self.slot(*self.path.entry(mask))
        copy = self.copy(p, mask, place, self.own if mask == 0 else place)
        copy.start()
        self.sent.append(copy)

    def start(self):
        for p in range(self.count):
            self.send(p, 0)

    def step(self, k):
        p, mask = self.order[k]
        place = self.slot(*self.path.entry(mask | 1 << p))
        there = self.path.mirrored(mask) if p == self.count - 1 else mask
        self.copy(p, there, place, place).wait_recv()
        for later in range(p + 1, self.count):
            self.send(later, mask | 1 << p)

    def finish(self):
        for copy in self.sent:
            copy.wait_send()


def low_bit(m):
    return (m & -m).bit_length() - 1 if m else 99


class Scatter:
    def __init__(self, path, part, landed, send_sem, recv_sem):
        self.path, self.count = path, path.count
        self.part, self.landed = part, landed
        self.send_sem, self.recv_sem = send_sem, recv_sem
        self.sent = []
        self.order = send_order(path)

    def index(self, q, m):
        return (1 << (self.count - 1 - q)) - 1 + (m >> (q + 1))

    def describe(self, q, m, source):
        k = self.index(q, other_name(self.path, m) if q == 0 else m)
        return pltpu.make_async_remote_copy(
            src_ref=source,
            dst_ref=self.landed.at[k],
            send_sem=self.send_sem.at[k],
            recv_sem=self.recv_sem.at[k],
            device_id=self.path.partner(self.count - 1 - q),
            device_id_type=MESH,
        )

    def send(self, q, m):
        copy = self.describe(q, m, self.part(m))
        copy.start()
        self.sent.append(copy)

    def total(self, m):
        total = self.part(m)[...].astype(F32)
        for q in range(min(low_bit(m), self.count)):
            k = self.index(q, m)
            name = other_name(self.path, m) if q == 0 else m
            self.describe(q, name, self.landed.at[k]).wait_recv()
            total = total + self.landed[k].astype(F32)
        return total

    def step(self, m):
        self.part(m)[...] = self.total(m).astype(BF16)
        self.send(low_bit(m), m)

    def finish(self):
        for copy in self.sent:
            copy.wait_send()


def reverse(count, m):
    return sum((m >> q & 1) << (count - 1 - q) for q in range(count))


def other_name(path, m):
    return reverse(path.count, path.mirrored(reverse(path.count, m)))


def send_order(path):
    def rank(name):
        rest = name & ~3
        return (low_bit(rest), low_bit(rest & (rest - 1)), name)

    masks = range(1 << path.count)
    given = sorted((m for m in masks if m & 1), key=lambda m: rank(other_name(path, m)))
    kept = sorted((m for m in masks if not m & 1), key=rank)
    return [
        [m for m in given if other_name(path, m) & 2],
        [m for m in kept if m & 2],
        [m for m in given if not other_name(path, m) & 2],
        [m for m in kept if not m & 2],
    ]


def scatter_entry(path, m):
    return path.entry(reverse(path.count, m))


def spread(cube, half, out, send_sem, recv_sem):
    c, t = cube.core, cube.t
    mine = out.at[c]

    def push(device, k):
        return pltpu.make_async_remote_copy(
            src_ref=half,
            dst_ref=mine,
            send_sem=send_sem.at[k],
            recv_sem=recv_sem.at[c],
            device_id=device,
            device_id_type=MESH,
        )

    def arrival(h):
        return pltpu.make_async_remote_copy(
            src_ref=half,
            dst_ref=out.at[h],
            send_sem=send_sem.at[0],
            recv_sem=recv_sem.at[h],
            device_id=cube.sibling,
            device_id_type=MESH,
        )

    keep = pltpu.make_async_copy(half, mine, send_sem.at[0])

    @pl.when(c == t)
    def _():
        push(cube.across, 1).start()
        keep.start()

    @pl.when(c != t)
    def _():
        push(cube.diagonal, 1).start()
        push(cube.sibling, 0).start()

    def wait():
        @pl.when(c == t)
        def _():
            keep.wait()
            push(cube.across, 1).wait_send()
            arrival(1 - c).wait_recv()

        @pl.when(c != t)
        def _():
            push(cube.sibling, 0).wait_send()
            push(cube.diagonal, 1).wait_send()
            arrival(c).wait_recv()
            arrival(1 - c).wait_recv()

    return wait


PACK = 32


def centre(values):
    mean = jnp.mean(values, axis=-1, keepdims=True)
    centred = values - mean
    rstd = lax.rsqrt(jnp.mean(centred * centred, axis=-1, keepdims=True) + EPS)
    return centred * rstd, rstd


def row_live(count, offset, rows):
    places = lax.broadcasted_iota(jnp.int32, (rows, 1), 0) + offset
    return (places < count + 2).astype(F32)


def lane_sets():
    lane = lax.broadcasted_iota(jnp.int32, (1, PAIR), 1)
    own = [(lane < HD).astype(F32).astype(BF16), (lane >= HD).astype(F32).astype(BF16)]
    mark = [(lane == HD).astype(F32).astype(BF16), (lane == 0).astype(F32).astype(BF16)]
    return lane, own, mark


def place_rows(rows, offset, columns):
    a, r = divmod(offset, 128)
    lane = lax.broadcasted_iota(jnp.int32, rows.shape, 1)
    turned = pltpu.roll(rows, r, 1) if r else rows
    columns[a] = columns[a] + jnp.where(lane >= r, turned, 0.0)
    if r and a + 1 < len(columns):
        columns[a + 1] = columns[a + 1] + jnp.where(lane < r, turned, 0.0)


def read_packs(dp_size, heads, slots, packs, vec, bias, hidden, room):
    per = vec.shape[1] // dp_size
    tensor = packs.shape[1]
    each = hidden.shape[1] // (dp_size * tensor)
    inner = HD // dp_size
    row = lax.broadcasted_iota(jnp.int32, (8, 128), 0)
    vec_columns = [jnp.zeros((8, 128), F32) for k in range(vec.shape[1] // 128)]
    hidden_columns = [jnp.zeros((1, 128), F32) for k in range(hidden.shape[1] // 128)]
    room[...] = jnp.zeros_like(room)
    for dp in range(dp_size):
        for t in range(tensor):
            data = packs[dp, t].astype(F32)
            if t == 0:
                place_rows(jnp.where(row < 6, data[0:8], 0.0), dp * per, vec_columns)
            for k in range(2):
                room[t, k, dp * inner : (dp + 1) * inner, :] = data[8 + 8 * k : 8 + 8 * k + inner]
    for k, (dp, t) in enumerate(slots):
        place_rows(packs[dp, t].astype(F32)[6:7], k * each, hidden_columns)
    for k, column in enumerate(vec_columns):
        vec[:, k * 128 : (k + 1) * 128] = column
    for k, column in enumerate(hidden_columns):
        hidden[:, k * 128 : (k + 1) * 128] = column
    for k in range(2):
        columns = [jnp.zeros((1, 128), F32) for j in range(bias.shape[1] // 128)]
        for t in range(tensor):
            lines = room[t, k].T
            for h in range(heads):
                place_rows(lines[h : h + 1], (t * heads + h) * HD, columns)
        for j, column in enumerate(columns):
            bias[k : k + 1, j * 128 : (j + 1) * 128] = column


def front_kernel(
    dp_size,
    heads,
    counts,
    ground,
    indices,
    omega,
    tok,
    cot,
    attn_f,
    out_f,
    up_f,
    down_f,
    vec_f,
    bias_f,
    hidden_f,
    cot2,
    feed_all,
    start_own,
    weights,
    normed,
    qs,
    keys,
    values,
    mixed_heads,
    attended,
    lse,
    mid,
    vec,
    hidden_bias,
    ints,
    attn_in,
    out_in,
    up_in,
    down_in,
    vec_in,
    bias_in,
    hidden_in,
    attn,
    pack,
    packs,
    up,
    down,
    tok2,
    cot_in,
    ints2,
    line,
    start,
    bias,
    room,
    loose,
    send_sem,
    recv_sem,
    pair_sem,
    local_sem,
):
    cube = Cube(dp_size)
    c, own_image = cube.core, cube.t
    length, half = normed.shape[0], qs.shape[0]
    base = pl.multiple_of(c * half, half)
    other = pl.multiple_of((1 - c) * half, half)
    loads = [
        pltpu.make_async_copy(source, target, local_sem.at[k])
        for k, (source, target) in enumerate(
            (
                (attn_f, attn_in),
                (out_f, out_in),
                (vec_f, vec_in),
                (bias_f, bias_in),
                (hidden_f, hidden_in),
                (tok, tok2.at[c]),
                (cot, cot_in),
                (up_f, up_in),
                (down_f, down_in),
            )
        )
    ]
    for copy in loads:
        copy.start()
    announce(cube.partners())
    line[...] = jnp.zeros_like(line)
    line[0:1, 0 : indices.shape[1]] = indices[...]
    slot = lax.broadcasted_iota(jnp.int32, line.shape, 1)
    shifted = pltpu.roll(line[...], 2, 1)
    shifted = jnp.where(slot == 0, counts[0], jnp.where(slot == 1, ground[0], shifted))
    ints2[c] = shifted
    for copy in loads[:5]:
        copy.wait()
    attn[0:3] = attn_in[...].astype(BF16)
    attn[3] = out_in[...].astype(BF16)
    pack[...] = jnp.zeros_like(pack)
    pack[0:6, 0 : vec_in.shape[1]] = vec_in[...]
    pack[6:7, 0 : hidden_in.shape[1]] = hidden_in[...]
    for k in range(2):
        pack[8 + 8 * k : 8 + 8 * k + bias_in.shape[1], 0 : bias_in.shape[2]] = bias_in[k]
    packs[cube.dp, cube.t] = pack[...].astype(BF16)
    weights[cube.t, :, cube.dp] = attn[...]
    meet(cube.partners())
    path = cube.path("XzY")
    pack_job = Gather(
        path,
        packs.at[cube.dp, cube.t],
        lambda dp, t: packs.at[dp, t],
        send_sem.at[0],
        recv_sem.at[0],
    )
    attn_jobs = [
        Gather(
            path,
            attn.at[2 * k : 2 * k + 2],
            lambda dp, t, k=k: weights.at[t, 2 * k : 2 * k + 2, dp],
            send_sem.at[k + 1],
            recv_sem.at[k + 1],
        )
        for k in range(2)
    ]
    feed_jobs = [
        Gather(
            path,
            source,
            lambda dp, t, k=k: feed_all.at[dp, t, k],
            send_sem.at[k + 3],
            recv_sem.at[k + 3],
        )
        for k, source in enumerate((up, down))
    ]
    pairs = [
        pltpu.make_async_remote_copy(
            src_ref=source,
            dst_ref=target.at[c],
            send_sem=pair_sem.at[0, k],
            recv_sem=pair_sem.at[1, k],
            device_id=cube.sibling,
            device_id_type=MESH,
        )
        for k, (source, target) in enumerate(
            ((ints2.at[c], ints2), (tok2.at[c], tok2), (cot_in.at[pl.ds(other, half)], cot2))
        )
    ]
    steps = len(pack_job.order)
    pack_job.start()
    for job in attn_jobs:
        job.start()
    pairs[0].start()
    loads[5].wait()
    pairs[1].start()
    early, late, feed_todo = [], [], []
    for k in range(steps):
        (early if 2 * k < steps else late).extend((job, k) for job in attn_jobs)
        early.extend((pack_job, j) for j in (2 * k, 2 * k + 1) if j < steps)
        feed_todo.extend((job, k) for job in feed_jobs)

    def pump(todo, number):
        for job, k in todo[:number]:
            job.step(k)
        del todo[:number]

    for copy in loads[7:]:
        copy.wait()
    up[...] = up_in[...].astype(BF16)
    down[...] = down_in[...].astype(BF16)
    loads[6].wait()
    pairs[2].start()
    keeps = [
        pltpu.make_async_copy(up, feed_all.at[cube.dp, cube.t, 0], local_sem.at[9]),
        pltpu.make_async_copy(down, feed_all.at[cube.dp, cube.t, 1], local_sem.at[10]),
        pltpu.make_async_copy(cot_in.at[pl.ds(base, half)], cot2.at[c], local_sem.at[11]),
    ]
    for copy in keeps:
        copy.start()
    pump(early, 12)
    pairs[0].wait_recv()
    pairs[1].wait_recv()

    ints[...] = ints2[own_image]
    count = ints[0:1, 0:1]
    quarter = D // 4
    scale = ints[0:1, 1:2].astype(F32) / 10.0
    angle = lax.broadcasted_iota(jnp.int32, (GRID, 2 * quarter), 0).astype(F32) * scale * omega[0:1, :]
    wave = lax.broadcasted_iota(jnp.int32, (GRID, 2 * quarter), 1)
    full = jnp.where(wave < quarter, jnp.sin(angle), jnp.cos(angle))
    hi = full.astype(BF16)
    rest = full - hi.astype(F32)
    middle = rest.astype(BF16)
    little = (rest - middle.astype(F32)).astype(BF16)
    stack = jnp.concatenate([hi, middle, little], axis=0)
    tile = 256
    for r in range(length // tile):
        span = slice(r * tile, (r + 1) * tile)
        index = ints[0:1, span]
        slots = lax.broadcasted_iota(jnp.int32, (1, tile), 1) + r * tile
        places = lax.broadcasted_iota(jnp.int32, (GRID, tile), 0)
        parts = []
        for part in (lax.shift_right_logical(index, 5), lax.bitwise_and(index, GRID - 1)):
            part = jnp.where(slots < 2, -1, part)
            hot = (places == part).astype(F32).astype(BF16)
            parts.append(tn(jnp.concatenate([hot, hot, hot], axis=0), stack))
        code = jnp.concatenate(parts, axis=1)
        live = row_live(count, r * tile, tile)
        start[span, :] = (tok2[own_image, span, :].astype(F32) + code) * live
        pump(early, 10)
    keep = pltpu.make_async_copy(start.at[pl.ds(base, half)], start_own, local_sem.at[12])
    keep.start()
    keeps.append(keep)
    pump(early, len(early))
    for job in feed_jobs:
        job.start()
    back_path = cube.path(BACK)
    slots = [scatter_entry(back_path, m) for group in send_order(back_path) for m in group]
    read_packs(dp_size, heads, slots, packs, vec, bias, hidden_bias, room)
    for r in range(length // tile):
        span = slice(r * tile, (r + 1) * tile)
        xhat, rstd = centre(start[span, :])
        normed[span, :] = (xhat * vec[0:1, :] + vec[1:2, :]).astype(BF16)
        pump(late, 4)
    pump(late, len(late))

    width = weights.shape[4]

    def weight(t, k):
        rows = weights.shape[3]
        if rows % 16 == 0:
            return weights[t, k].reshape(D, width)
        for e in range(dp_size):
            loose[e * rows : (e + 1) * rows, :] = weights[t, k, e].astype(F32)
        return loose[...].astype(BF16)

    for t in range(weights.shape[0]):
        cols = slice(t * width, (t + 1) * width)
        query = nn(normed[pl.ds(base, half), :], weight(t, 0)) + bias[0:1, cols]
        qs[:, cols] = query.astype(BF16) * jnp.asarray(HD**-0.5, BF16)
        for r in range(length // half):
            span = slice(r * half, (r + 1) * half)
            keys[span, cols] = nn(normed[span, :], weight(t, 1)).astype(BF16)
            values[span, cols] = (nn(normed[span, :], weight(t, 2)) + bias[1:2, cols]).astype(BF16)
        pump(feed_todo, 6)

    lane, own, mark = lane_sets()
    dead = ((1.0 - row_live(count, 0, length)) * DEAD).astype(BF16)
    wide = lax.broadcasted_iota(jnp.int32, (1, PAIR), 1)
    block = 256
    for r in range(half // block):
        span = slice(r * block, (r + 1) * block)
        sums = jnp.zeros((block, PAIR), F32)
        for p in range(D // PAIR):
            cols = slice(p * PAIR, (p + 1) * PAIR)
            outs = []
            for h in range(2):
                kx = keys[:, cols] * own[h] + dead * mark[h]
                qx = qs[span, cols] * own[h] + mark[h]
                scores = nt(qx, kx)
                top = jnp.max(scores, axis=1, keepdims=True)
                grown = jnp.exp(scores - top)
                total = jnp.sum(grown, axis=1, keepdims=True)
                outs.append(nn(grown.astype(BF16), values[:, cols]) / total)
                sums = jnp.where(wide == 2 * p + h, top + jnp.log(total), sums)
            both = jnp.where(lane < HD, outs[0], outs[1])
            mixed_heads[span, cols] = both
            attended[span, cols] = both.astype(BF16)
            pump(feed_todo, 3)
        lse[:, span] = sums.T
    out = nt(attended[:, :width], weight(0, 3))
    for t in range(1, weights.shape[0]):
        out = out + nt(attended[:, t * width : (t + 1) * width], weight(t, 3))
    mid[...] = start[pl.ds(base, half), :] + (out + vec[4:5, :])
    pump(feed_todo, len(feed_todo))
    for job in [pack_job] + attn_jobs + feed_jobs:
        job.finish()
    for copy in pairs[:2]:
        copy.wait_send()
    pairs[2].wait()
    for copy in keeps:
        copy.wait()


def norm_back(xhat, rstd, gain, upstream):
    scaled = upstream * gain
    return rstd * (
        scaled
        - jnp.mean(scaled, axis=-1, keepdims=True)
        - xhat * jnp.mean(scaled * xhat, axis=-1, keepdims=True)
    )


def total_rows(values):
    return jnp.sum(values, axis=0, keepdims=True)


def rows_of(ref, start, number, k, loose):
    rows = ref.shape[2]
    if rows % 16 == 0:
        return ref[start : start + number, k].reshape(number * rows, ref.shape[3])
    parts = []
    per = loose.shape[0] // rows
    for e in range(number):
        place = e % per * rows
        loose[place : place + rows, :] = ref[start + e, k].astype(F32)
        if place + rows == per * rows:
            parts.append(loose[0 : per * rows, :].astype(BF16))
    return jnp.concatenate(parts, axis=0)


def put_rows(ref, start, number, k, value, loose):
    rows = ref.shape[2]
    if rows % 16 == 0:
        ref[start : start + number, k] = value.astype(BF16).reshape(number, rows, ref.shape[3])
        return
    per = loose.shape[0] // rows
    for e in range(number):
        place = e % per * rows
        if place == 0:
            loose[0 : per * rows, :] = value[e * rows : (e + per) * rows, :]
        ref[start + e, k] = loose[place : place + rows, :].astype(BF16)


def put_attn(ref, t, k, value, loose):
    number, rows, cols = ref.shape[2:]
    if rows % 16 == 0:
        ref[t, k] = value.astype(BF16).reshape(number, rows, cols)
        return
    per = loose.shape[0] // rows
    for e in range(number):
        place = e % per * rows
        if place == 0:
            loose[0 : per * rows, 0:cols] = value[e * rows : (e + per) * rows, :]
        ref[t, k, e] = loose[place : place + rows, 0:cols].astype(BF16)


def back_kernel(
    dp_size,
    mid,
    cot2,
    feed_all,
    vec,
    hidden_bias,
    weights,
    attended,
    mixed_heads,
    qs,
    keys,
    values,
    lse,
    normed,
    ints,
    start_own,
    attn_sum,
    feed_sum,
    small_sum,
    mixed_out,
    input_out,
    feed,
    feed_land,
    attn,
    attn_land,
    normed2,
    act,
    hidden_low,
    grad_low,
    down_sum,
    norm_sum,
    mid_low,
    k_low,
    v_low,
    norm_land,
    delta,
    small_send,
    small_land,
    loose,
    load_sem,
    local_sem,
    feed_send,
    feed_recv,
    attn_send,
    attn_recv,
    small_sem,
    spread_send,
    spread_recv,
    pair_sem,
):
    cube = Cube(dp_size)
    c = cube.core
    mixed, heads_grad, q_low, start, mid_grad = normed2, act, hidden_low, down_sum, norm_sum
    input_half, norm_other = grad_low, mid_low
    path = cube.path(BACK)
    groups = send_order(path)
    slots = [m for group in groups for m in group]
    place = {m: k for k, m in enumerate(slots)}
    cot_load = pltpu.make_async_copy(cot2.at[cube.t], grad_low, local_sem.at[0])
    cot_load.start()
    loads = []
    for k, m in enumerate(slots):
        dp, t = scatter_entry(path, m)
        loads.append(pltpu.make_async_copy(feed_all.at[dp, t], feed.at[k], load_sem.at[k]))
        loads[k].start()
    neighbours = cube.partners() + [cube.diagonal]
    announce(neighbours)
    feed_job = Scatter(path, lambda m: feed.at[place[m]], feed_land, feed_send, feed_recv)

    def attn_part(m):
        dp, t = scatter_entry(path, m)
        return attn.at[t, :, dp]

    attn_job = Scatter(path, attn_part, attn_land, attn_send, attn_recv)

    half = mid.shape[0]
    length = keys.shape[0]
    width = weights.shape[3]
    base = pl.multiple_of(c * half, half)
    other = pl.multiple_of((1 - c) * half, half)
    count = ints[0:1, 0:1]
    live = row_live(count, c * half, half)
    rows = feed.shape[2]
    xhat, rstd = centre(mid[...])
    normed2[...] = (xhat * vec[2:3, :] + vec[3:4, :]).astype(BF16)
    cot_load.wait()
    grad_low[...] = (grad_low[...].astype(F32) * live).astype(BF16)
    down_sum[...] = mid[...] + vec[5:6, :]
    norm_sum[...] = jnp.zeros_like(norm_sum)
    meet(neighbours)
    first = 0
    for g, group in enumerate(groups):
        number = len(group)
        for k in range(first, first + number):
            loads[k].wait()
        up = rows_of(feed, first, number, 0, loose)
        down = rows_of(feed, first, number, 1, loose)
        span = slice(first * rows, (first + number) * rows)
        bias_grad = 0.0
        for r in range(2):
            part = slice(r * half // 2, (r + 1) * half // 2)
            hidden = nt(normed2[part, :], up) + hidden_bias[:, span]
            bell = 0.5 + 0.5 * lax.erf(hidden * ROOT_HALF)
            act[part, :] = (hidden * bell).astype(BF16)
            slope = bell + hidden * (ROOT_TWO_PI_INV * jnp.exp(-0.5 * hidden * hidden))
            hidden_grad = nt(grad_low[part, :], down) * slope
            bias_grad = bias_grad + total_rows(hidden_grad)
            hidden_low[part, :] = hidden_grad.astype(BF16)
        down_sum[...] += nn(act[...], down)
        norm_sum[...] += nn(hidden_low[...], up)
        put_rows(feed, first, number, 0, tn(hidden_low[...], normed2[...]), loose)
        put_rows(feed, first, number, 1, tn(act[...], grad_low[...]), loose)
        for e, m in enumerate(group):
            dp, t = scatter_entry(path, m)
            begin, turn = divmod(e * rows, 128)
            piece = bias_grad[:, begin * 128 : min((begin + 2) * 128, bias_grad.shape[1])]
            piece = pltpu.roll(piece, piece.shape[1] - turn, 1) if turn else piece
            small_send[0, pl.ds(48 + dp * 2 + t, 1), :] = piece[:, 0:128]
        if g % 2 == 0:
            for m in group:
                feed_job.send(0, m)
        elif g == 1:
            for m in group:
                feed_job.step(m)
        first += number
    later = [m for m in groups[3] if m]

    def pump(number):
        for m in later[:number]:
            feed_job.step(m)
        del later[:number]

    mixed[...] = (live * down_sum[...]).astype(BF16)
    start_load = pltpu.make_async_copy(start_own, start, local_sem.at[1])
    start_load.start()
    wait_mixed = spread(cube, mixed, mixed_out, spread_send.at[0], spread_recv.at[0])
    xhat, rstd = centre(mid[...])
    upstream = norm_sum[...]
    grad_out = grad_low[...].astype(F32)
    grad = grad_out + norm_back(xhat, rstd, vec[2:3, :], upstream)
    mid_grad[...] = grad
    mid_low[...] = grad.astype(BF16)
    sums = [
        None,
        None,
        total_rows(upstream * xhat),
        total_rows(upstream),
        total_rows(grad),
        total_rows(grad_out),
    ]

    for t in range(weights.shape[0]):
        cols = slice(t * width, (t + 1) * width)
        heads_grad[:, cols] = nn(mid_low[...], weights[t, 3]).astype(BF16)
        put_attn(attn, t, 3, tn(mid_low[...], attended[:, cols]), loose)
    product = heads_grad[...].astype(F32) * mixed_heads[...]
    head_of = lax.broadcasted_iota(jnp.int32, (16, D), 0)
    lanes = lax.broadcasted_iota(jnp.int32, (16, D), 1)
    pick = jnp.where(
        (lanes >= head_of * HD) & (lanes < head_of * HD + HD), 1.0, 0.0
    ).astype(BF16)
    hi = product.astype(BF16)
    delta[...] = nt(pick, hi) + nt(pick, (product - hi.astype(F32)).astype(BF16))
    lane, own, mark = lane_sets()
    dead = ((1.0 - row_live(count, 0, length)) * DEAD).astype(BF16)
    block = 512
    pumps = (2, 1, 1, 0, 0, 2)
    q_sums, v_sums = [], []
    for p in range(D // PAIR):
        cols = slice(p * PAIR, (p + 1) * PAIR)
        q_parts = []
        v_parts = [0.0] * (length // block)
        k_parts = [0.0] * (length // block)
        for h in range(2):
            head = 2 * p + h
            qx = qs[:, cols] * own[h] + mark[h]
            gx = heads_grad[:, cols] * own[h]
            q_sum = jnp.zeros((PAIR, half), F32)
            for b in range(length // block):
                span = slice(b * block, (b + 1) * block)
                kx = keys[span, cols] * own[h] + dead[span] * mark[h]
                probs = jnp.exp(nt(kx, qx) - lse[head : head + 1, :])
                prob_grad = nt(values[span, cols], gx)
                score_low = (probs * (prob_grad - delta[head : head + 1, :])).astype(BF16)
                v_parts[b] = v_parts[b] + nn(probs.astype(BF16), gx)
                k_parts[b] = k_parts[b] + nn(score_low, qx) * own[h].astype(F32)
                q_sum = q_sum + tn(kx, score_low)
            q_parts.append(q_sum.T)
        q_grad = jnp.where(lane < HD, q_parts[0], q_parts[1]) * HD**-0.5
        q_low[:, cols] = q_grad.astype(BF16)
        q_sums.append(total_rows(q_grad))
        v_total = 0.0
        for b in range(length // block):
            span = slice(b * block, (b + 1) * block)
            k_low[span, cols] = k_parts[b].astype(BF16)
            v_low[span, cols] = v_parts[b].astype(BF16)
            v_total = v_total + total_rows(v_parts[b])
        v_sums.append(v_total)
        pump(pumps[p])

    halves = [slice(t * width, (t + 1) * width) for t in range(weights.shape[0])]
    part = 0.0
    for t, cols in enumerate(halves):
        part = (
            part
            + nt(k_low[pl.ds(other, half), cols], weights[t, 1])
            + nt(v_low[pl.ds(other, half), cols], weights[t, 2])
        )
    norm_other[...] = part.astype(BF16)
    exchange = pltpu.make_async_remote_copy(
        src_ref=norm_other,
        dst_ref=norm_land,
        send_sem=pair_sem.at[0],
        recv_sem=pair_sem.at[1],
        device_id=cube.sibling,
        device_id_type=MESH,
    )
    exchange.start()
    for t, cols in enumerate(halves):
        put_attn(attn, t, 0, tn(normed[pl.ds(base, half), :], q_low[:, cols]), loose)
        put_attn(attn, t, 1, tn(normed[...], k_low[:, cols]), loose)
        put_attn(attn, t, 2, tn(normed[...], v_low[:, cols]), loose)
    for g in (0, 2):
        for m in groups[g]:
            attn_job.send(0, m)
    pump(len(later))
    upstream = 0.0
    for t, cols in enumerate(halves):
        upstream = (
            upstream
            + nt(q_low[:, cols], weights[t, 0])
            + nt(k_low[pl.ds(base, half), cols], weights[t, 1])
            + nt(v_low[pl.ds(base, half), cols], weights[t, 2])
        )
    for m in groups[1]:
        attn_job.step(m)
    start_load.wait()
    xhat, rstd = centre(start[...])
    exchange.wait()
    upstream = upstream + norm_land[...].astype(F32)
    grad = mid_grad[...] + norm_back(xhat, rstd, vec[0:1, :], upstream)
    input_half[...] = (live * grad).astype(BF16)
    wait_input = spread(cube, input_half, input_out, spread_send.at[1], spread_recv.at[1])
    sums[0], sums[1] = total_rows(upstream * xhat), total_rows(upstream)
    for j in range(D // 128):
        cols = slice(j * 128, (j + 1) * 128)
        for k, line in enumerate(sums):
            small_send[0, 8 * j + k : 8 * j + k + 1, :] = line[:, cols]
        small_send[0, 8 * j + 6 : 8 * j + 7, :] = q_sums[j]
        small_send[0, 8 * j + 7 : 8 * j + 8, :] = v_sums[j]
    smalls = []

    def small_step(p):
        copy = pltpu.make_async_remote_copy(
            src_ref=small_send.at[p],
            dst_ref=small_land.at[p],
            send_sem=small_sem.at[0, p],
            recv_sem=small_sem.at[1, p],
            device_id=path.partner(path.count - 1 - p),
            device_id_type=MESH,
        )
        copy.start()
        smalls.append(copy)

    def small_close(p):
        smalls[p].wait_recv()
        value = small_send[p] + small_land[p]
        if p + 1 < path.count:
            small_send[p + 1] = value
            small_step(p + 1)
        else:
            small_sum[...] = value

    small_step(0)
    closed = 0
    rest = [m for m in groups[3] if m]
    for k, m in enumerate(rest):
        attn_job.step(m)
        if k % 2 == 1 and closed < path.count:
            small_close(closed)
            closed += 1
    feed_sum[...] = feed_job.total(0)
    while closed < path.count:
        small_close(closed)
        closed += 1
    attn_sum[...] = attn_job.total(0)
    wait_mixed()
    wait_input()
    exchange_sent = smalls
    for copy in exchange_sent:
        copy.wait_send()
    feed_job.finish()
    attn_job.finish()


def finish_kernel(
    dp_size,
    heads,
    attn_sum,
    feed_sum,
    small,
    mixed_half,
    input_half,
    mixed,
    inputs,
    attn_out,
    bias_out,
    out_out,
    vec_out,
    up_out,
    hidden_out,
    down_out,
    room,
    local_sem,
):
    copies = []
    for k, (source, target) in enumerate(((mixed_half, mixed), (input_half, inputs))):
        for h in range(2):
            load = pltpu.make_async_copy(source.at[h], room.at[k, h], local_sem.at[0, k, h])
            load.start()
            copies.append(
                (load, pltpu.make_async_copy(room.at[k, h], target.at[h], local_sem.at[1, k, h]))
            )
    dp, t = lax.axis_index("dp"), lax.axis_index("tensor")
    attn_out[...] = attn_sum[0:3]
    out_out[...] = attn_sum[3]
    up_out[...] = feed_sum[0]
    down_out[...] = feed_sum[1]
    for load, store in copies:
        load.wait()
        store.start()
    per = vec_out.shape[1]
    lines = jnp.concatenate([small[8 * j : 8 * j + 8, :] for j in range(D // 128)], axis=1)
    vec_out[...] = pltpu.roll(lines, lax.rem(D - dp * per, D), 1)[0:6, 0:per]
    each = bias_out.shape[1]
    turned = pltpu.roll(lines, lax.rem(2 * D - t * (D // 2) - dp * each, D), 1)
    for k in range(2):
        lines = [turned[6 + k : 7 + k, h * HD : (h + 1) * HD] for h in range(heads)]
        lines.append(jnp.zeros((8 - heads, HD), F32))
        bias_out[k] = jnp.concatenate(lines, axis=0).T[0:each, 0:heads]
    hidden_out[...] = small[pl.ds(48 + dp * 2 + t, 1), :][:, 0 : hidden_out.shape[1]]
    for load, store in copies:
        store.wait()


ANY = pl.BlockSpec(memory_space=pltpu.HBM)
VMEM = pl.BlockSpec(memory_space=pltpu.VMEM)
SMEM = pl.BlockSpec(memory_space=pltpu.SMEM)


def shape(dims, kind):
    return jax.ShapeDtypeStruct(dims, kind)


def local(
    dp_size,
    tokens,
    counts,
    indices,
    ground_dist,
    cotangent,
    attn_weight,
    attn_bias,
    out_weight,
    vectors,
    up_weight,
    up_bias,
    down_weight,
):
    tensor = 2
    chips, length, width = tokens.shape
    half = length // 2
    attn_rows, attn_cols = attn_weight.shape[1:]
    ff_rows = down_weight.shape[0]
    ff = ff_rows * dp_size * tensor
    heads = attn_bias.shape[1]
    count = phases_of(dp_size)
    devices = 1 << count
    dma = pltpu.SemaphoreType.DMA

    quarter = width // 4
    omega = 1.0 / 10000.0 ** (np.arange(quarter) / quarter)
    omega = jnp.asarray(np.tile(omega.astype(np.float32), (8, 2)))
    inner = attn_bias.shape[2]
    half_rows, all_rows = (half, width), (length, width)
    tight = attn_rows % 16 == 0 and ff_rows % 16 == 0

    (
        cot2,
        feed_all,
        start_own,
        weights,
        normed,
        qs,
        keys,
        values,
        mixed_heads,
        attended,
        lse,
        mid,
        vec,
        hidden_bias,
        image,
    ) = pl.pallas_call(
        functools.partial(front_kernel, dp_size, heads),
        name="front",
        out_shape=[
            shape((2, half, width), BF16),
            shape((dp_size, tensor, 2, ff_rows, width), BF16),
            shape(half_rows, F32),
            shape((tensor, 4, dp_size, attn_rows, attn_cols), BF16),
            shape(all_rows, BF16),
            shape(half_rows, BF16),
            shape(all_rows, BF16),
            shape(all_rows, BF16),
            shape(half_rows, F32),
            shape(half_rows, BF16),
            shape((PAIR, half), F32),
            shape(half_rows, F32),
            shape((8, width), F32),
            shape((1, ff), F32),
            shape((8, length), jnp.int32),
        ],
        in_specs=[SMEM] * 2 + [VMEM] * 2 + [ANY] * 9,
        out_specs=[ANY] * 3 + [VMEM] * 12,
        scratch_shapes=[
            pltpu.VMEM(attn_weight.shape, F32),
            pltpu.VMEM(out_weight.shape[::-1], F32),
            pltpu.VMEM(up_weight.shape[::-1], F32),
            pltpu.VMEM(down_weight.shape, F32),
            pltpu.VMEM(vectors.shape, F32),
            pltpu.VMEM((2, inner, heads), F32),
            pltpu.VMEM((1,) + up_bias.shape, F32),
            pltpu.VMEM((4, attn_rows, attn_cols), BF16),
            pltpu.VMEM((PACK, 128), F32),
            pltpu.VMEM((dp_size, tensor, PACK, 128), BF16),
            pltpu.VMEM((ff_rows, width), BF16),
            pltpu.VMEM((ff_rows, width), BF16),
            pltpu.VMEM((2,) + all_rows, BF16),
            pltpu.VMEM(all_rows, BF16),
            pltpu.VMEM((2, 8, length), jnp.int32),
            pltpu.VMEM((8, length), jnp.int32),
            pltpu.VMEM(all_rows, F32),
            pltpu.VMEM((8, width), F32),
            pltpu.VMEM((tensor, 2, 128, 128), F32),
            pltpu.VMEM((8, 128) if tight else (width, attn_cols), F32),
            dma((5, devices)),
            dma((5, devices)),
            dma((2, 3)),
            dma((13,)),
        ],
        compiler_params=pltpu.CompilerParams(
            collective_id=0, has_side_effects=True, vmem_limit_bytes=60 * MIB
        ),
    )(
        counts,
        ground_dist,
        indices,
        omega,
        tokens[0],
        cotangent[0],
        attn_weight,
        out_weight.T,
        up_weight.T,
        down_weight,
        vectors,
        attn_bias.transpose(0, 2, 1),
        up_bias[None],
    )
    weights = weights.reshape(tensor, 4, width, attn_cols)

    ff_dims = (2, ff_rows, width)
    attn_dims = (4, attn_rows, attn_cols)
    quarter_ff = ff // 4
    small_dims = (-(-(48 + devices) // 8) * 8, 128)
    attn_sum, feed_sum, small_sum, mixed_out, input_out = pl.pallas_call(
        functools.partial(back_kernel, dp_size),
        name="back",
        out_shape=[
            shape(attn_dims, F32),
            shape(ff_dims, F32),
            shape(small_dims, F32),
            shape((2, half, width), BF16),
            shape((2, half, width), BF16),
        ],
        in_specs=[VMEM] + [ANY] * 2 + [VMEM] * 11 + [ANY],
        out_specs=[VMEM] * 3 + [ANY] * 2,
        scratch_shapes=[
            pltpu.VMEM((devices,) + ff_dims, BF16),
            pltpu.VMEM((devices - 1,) + ff_dims, BF16),
            pltpu.VMEM((tensor, 4, dp_size, attn_rows, attn_cols), BF16),
            pltpu.VMEM((devices - 1,) + attn_dims, BF16),
            pltpu.VMEM(half_rows, BF16),
            pltpu.VMEM((half, quarter_ff), BF16),
            pltpu.VMEM((half, quarter_ff), BF16),
            pltpu.VMEM(half_rows, BF16),
            pltpu.VMEM(half_rows, F32),
            pltpu.VMEM(half_rows, F32),
            pltpu.VMEM(half_rows, BF16),
            pltpu.VMEM(all_rows, BF16),
            pltpu.VMEM(all_rows, BF16),
            pltpu.VMEM(half_rows, BF16),
            pltpu.VMEM((16, half), F32),
            pltpu.VMEM((count,) + small_dims, F32),
            pltpu.VMEM((count,) + small_dims, F32),
            pltpu.VMEM((8, 128) if tight else (quarter_ff // 4, width), F32),
            dma((devices,)),
            dma((2,)),
            dma((devices,)),
            dma((devices,)),
            dma((devices,)),
            dma((devices,)),
            dma((2, count)),
            dma((2, 2)),
            dma((2, 2)),
            dma((2,)),
        ],
        compiler_params=pltpu.CompilerParams(
            collective_id=2, has_side_effects=True, vmem_limit_bytes=64 * MIB - 65536
        ),
    )(
        mid,
        cot2,
        feed_all,
        vec,
        hidden_bias,
        weights,
        attended,
        mixed_heads,
        qs,
        keys,
        values,
        lse,
        normed,
        image,
        start_own,
    )

    results = pl.pallas_call(
        functools.partial(finish_kernel, dp_size, heads),
        name="finish",
        out_shape=[
            shape((2, half, width), BF16),
            shape((2, half, width), BF16),
            shape(attn_weight.shape, F32),
            shape((2, inner, heads), F32),
            shape(out_weight.shape[::-1], F32),
            shape(vectors.shape, F32),
            shape(up_weight.shape[::-1], F32),
            shape((1, ff_rows), F32),
            shape(down_weight.shape, F32),
        ],
        in_specs=[VMEM] * 3 + [ANY] * 2,
        out_specs=[ANY] * 2 + [VMEM] * 7,
        scratch_shapes=[pltpu.VMEM((2, 2, half, width), BF16), dma((2, 2, 2))],
        compiler_params=pltpu.CompilerParams(vmem_limit_bytes=60 * MIB),
    )(attn_sum, feed_sum, small_sum, mixed_out, input_out)
    return (
        results[0].reshape(1, length, width),
        results[1].reshape(1, length, width),
        results[2],
        results[3].transpose(0, 2, 1),
        results[4].T,
        results[5],
        results[6].T,
        results[7].reshape(ff_rows),
        results[8],
    )


def solution(mesh):
    placed = (
        P("dp", None, None),
        P("dp"),
        P("dp", None),
        P("dp"),
        P("dp", None, None),
        P(None, "dp", "tensor"),
        P(None, "tensor", "dp"),
        P("tensor", "dp"),
        P(None, "dp"),
        P(None, ("dp", "tensor")),
        P(("dp", "tensor")),
        P(("dp", "tensor"), None),
    )
    return jax.shard_map(
        functools.partial(local, mesh.shape["dp"]),
        mesh=mesh,
        in_specs=placed,
        out_specs=(
            P("dp", None, None),
            P("dp", None, None),
            P(None, "dp", "tensor"),
            P(None, "tensor", "dp"),
            P("tensor", "dp"),
            P(None, "dp"),
            P(None, ("dp", "tensor")),
            P(("dp", "tensor")),
            P(("dp", "tensor"), None),
        ),
        check_vma=False,
    )
```

```python
import functools

import jax
import jax.numpy as jnp
import numpy as np
from jax import lax
from jax.experimental import pallas as pl
from jax.experimental.pallas import tpu as pltpu
from jax.sharding import PartitionSpec as P

D = 768
HD = 64
GRID = 32
EPS = 1e-06
DEAD = -1e30
PAIR = 2 * HD
ROOT_HALF = 0.7071067811865476
ROOT_TWO_PI_INV = 0.3989422804014327

F32 = jnp.float32
BF16 = jnp.bfloat16
MESH = pl.DeviceIdType.MESH
MIB = 1 << 20
BACK = "xYZ"


def nn(a, b):
    return lax.dot_general(a, b, (((1,), (0,)), ((), ())), preferred_element_type=F32)


def nt(a, b):
    return lax.dot_general(a, b, (((1,), (1,)), ((), ())), preferred_element_type=F32)


def tn(a, b):
    return lax.dot_general(a, b, (((0,), (0,)), ((), ())), preferred_element_type=F32)


class Path:
    def __init__(self, cube, steps, mirror):
        self.cube, self.steps, self.mirror = cube, steps, mirror
        self.count = len(steps)

    def partner(self, p):
        return (self.cube.dp + self.steps[p][0], self.cube.t + self.steps[p][1])

    def entry(self, mask):
        dp, t = self.cube.dp, self.cube.t
        for p, (ddp, dt) in enumerate(self.steps):
            if mask >> p & 1:
                dp, t = dp + ddp, t + dt
        return dp, t

    def mirrored(self, mask):
        if self.mirror is None:
            return mask
        i, j = self.mirror
        return mask & ~(1 << i | 1 << j) | (mask >> i & 1) << j | (mask >> j & 1) << i


class Cube:
    def __init__(self, dp_size):
        self.dp = lax.axis_index("dp")
        self.t = lax.axis_index("tensor")
        self.core = lax.rem(self.dp, 2)

        def flip(b):
            return b * (1 - 2 * lax.rem(lax.div(self.dp, b), 2))

        self.dt, self.dy, self.dc = 1 - 2 * self.t, flip(2), flip(1)
        self.far = []
        b = dp_size // 2
        while b >= 4:
            self.far.append((flip(b), 0))
            b //= 2
        self.sibling = (self.dp + self.dc, self.t)
        self.across = (self.dp, self.t + self.dt)
        self.diagonal = (self.dp + self.dc, self.t + self.dt)

    def path(self, kind):
        c = self.core
        x, y, far, last = (0, self.dt), (self.dy, 0), self.far[:-1], self.far[-1]
        n = len(self.far)

        def pick(first, second):
            return tuple((1 - c) * f + c * s for f, s in zip(first, second))

        if kind == "zXY":
            steps, mirror = [*far, last, pick(x, y), pick(y, x)], (n, n + 1)
        elif kind == "XzY":
            steps, mirror = [*far, pick(x, y), last, pick(y, x)], (n - 1, n + 1)
        elif kind == "xYZ":
            steps, mirror = [*far, x, pick(y, last), pick(last, y)], (n, n + 1)
        else:
            steps, mirror = [*far, x, last, y], None
        return Path(self, steps + [(self.dc, 0)], mirror)

    def partners(self):
        return [(self.dp + ddp, self.t + dt) for ddp, dt in self.far] + [
            (self.dp + self.dy, self.t),
            self.across,
            self.sibling,
        ]


def phases_of(dp_size):
    return (2 * dp_size).bit_length() - 1


def announce(devices):
    barrier = pltpu.get_barrier_semaphore()
    for device in devices:
        pl.semaphore_signal(barrier, inc=1, device_id=device, device_id_type=MESH)


def meet(devices):
    pl.semaphore_wait(pltpu.get_barrier_semaphore(), len(devices))


class Gather:
    def __init__(self, path, own, slot, send_sem, recv_sem):
        self.path, self.own, self.slot = path, own, slot
        self.send_sem, self.recv_sem = send_sem, recv_sem
        self.count = path.count
        self.sent = []
        self.order = sorted(
            ((p, m) for p in range(self.count) for m in range(1 << p)),
            key=lambda item: (item[1].bit_count(), item[0], item[1]),
        )

    def copy(self, p, mask, place, source):
        k = (1 << p) - 1 + mask
        there = (1 << p) - 1 + (self.path.mirrored(mask) if p == self.count - 1 else mask)
        return pltpu.make_async_remote_copy(
            src_ref=source,
            dst_ref=place,
            send_sem=self.send_sem.at[k],
            recv_sem=self.recv_sem.at[there],
            device_id=self.path.partner(p),
            device_id_type=MESH,
        )

    def send(self, p, mask):
        place = self.slot(*self.path.entry(mask))
        copy = self.copy(p, mask, place, self.own if mask == 0 else place)
        copy.start()
        self.sent.append(copy)

    def start(self):
        for p in range(self.count):
            self.send(p, 0)

    def step(self, k):
        p, mask = self.order[k]
        place = self.slot(*self.path.entry(mask | 1 << p))
        there = self.path.mirrored(mask) if p == self.count - 1 else mask
        self.copy(p, there, place, place).wait_recv()
        for later in range(p + 1, self.count):
            self.send(later, mask | 1 << p)

    def finish(self):
        for copy in self.sent:
            copy.wait_send()


def low_bit(m):
    return (m & -m).bit_length() - 1 if m else 99


class Scatter:
    def __init__(self, path, part, landed, send_sem, recv_sem):
        self.path, self.count = path, path.count
        self.part, self.landed = part, landed
        self.send_sem, self.recv_sem = send_sem, recv_sem
        self.sent = []
        self.order = send_order(path)

    def index(self, q, m):
        return (1 << (self.count - 1 - q)) - 1 + (m >> (q + 1))

    def describe(self, q, m, source):
        k = self.index(q, other_name(self.path, m) if q == 0 else m)
        return pltpu.make_async_remote_copy(
            src_ref=source,
            dst_ref=self.landed.at[k],
            send_sem=self.send_sem.at[k],
            recv_sem=self.recv_sem.at[k],
            device_id=self.path.partner(self.count - 1 - q),
            device_id_type=MESH,
        )

    def send(self, q, m):
        copy = self.describe(q, m, self.part(m))
        copy.start()
        self.sent.append(copy)

    def total(self, m):
        total = self.part(m)[...].astype(F32)
        for q in range(min(low_bit(m), self.count)):
            k = self.index(q, m)
            name = other_name(self.path, m) if q == 0 else m
            self.describe(q, name, self.landed.at[k]).wait_recv()
            total = total + self.landed[k].astype(F32)
        return total

    def step(self, m):
        self.part(m)[...] = self.total(m).astype(BF16)
        self.send(low_bit(m), m)

    def finish(self):
        for copy in self.sent:
            copy.wait_send()


def reverse(count, m):
    return sum((m >> q & 1) << (count - 1 - q) for q in range(count))


def other_name(path, m):
    return reverse(path.count, path.mirrored(reverse(path.count, m)))


def send_order(path):
    def rank(name):
        rest = name & ~3
        return (low_bit(rest), low_bit(rest & (rest - 1)), name)

    masks = range(1 << path.count)
    given = sorted((m for m in masks if m & 1), key=lambda m: rank(other_name(path, m)))
    kept = sorted((m for m in masks if not m & 1), key=rank)
    return [
        [m for m in given if other_name(path, m) & 2],
        [m for m in kept if m & 2],
        [m for m in given if not other_name(path, m) & 2],
        [m for m in kept if not m & 2],
    ]


def scatter_entry(path, m):
    return path.entry(reverse(path.count, m))


def spread(cube, half, out, send_sem, recv_sem):
    c, t = cube.core, cube.t
    mine = out.at[c]

    def push(device, k):
        return pltpu.make_async_remote_copy(
            src_ref=half,
            dst_ref=mine,
            send_sem=send_sem.at[k],
            recv_sem=recv_sem.at[c],
            device_id=device,
            device_id_type=MESH,
        )

    def arrival(h):
        return pltpu.make_async_remote_copy(
            src_ref=half,
            dst_ref=out.at[h],
            send_sem=send_sem.at[0],
            recv_sem=recv_sem.at[h],
            device_id=cube.sibling,
            device_id_type=MESH,
        )

    keep = pltpu.make_async_copy(half, mine, send_sem.at[0])

    @pl.when(c == t)
    def _():
        push(cube.across, 1).start()
        keep.start()

    @pl.when(c != t)
    def _():
        push(cube.diagonal, 1).start()
        push(cube.sibling, 0).start()

    def wait():
        @pl.when(c == t)
        def _():
            keep.wait()
            push(cube.across, 1).wait_send()
            arrival(1 - c).wait_recv()

        @pl.when(c != t)
        def _():
            push(cube.sibling, 0).wait_send()
            push(cube.diagonal, 1).wait_send()
            arrival(c).wait_recv()
            arrival(1 - c).wait_recv()

    return wait


PACK = 32


def centre(values):
    mean = jnp.mean(values, axis=-1, keepdims=True)
    centred = values - mean
    rstd = lax.rsqrt(jnp.mean(centred * centred, axis=-1, keepdims=True) + EPS)
    return centred * rstd, rstd


def row_live(count, offset, rows):
    places = lax.broadcasted_iota(jnp.int32, (rows, 1), 0) + offset
    return (places < count + 2).astype(F32)


def lane_sets():
    lane = lax.broadcasted_iota(jnp.int32, (1, PAIR), 1)
    own = [(lane < HD).astype(F32).astype(BF16), (lane >= HD).astype(F32).astype(BF16)]
    mark = [(lane == HD).astype(F32).astype(BF16), (lane == 0).astype(F32).astype(BF16)]
    return lane, own, mark


def place_rows(rows, offset, columns):
    a, r = divmod(offset, 128)
    lane = lax.broadcasted_iota(jnp.int32, rows.shape, 1)
    turned = pltpu.roll(rows, r, 1) if r else rows
    columns[a] = columns[a] + jnp.where(lane >= r, turned, 0.0)
    if r and a + 1 < len(columns):
        columns[a + 1] = columns[a + 1] + jnp.where(lane < r, turned, 0.0)


def read_packs(dp_size, heads, slots, packs, vec, bias, hidden, room):
    per = vec.shape[1] // dp_size
    tensor = packs.shape[1]
    each = hidden.shape[1] // (dp_size * tensor)
    inner = HD // dp_size
    row = lax.broadcasted_iota(jnp.int32, (8, 128), 0)
    vec_columns = [jnp.zeros((8, 128), F32) for k in range(vec.shape[1] // 128)]
    hidden_columns = [jnp.zeros((1, 128), F32) for k in range(hidden.shape[1] // 128)]
    room[...] = jnp.zeros_like(room)
    for dp in range(dp_size):
        for t in range(tensor):
            data = packs[dp, t].astype(F32)
            if t == 0:
                place_rows(jnp.where(row < 6, data[0:8], 0.0), dp * per, vec_columns)
            for k in range(2):
                room[t, k, dp * inner : (dp + 1) * inner, :] = data[8 + 8 * k : 8 + 8 * k + inner]
    for k, (dp, t) in enumerate(slots):
        place_rows(packs[dp, t].astype(F32)[6:7], k * each, hidden_columns)
    for k, column in enumerate(vec_columns):
        vec[:, k * 128 : (k + 1) * 128] = column
    for k, column in enumerate(hidden_columns):
        hidden[:, k * 128 : (k + 1) * 128] = column
    for k in range(2):
        columns = [jnp.zeros((1, 128), F32) for j in range(bias.shape[1] // 128)]
        for t in range(tensor):
            lines = room[t, k].T
            for h in range(heads):
                place_rows(lines[h : h + 1], (t * heads + h) * HD, columns)
        for j, column in enumerate(columns):
            bias[k : k + 1, j * 128 : (j + 1) * 128] = column


def front_kernel(
    dp_size,
    heads,
    counts,
    ground,
    indices,
    omega,
    tok,
    cot,
    attn_f,
    out_f,
    up_f,
    down_f,
    vec_f,
    bias_f,
    hidden_f,
    cot2,
    feed_all,
    start_own,
    weights,
    normed,
    qs,
    keys,
    values,
    mixed_heads,
    attended,
    lse,
    mid,
    vec,
    hidden_bias,
    ints,
    attn_in,
    out_in,
    up_in,
    down_in,
    vec_in,
    bias_in,
    hidden_in,
    attn,
    pack,
    packs,
    up,
    down,
    tok2,
    cot_in,
    ints2,
    line,
    start,
    bias,
    room,
    loose,
    send_sem,
    recv_sem,
    pair_sem,
    local_sem,
):
    cube = Cube(dp_size)
    c, own_image = cube.core, cube.t
    length, half = normed.shape[0], qs.shape[0]
    base = pl.multiple_of(c * half, half)
    other = pl.multiple_of((1 - c) * half, half)
    loads = [
        pltpu.make_async_copy(source, target, local_sem.at[k])
        for k, (source, target) in enumerate(
            (
                (attn_f, attn_in),
                (out_f, out_in),
                (vec_f, vec_in),
                (bias_f, bias_in),
                (hidden_f, hidden_in),
                (tok, tok2.at[c]),
                (cot, cot_in),
                (up_f, up_in),
                (down_f, down_in),
            )
        )
    ]
    for copy in loads:
        copy.start()
    announce(cube.partners())
    line[...] = jnp.zeros_like(line)
    line[0:1, 0 : indices.shape[1]] = indices[...]
    slot = lax.broadcasted_iota(jnp.int32, line.shape, 1)
    shifted = pltpu.roll(line[...], 2, 1)
    shifted = jnp.where(slot == 0, counts[0], jnp.where(slot == 1, ground[0], shifted))
    ints2[c] = shifted
    for copy in loads[:5]:
        copy.wait()
    attn[0:3] = attn_in[...].astype(BF16)
    attn[3] = out_in[...].astype(BF16)
    pack[...] = jnp.zeros_like(pack)
    pack[0:6, 0 : vec_in.shape[1]] = vec_in[...]
    pack[6:7, 0 : hidden_in.shape[1]] = hidden_in[...]
    for k in range(2):
        pack[8 + 8 * k : 8 + 8 * k + bias_in.shape[1], 0 : bias_in.shape[2]] = bias_in[k]
    packs[cube.dp, cube.t] = pack[...].astype(BF16)
    weights[cube.t, :, cube.dp] = attn[...]
    meet(cube.partners())
    path = cube.path("XzY")
    pack_job = Gather(
        path,
        packs.at[cube.dp, cube.t],
        lambda dp, t: packs.at[dp, t],
        send_sem.at[0],
        recv_sem.at[0],
    )
    attn_jobs = [
        Gather(
            path,
            attn.at[2 * k : 2 * k + 2],
            lambda dp, t, k=k: weights.at[t, 2 * k : 2 * k + 2, dp],
            send_sem.at[k + 1],
            recv_sem.at[k + 1],
        )
        for k in range(2)
    ]
    feed_jobs = [
        Gather(
            path,
            source,
            lambda dp, t, k=k: feed_all.at[dp, t, k],
            send_sem.at[k + 3],
            recv_sem.at[k + 3],
        )
        for k, source in enumerate((up, down))
    ]
    pairs = [
        pltpu.make_async_remote_copy(
            src_ref=source,
            dst_ref=target.at[c],
            send_sem=pair_sem.at[0, k],
            recv_sem=pair_sem.at[1, k],
            device_id=cube.sibling,
            device_id_type=MESH,
        )
        for k, (source, target) in enumerate(
            ((ints2.at[c], ints2), (tok2.at[c], tok2), (cot_in.at[pl.ds(other, half)], cot2))
        )
    ]
    steps = len(pack_job.order)
    pack_job.start()
    for job in attn_jobs:
        job.start()
    pairs[0].start()
    loads[5].wait()
    pairs[1].start()
    early, late, feed_todo = [], [], []
    for k in range(steps):
        (early if 2 * k < steps else late).extend((job, k) for job in attn_jobs)
        early.extend((pack_job, j) for j in (2 * k, 2 * k + 1) if j < steps)
        feed_todo.extend((job, k) for job in feed_jobs)

    def pump(todo, number):
        for job, k in todo[:number]:
            job.step(k)
        del todo[:number]

    for copy in loads[7:]:
        copy.wait()
    up[...] = up_in[...].astype(BF16)
    down[...] = down_in[...].astype(BF16)
    loads[6].wait()
    pairs[2].start()
    keeps = [
        pltpu.make_async_copy(up, feed_all.at[cube.dp, cube.t, 0], local_sem.at[9]),
        pltpu.make_async_copy(down, feed_all.at[cube.dp, cube.t, 1], local_sem.at[10]),
        pltpu.make_async_copy(cot_in.at[pl.ds(base, half)], cot2.at[c], local_sem.at[11]),
    ]
    for copy in keeps:
        copy.start()
    pump(early, 12)
    pairs[0].wait_recv()
    pairs[1].wait_recv()

    ints[...] = ints2[own_image]
    count = ints[0:1, 0:1]
    quarter = D // 4
    scale = ints[0:1, 1:2].astype(F32) / 10.0
    angle = lax.broadcasted_iota(jnp.int32, (GRID, 2 * quarter), 0).astype(F32) * scale * omega[0:1, :]
    wave = lax.broadcasted_iota(jnp.int32, (GRID, 2 * quarter), 1)
    full = jnp.where(wave < quarter, jnp.sin(angle), jnp.cos(angle))
    hi = full.astype(BF16)
    rest = full - hi.astype(F32)
    middle = rest.astype(BF16)
    little = (rest - middle.astype(F32)).astype(BF16)
    stack = jnp.concatenate([hi, middle, little], axis=0)
    tile = 256
    for r in range(length // tile):
        span = slice(r * tile, (r + 1) * tile)
        index = ints[0:1, span]
        slots = lax.broadcasted_iota(jnp.int32, (1, tile), 1) + r * tile
        places = lax.broadcasted_iota(jnp.int32, (GRID, tile), 0)
        parts = []
        for part in (lax.shift_right_logical(index, 5), lax.bitwise_and(index, GRID - 1)):
            part = jnp.where(slots < 2, -1, part)
            hot = (places == part).astype(F32).astype(BF16)
            parts.append(tn(jnp.concatenate([hot, hot, hot], axis=0), stack))
        code = jnp.concatenate(parts, axis=1)
        live = row_live(count, r * tile, tile)
        start[span, :] = (tok2[own_image, span, :].astype(F32) + code) * live
        pump(early, 10)
    keep = pltpu.make_async_copy(start.at[pl.ds(base, half)], start_own, local_sem.at[12])
    keep.start()
    keeps.append(keep)
    pump(early, len(early))
    for job in feed_jobs:
        job.start()
    back_path = cube.path(BACK)
    slots = [scatter_entry(back_path, m) for group in send_order(back_path) for m in group]
    read_packs(dp_size, heads, slots, packs, vec, bias, hidden_bias, room)
    for r in range(length // tile):
        span = slice(r * tile, (r + 1) * tile)
        xhat, rstd = centre(start[span, :])
        normed[span, :] = (xhat * vec[0:1, :] + vec[1:2, :]).astype(BF16)
        pump(late, 4)
    pump(late, len(late))

    width = weights.shape[4]

    def weight(t, k):
        rows = weights.shape[3]
        if rows % 16 == 0:
            return weights[t, k].reshape(D, width)
        for e in range(dp_size):
            loose[e * rows : (e + 1) * rows, :] = weights[t, k, e].astype(F32)
        return loose[...].astype(BF16)

    for t in range(weights.shape[0]):
        cols = slice(t * width, (t + 1) * width)
        query = nn(normed[pl.ds(base, half), :], weight(t, 0)) + bias[0:1, cols]
        qs[:, cols] = query.astype(BF16) * jnp.asarray(HD**-0.5, BF16)
        for r in range(length // half):
            span = slice(r * half, (r + 1) * half)
            keys[span, cols] = nn(normed[span, :], weight(t, 1)).astype(BF16)
            values[span, cols] = (nn(normed[span, :], weight(t, 2)) + bias[1:2, cols]).astype(BF16)
        pump(feed_todo, 6)

    lane, own, mark = lane_sets()
    dead = ((1.0 - row_live(count, 0, length)) * DEAD).astype(BF16)
    wide = lax.broadcasted_iota(jnp.int32, (1, PAIR), 1)
    block = 256
    for r in range(half // block):
        span = slice(r * block, (r + 1) * block)
        sums = jnp.zeros((block, PAIR), F32)
        for p in range(D // PAIR):
            cols = slice(p * PAIR, (p + 1) * PAIR)
            outs = []
            for h in range(2):
                kx = keys[:, cols] * own[h] + dead * mark[h]
                qx = qs[span, cols] * own[h] + mark[h]
                scores = nt(qx, kx)
                top = jnp.max(scores, axis=1, keepdims=True)
                grown = jnp.exp(scores - top)
                total = jnp.sum(grown, axis=1, keepdims=True)
                outs.append(nn(grown.astype(BF16), values[:, cols]) / total)
                sums = jnp.where(wide == 2 * p + h, top + jnp.log(total), sums)
            both = jnp.where(lane < HD, outs[0], outs[1])
            mixed_heads[span, cols] = both
            attended[span, cols] = both.astype(BF16)
            pump(feed_todo, 3)
        lse[:, span] = sums.T
    out = nt(attended[:, :width], weight(0, 3))
    for t in range(1, weights.shape[0]):
        out = out + nt(attended[:, t * width : (t + 1) * width], weight(t, 3))
    mid[...] = start[pl.ds(base, half), :] + (out + vec[4:5, :])
    pump(feed_todo, len(feed_todo))
    for job in [pack_job] + attn_jobs + feed_jobs:
        job.finish()
    for copy in pairs[:2]:
        copy.wait_send()
    pairs[2].wait()
    for copy in keeps:
        copy.wait()


def norm_back(xhat, rstd, gain, upstream):
    scaled = upstream * gain
    return rstd * (
        scaled
        - jnp.mean(scaled, axis=-1, keepdims=True)
        - xhat * jnp.mean(scaled * xhat, axis=-1, keepdims=True)
    )


def total_rows(values):
    return jnp.sum(values, axis=0, keepdims=True)


def rows_of(ref, start, number, k, loose):
    rows = ref.shape[2]
    if rows % 16 == 0:
        return ref[start : start + number, k].reshape(number * rows, ref.shape[3])
    parts = []
    per = loose.shape[0] // rows
    for e in range(number):
        place = e % per * rows
        loose[place : place + rows, :] = ref[start + e, k].astype(F32)
        if place + rows == per * rows:
            parts.append(loose[0 : per * rows, :].astype(BF16))
    return jnp.concatenate(parts, axis=0)


def put_rows(ref, start, number, k, value, loose):
    rows = ref.shape[2]
    if rows % 16 == 0:
        ref[start : start + number, k] = value.astype(BF16).reshape(number, rows, ref.shape[3])
        return
    per = loose.shape[0] // rows
    for e in range(number):
        place = e % per * rows
        if place == 0:
            loose[0 : per * rows, :] = value[e * rows : (e + per) * rows, :]
        ref[start + e, k] = loose[place : place + rows, :].astype(BF16)


def put_attn(ref, t, k, value, loose):
    number, rows, cols = ref.shape[2:]
    if rows % 16 == 0:
        ref[t, k] = value.astype(BF16).reshape(number, rows, cols)
        return
    per = loose.shape[0] // rows
    for e in range(number):
        place = e % per * rows
        if place == 0:
            loose[0 : per * rows, 0:cols] = value[e * rows : (e + per) * rows, :]
        ref[t, k, e] = loose[place : place + rows, 0:cols].astype(BF16)


def back_kernel(
    dp_size,
    mid,
    cot2,
    feed_all,
    vec,
    hidden_bias,
    weights,
    attended,
    mixed_heads,
    qs,
    keys,
    values,
    lse,
    normed,
    ints,
    start_own,
    attn_sum,
    feed_sum,
    small_sum,
    mixed_out,
    input_out,
    feed,
    feed_land,
    attn,
    attn_land,
    normed2,
    act,
    hidden_low,
    grad_low,
    down_sum,
    norm_sum,
    mid_low,
    k_low,
    v_low,
    norm_land,
    delta,
    small_send,
    small_land,
    loose,
    load_sem,
    local_sem,
    feed_send,
    feed_recv,
    attn_send,
    attn_recv,
    small_sem,
    spread_send,
    spread_recv,
    pair_sem,
):
    cube = Cube(dp_size)
    c = cube.core
    mixed, heads_grad, q_low, start, mid_grad = normed2, act, hidden_low, down_sum, norm_sum
    input_half, norm_other = grad_low, mid_low
    path = cube.path(BACK)
    groups = send_order(path)
    slots = [m for group in groups for m in group]
    place = {m: k for k, m in enumerate(slots)}
    cot_load = pltpu.make_async_copy(cot2.at[cube.t], grad_low, local_sem.at[0])
    cot_load.start()
    loads = []
    for k, m in enumerate(slots):
        dp, t = scatter_entry(path, m)
        loads.append(pltpu.make_async_copy(feed_all.at[dp, t], feed.at[k], load_sem.at[k]))
        loads[k].start()
    neighbours = cube.partners() + [cube.diagonal]
    announce(neighbours)
    feed_job = Scatter(path, lambda m: feed.at[place[m]], feed_land, feed_send, feed_recv)

    attn_path = cube.path("XzY")
    attn_groups = send_order(attn_path)

    def attn_part(m):
        dp, t = scatter_entry(attn_path, m)
        return attn.at[t, :, dp]

    attn_job = Scatter(attn_path, attn_part, attn_land, attn_send, attn_recv)

    half = mid.shape[0]
    length = keys.shape[0]
    width = weights.shape[3]
    base = pl.multiple_of(c * half, half)
    other = pl.multiple_of((1 - c) * half, half)
    count = ints[0:1, 0:1]
    live = row_live(count, c * half, half)
    rows = feed.shape[2]
    xhat, rstd = centre(mid[...])
    normed2[...] = (xhat * vec[2:3, :] + vec[3:4, :]).astype(BF16)
    cot_load.wait()
    grad_low[...] = (grad_low[...].astype(F32) * live).astype(BF16)
    down_sum[...] = mid[...] + vec[5:6, :]
    norm_sum[...] = jnp.zeros_like(norm_sum)
    meet(neighbours)
    first = 0
    for g, group in enumerate(groups):
        number = len(group)
        for k in range(first, first + number):
            loads[k].wait()
        up = rows_of(feed, first, number, 0, loose)
        down = rows_of(feed, first, number, 1, loose)
        span = slice(first * rows, (first + number) * rows)
        bias_grad = 0.0
        for r in range(2):
            part = slice(r * half // 2, (r + 1) * half // 2)
            hidden = nt(normed2[part, :], up) + hidden_bias[:, span]
            bell = 0.5 + 0.5 * lax.erf(hidden * ROOT_HALF)
            act[part, :] = (hidden * bell).astype(BF16)
            slope = bell + hidden * (ROOT_TWO_PI_INV * jnp.exp(-0.5 * hidden * hidden))
            hidden_grad = nt(grad_low[part, :], down) * slope
            bias_grad = bias_grad + total_rows(hidden_grad)
            hidden_low[part, :] = hidden_grad.astype(BF16)
        down_sum[...] += nn(act[...], down)
        norm_sum[...] += nn(hidden_low[...], up)
        put_rows(feed, first, number, 0, tn(hidden_low[...], normed2[...]), loose)
        put_rows(feed, first, number, 1, tn(act[...], grad_low[...]), loose)
        for e, m in enumerate(group):
            dp, t = scatter_entry(path, m)
            begin, turn = divmod(e * rows, 128)
            piece = bias_grad[:, begin * 128 : min((begin + 2) * 128, bias_grad.shape[1])]
            piece = pltpu.roll(piece, piece.shape[1] - turn, 1) if turn else piece
            small_send[0, pl.ds(48 + dp * 2 + t, 1), :] = piece[:, 0:128]
        if g % 2 == 0:
            for m in group:
                feed_job.send(0, m)
        elif g == 1:
            for m in group:
                feed_job.step(m)
        first += number
    later = [m for m in groups[3] if m]

    def pump(number):
        for m in later[:number]:
            feed_job.step(m)
        del later[:number]

    mixed[...] = (live * down_sum[...]).astype(BF16)
    start_load = pltpu.make_async_copy(start_own, start, local_sem.at[1])
    start_load.start()
    wait_mixed = spread(cube, mixed, mixed_out, spread_send.at[0], spread_recv.at[0])
    xhat, rstd = centre(mid[...])
    upstream = norm_sum[...]
    grad_out = grad_low[...].astype(F32)
    grad = grad_out + norm_back(xhat, rstd, vec[2:3, :], upstream)
    mid_grad[...] = grad
    mid_low[...] = grad.astype(BF16)
    sums = [
        None,
        None,
        total_rows(upstream * xhat),
        total_rows(upstream),
        total_rows(grad),
        total_rows(grad_out),
    ]

    for t in range(weights.shape[0]):
        cols = slice(t * width, (t + 1) * width)
        heads_grad[:, cols] = nn(mid_low[...], weights[t, 3]).astype(BF16)
        put_attn(attn, t, 3, tn(mid_low[...], attended[:, cols]), loose)
    product = heads_grad[...].astype(F32) * mixed_heads[...]
    head_of = lax.broadcasted_iota(jnp.int32, (16, D), 0)
    lanes = lax.broadcasted_iota(jnp.int32, (16, D), 1)
    pick = jnp.where(
        (lanes >= head_of * HD) & (lanes < head_of * HD + HD), 1.0, 0.0
    ).astype(BF16)
    hi = product.astype(BF16)
    delta[...] = nt(pick, hi) + nt(pick, (product - hi.astype(F32)).astype(BF16))
    lane, own, mark = lane_sets()
    dead = ((1.0 - row_live(count, 0, length)) * DEAD).astype(BF16)
    block = 512
    pumps = (2, 1, 1, 0, 0, 2)
    q_sums, v_sums = [], []
    for p in range(D // PAIR):
        cols = slice(p * PAIR, (p + 1) * PAIR)
        q_parts = []
        v_parts = [0.0] * (length // block)
        k_parts = [0.0] * (length // block)
        for h in range(2):
            head = 2 * p + h
            qx = qs[:, cols] * own[h] + mark[h]
            gx = heads_grad[:, cols] * own[h]
            q_sum = jnp.zeros((PAIR, half), F32)
            for b in range(length // block):
                span = slice(b * block, (b + 1) * block)
                kx = keys[span, cols] * own[h] + dead[span] * mark[h]
                probs = jnp.exp(nt(kx, qx) - lse[head : head + 1, :])
                prob_grad = nt(values[span, cols], gx)
                score_low = (probs * (prob_grad - delta[head : head + 1, :])).astype(BF16)
                v_parts[b] = v_parts[b] + nn(probs.astype(BF16), gx)
                k_parts[b] = k_parts[b] + nn(score_low, qx) * own[h].astype(F32)
                q_sum = q_sum + tn(kx, score_low)
            q_parts.append(q_sum.T)
        q_grad = jnp.where(lane < HD, q_parts[0], q_parts[1]) * HD**-0.5
        q_low[:, cols] = q_grad.astype(BF16)
        q_sums.append(total_rows(q_grad))
        v_total = 0.0
        for b in range(length // block):
            span = slice(b * block, (b + 1) * block)
            k_low[span, cols] = k_parts[b].astype(BF16)
            v_low[span, cols] = v_parts[b].astype(BF16)
            v_total = v_total + total_rows(v_parts[b])
        v_sums.append(v_total)
        pump(pumps[p])

    halves = [slice(t * width, (t + 1) * width) for t in range(weights.shape[0])]
    part = 0.0
    for t, cols in enumerate(halves):
        part = (
            part
            + nt(k_low[pl.ds(other, half), cols], weights[t, 1])
            + nt(v_low[pl.ds(other, half), cols], weights[t, 2])
        )
    norm_other[...] = part.astype(BF16)
    exchange = pltpu.make_async_remote_copy(
        src_ref=norm_other,
        dst_ref=norm_land,
        send_sem=pair_sem.at[0],
        recv_sem=pair_sem.at[1],
        device_id=cube.sibling,
        device_id_type=MESH,
    )
    exchange.start()
    for t, cols in enumerate(halves):
        put_attn(attn, t, 0, tn(normed[pl.ds(base, half), :], q_low[:, cols]), loose)
        put_attn(attn, t, 1, tn(normed[...], k_low[:, cols]), loose)
        put_attn(attn, t, 2, tn(normed[...], v_low[:, cols]), loose)
    for g in (0, 2):
        for m in attn_groups[g]:
            attn_job.send(0, m)
    pump(len(later))
    upstream = 0.0
    for t, cols in enumerate(halves):
        upstream = (
            upstream
            + nt(q_low[:, cols], weights[t, 0])
            + nt(k_low[pl.ds(base, half), cols], weights[t, 1])
            + nt(v_low[pl.ds(base, half), cols], weights[t, 2])
        )
    for m in attn_groups[1]:
        attn_job.step(m)
    start_load.wait()
    xhat, rstd = centre(start[...])
    exchange.wait()
    upstream = upstream + norm_land[...].astype(F32)
    grad = mid_grad[...] + norm_back(xhat, rstd, vec[0:1, :], upstream)
    input_half[...] = (live * grad).astype(BF16)
    wait_input = spread(cube, input_half, input_out, spread_send.at[1], spread_recv.at[1])
    sums[0], sums[1] = total_rows(upstream * xhat), total_rows(upstream)
    for j in range(D // 128):
        cols = slice(j * 128, (j + 1) * 128)
        for k, line in enumerate(sums):
            small_send[0, 8 * j + k : 8 * j + k + 1, :] = line[:, cols]
        small_send[0, 8 * j + 6 : 8 * j + 7, :] = q_sums[j]
        small_send[0, 8 * j + 7 : 8 * j + 8, :] = v_sums[j]
    smalls = []

    def small_step(p):
        copy = pltpu.make_async_remote_copy(
            src_ref=small_send.at[p],
            dst_ref=small_land.at[p],
            send_sem=small_sem.at[0, p],
            recv_sem=small_sem.at[1, p],
            device_id=path.partner(path.count - 1 - p),
            device_id_type=MESH,
        )
        copy.start()
        smalls.append(copy)

    def small_close(p):
        smalls[p].wait_recv()
        value = small_send[p] + small_land[p]
        if p + 1 < path.count:
            small_send[p + 1] = value
            small_step(p + 1)
        else:
            small_sum[...] = value

    small_step(0)
    closed = 0
    rest = [m for m in attn_groups[3] if m]
    for k, m in enumerate(rest):
        attn_job.step(m)
        if k % 2 == 1 and closed < path.count:
            small_close(closed)
            closed += 1
    feed_sum[...] = feed_job.total(0)
    while closed < path.count:
        small_close(closed)
        closed += 1
    attn_sum[...] = attn_job.total(0)
    wait_mixed()
    wait_input()
    exchange_sent = smalls
    for copy in exchange_sent:
        copy.wait_send()
    feed_job.finish()
    attn_job.finish()


def finish_kernel(
    dp_size,
    heads,
    attn_sum,
    feed_sum,
    small,
    mixed_half,
    input_half,
    mixed,
    inputs,
    attn_out,
    bias_out,
    out_out,
    vec_out,
    up_out,
    hidden_out,
    down_out,
    room,
    local_sem,
):
    copies = []
    for k, (source, target) in enumerate(((mixed_half, mixed), (input_half, inputs))):
        for h in range(2):
            load = pltpu.make_async_copy(source.at[h], room.at[k, h], local_sem.at[0, k, h])
            load.start()
            copies.append(
                (load, pltpu.make_async_copy(room.at[k, h], target.at[h], local_sem.at[1, k, h]))
            )
    dp, t = lax.axis_index("dp"), lax.axis_index("tensor")
    attn_out[...] = attn_sum[0:3]
    out_out[...] = attn_sum[3]
    up_out[...] = feed_sum[0]
    down_out[...] = feed_sum[1]
    for load, store in copies:
        load.wait()
        store.start()
    per = vec_out.shape[1]
    lines = jnp.concatenate([small[8 * j : 8 * j + 8, :] for j in range(D // 128)], axis=1)
    vec_out[...] = pltpu.roll(lines, lax.rem(D - dp * per, D), 1)[0:6, 0:per]
    each = bias_out.shape[1]
    turned = pltpu.roll(lines, lax.rem(2 * D - t * (D // 2) - dp * each, D), 1)
    for k in range(2):
        lines = [turned[6 + k : 7 + k, h * HD : (h + 1) * HD] for h in range(heads)]
        lines.append(jnp.zeros((8 - heads, HD), F32))
        bias_out[k] = jnp.concatenate(lines, axis=0).T[0:each, 0:heads]
    hidden_out[...] = small[pl.ds(48 + dp * 2 + t, 1), :][:, 0 : hidden_out.shape[1]]
    for load, store in copies:
        store.wait()


ANY = pl.BlockSpec(memory_space=pltpu.HBM)
VMEM = pl.BlockSpec(memory_space=pltpu.VMEM)
SMEM = pl.BlockSpec(memory_space=pltpu.SMEM)


def shape(dims, kind):
    return jax.ShapeDtypeStruct(dims, kind)


def local(
    dp_size,
    tokens,
    counts,
    indices,
    ground_dist,
    cotangent,
    attn_weight,
    attn_bias,
    out_weight,
    vectors,
    up_weight,
    up_bias,
    down_weight,
):
    tensor = 2
    chips, length, width = tokens.shape
    half = length // 2
    attn_rows, attn_cols = attn_weight.shape[1:]
    ff_rows = down_weight.shape[0]
    ff = ff_rows * dp_size * tensor
    heads = attn_bias.shape[1]
    count = phases_of(dp_size)
    devices = 1 << count
    dma = pltpu.SemaphoreType.DMA

    quarter = width // 4
    omega = 1.0 / 10000.0 ** (np.arange(quarter) / quarter)
    omega = jnp.asarray(np.tile(omega.astype(np.float32), (8, 2)))
    inner = attn_bias.shape[2]
    half_rows, all_rows = (half, width), (length, width)
    tight = attn_rows % 16 == 0 and ff_rows % 16 == 0

    (
        cot2,
        feed_all,
        start_own,
        weights,
        normed,
        qs,
        keys,
        values,
        mixed_heads,
        attended,
        lse,
        mid,
        vec,
        hidden_bias,
        image,
    ) = pl.pallas_call(
        functools.partial(front_kernel, dp_size, heads),
        name="front",
        out_shape=[
            shape((2, half, width), BF16),
            shape((dp_size, tensor, 2, ff_rows, width), BF16),
            shape(half_rows, F32),
            shape((tensor, 4, dp_size, attn_rows, attn_cols), BF16),
            shape(all_rows, BF16),
            shape(half_rows, BF16),
            shape(all_rows, BF16),
            shape(all_rows, BF16),
            shape(half_rows, F32),
            shape(half_rows, BF16),
            shape((PAIR, half), F32),
            shape(half_rows, F32),
            shape((8, width), F32),
            shape((1, ff), F32),
            shape((8, length), jnp.int32),
        ],
        in_specs=[SMEM] * 2 + [VMEM] * 2 + [ANY] * 9,
        out_specs=[ANY] * 3 + [VMEM] * 12,
        scratch_shapes=[
            pltpu.VMEM(attn_weight.shape, F32),
            pltpu.VMEM(out_weight.shape[::-1], F32),
            pltpu.VMEM(up_weight.shape[::-1], F32),
            pltpu.VMEM(down_weight.shape, F32),
            pltpu.VMEM(vectors.shape, F32),
            pltpu.VMEM((2, inner, heads), F32),
            pltpu.VMEM((1,) + up_bias.shape, F32),
            pltpu.VMEM((4, attn_rows, attn_cols), BF16),
            pltpu.VMEM((PACK, 128), F32),
            pltpu.VMEM((dp_size, tensor, PACK, 128), BF16),
            pltpu.VMEM((ff_rows, width), BF16),
            pltpu.VMEM((ff_rows, width), BF16),
            pltpu.VMEM((2,) + all_rows, BF16),
            pltpu.VMEM(all_rows, BF16),
            pltpu.VMEM((2, 8, length), jnp.int32),
            pltpu.VMEM((8, length), jnp.int32),
            pltpu.VMEM(all_rows, F32),
            pltpu.VMEM((8, width), F32),
            pltpu.VMEM((tensor, 2, 128, 128), F32),
            pltpu.VMEM((8, 128) if tight else (width, attn_cols), F32),
            dma((5, devices)),
            dma((5, devices)),
            dma((2, 3)),
            dma((13,)),
        ],
        compiler_params=pltpu.CompilerParams(
            collective_id=0, has_side_effects=True, vmem_limit_bytes=60 * MIB
        ),
    )(
        counts,
        ground_dist,
        indices,
        omega,
        tokens[0],
        cotangent[0],
        attn_weight,
        out_weight.T,
        up_weight.T,
        down_weight,
        vectors,
        attn_bias.transpose(0, 2, 1),
        up_bias[None],
    )
    weights = weights.reshape(tensor, 4, width, attn_cols)

    ff_dims = (2, ff_rows, width)
    attn_dims = (4, attn_rows, attn_cols)
    quarter_ff = ff // 4
    small_dims = (-(-(48 + devices) // 8) * 8, 128)
    attn_sum, feed_sum, small_sum, mixed_out, input_out = pl.pallas_call(
        functools.partial(back_kernel, dp_size),
        name="back",
        out_shape=[
            shape(attn_dims, F32),
            shape(ff_dims, F32),
            shape(small_dims, F32),
            shape((2, half, width), BF16),
            shape((2, half, width), BF16),
        ],
        in_specs=[VMEM] + [ANY] * 2 + [VMEM] * 11 + [ANY],
        out_specs=[VMEM] * 3 + [ANY] * 2,
        scratch_shapes=[
            pltpu.VMEM((devices,) + ff_dims, BF16),
            pltpu.VMEM((devices - 1,) + ff_dims, BF16),
            pltpu.VMEM((tensor, 4, dp_size, attn_rows, attn_cols), BF16),
            pltpu.VMEM((devices - 1,) + attn_dims, BF16),
            pltpu.VMEM(half_rows, BF16),
            pltpu.VMEM((half, quarter_ff), BF16),
            pltpu.VMEM((half, quarter_ff), BF16),
            pltpu.VMEM(half_rows, BF16),
            pltpu.VMEM(half_rows, F32),
            pltpu.VMEM(half_rows, F32),
            pltpu.VMEM(half_rows, BF16),
            pltpu.VMEM(all_rows, BF16),
            pltpu.VMEM(all_rows, BF16),
            pltpu.VMEM(half_rows, BF16),
            pltpu.VMEM((16, half), F32),
            pltpu.VMEM((count,) + small_dims, F32),
            pltpu.VMEM((count,) + small_dims, F32),
            pltpu.VMEM((8, 128) if tight else (quarter_ff // 4, width), F32),
            dma((devices,)),
            dma((2,)),
            dma((devices,)),
            dma((devices,)),
            dma((devices,)),
            dma((devices,)),
            dma((2, count)),
            dma((2, 2)),
            dma((2, 2)),
            dma((2,)),
        ],
        compiler_params=pltpu.CompilerParams(
            collective_id=2, has_side_effects=True, vmem_limit_bytes=64 * MIB - 65536
        ),
    )(
        mid,
        cot2,
        feed_all,
        vec,
        hidden_bias,
        weights,
        attended,
        mixed_heads,
        qs,
        keys,
        values,
        lse,
        normed,
        image,
        start_own,
    )

    results = pl.pallas_call(
        functools.partial(finish_kernel, dp_size, heads),
        name="finish",
        out_shape=[
            shape((2, half, width), BF16),
            shape((2, half, width), BF16),
            shape(attn_weight.shape, F32),
            shape((2, inner, heads), F32),
            shape(out_weight.shape[::-1], F32),
            shape(vectors.shape, F32),
            shape(up_weight.shape[::-1], F32),
            shape((1, ff_rows), F32),
            shape(down_weight.shape, F32),
        ],
        in_specs=[VMEM] * 3 + [ANY] * 2,
        out_specs=[ANY] * 2 + [VMEM] * 7,
        scratch_shapes=[pltpu.VMEM((2, 2, half, width), BF16), dma((2, 2, 2))],
        compiler_params=pltpu.CompilerParams(vmem_limit_bytes=60 * MIB),
    )(attn_sum, feed_sum, small_sum, mixed_out, input_out)
    return (
        results[0].reshape(1, length, width),
        results[1].reshape(1, length, width),
        results[2],
        results[3].transpose(0, 2, 1),
        results[4].T,
        results[5],
        results[6].T,
        results[7].reshape(ff_rows),
        results[8],
    )


def solution(mesh):
    placed = (
        P("dp", None, None),
        P("dp"),
        P("dp", None),
        P("dp"),
        P("dp", None, None),
        P(None, "dp", "tensor"),
        P(None, "tensor", "dp"),
        P("tensor", "dp"),
        P(None, "dp"),
        P(None, ("dp", "tensor")),
        P(("dp", "tensor")),
        P(("dp", "tensor"), None),
    )
    return jax.shard_map(
        functools.partial(local, mesh.shape["dp"]),
        mesh=mesh,
        in_specs=placed,
        out_specs=(
            P("dp", None, None),
            P("dp", None, None),
            P(None, "dp", "tensor"),
            P(None, "tensor", "dp"),
            P("tensor", "dp"),
            P(None, "dp"),
            P(None, ("dp", "tensor")),
            P(("dp", "tensor")),
            P(("dp", "tensor"), None),
        ),
        check_vma=False,
    )
```
